32 devices in a mesh: dp: 8 (over z, core), shard: 4 (over y, x).
Axes of the slice: x: 2, y: 2, z: 4, core: 2. Of those that a mesh axis runs over, the one named last changes fastest.
Arguments:
- tokens: bfloat16 [12288, 512], P(('dp', 'shard')), may hold values from -24 to 24
- w_proj: bfloat16 [512, 2048], P(None, 'shard'), may hold values from -0.25 to 0.25
- w_out: bfloat16 [512, 512], replicated, may hold values from -0.25 to 0.25
- item_rows: bfloat16 [4096, 512], P('shard'), may hold values from -1.5 to 1.5
- lengths: int32 [32, 4], P(('dp', 'shard')), may hold values from 1 to 192, 384 in all within a row
- target_owner: int32 [12288, 1], P(('dp', 'shard')), may hold values from 0 to 3; in each aligned block of 384 rows (0 to 383, 384 to 767, ...) at most 192 rows name the same one
- target_row: int32 [12288], P(('dp', 'shard')), may hold values from 0 to 1023
- negative_rows: int32 [256], P('shard'), may hold values from 0 to 1023
Outputs:
- grad_tokens: bfloat16 [12288, 512], P(('dp', 'shard'))
- weight_grads: float32 [512, 512], replicated
- item_grads: float32 [4096, 512], P('shard')
The draws below stay inside these ranges and needn't reach their ends.
Inputs may be any that keep to these rules, and one draw needn't show every extreme that they name: `target_owner`: in the rows of one device no owner is named more than 192 times, a bound that some block reaches.
All inputs are finite; a program needn't handle non-finite values.
Results may differ from the reference program's by a relative error of at most 0.02.
Values may be sent and summed in bfloat16 or wider, within the bound.
A program may use at most 64 MiB of HBM per device.

```python
import math
import jax
import jax.numpy as jnp
import numpy as np
from jax import lax

D = 512
HEADS = 4
DH = 128
TOK_DEV = 384
HIST_DEV = 4
MAXLEN = 192
ROWS_DEV = 1024
NEG_DEV = 64
CAP = 192
TOKENS = 12288
ITEMS = 4096
NEGS = 256
N_DP = 8
N_SHARD = 4
DEVICES = 32


def scaled_draw(key, rows_count, factor):
    base_key, row_key, col_key = jax.random.split(key, 3)
    row_scale = jnp.exp(jax.random.uniform(row_key, (rows_count, 1), minval=math.log(0.3), maxval=math.log(3.0)))
    col_scale = jnp.exp(jax.random.uniform(col_key, (1, D), minval=math.log(0.5), maxval=math.log(2.0)))
    base_values = jnp.clip(jax.random.normal(base_key, (rows_count, D)), -4.0, 4.0)
    return (base_values * row_scale * col_scale * factor).astype(jnp.float32)


def draw_tokens(key, part):
    return scaled_draw(jax.random.fold_in(key, 11), TOKENS, 1.0).astype(jnp.bfloat16)


def draw_item_rows(key, part):
    return scaled_draw(jax.random.fold_in(key, 23), ITEMS, 0.0625).astype(jnp.bfloat16)


def with_ends(drawn, own_key, least, largest):
    longest = drawn.shape.index(max(drawn.shape))
    spots = []
    for shift in (0, 1):
        where = [jax.random.randint(jax.random.fold_in(own_key, axis), (), 0, length) for axis, length in enumerate(drawn.shape)]
        where[longest] = (where[longest] + shift) % drawn.shape[longest]
        spots.append(tuple(where))
    return drawn.at[spots[0]].set(least).at[spots[1]].set(largest)


def levels(rng, shape, pieces, smallest, top_value):
    level, own = 1.0, jax.random.fold_in(rng, 6)
    for dim, shards_of in pieces:
        steps = jnp.exp(jax.random.uniform(jax.random.fold_in(own, dim), (shards_of,), jnp.float32, smallest / len(pieces), top_value / len(pieces)))
        level = level * jnp.repeat(steps, shape[dim] // shards_of).reshape([-1 if axis == dim else 1 for axis in range(len(shape))])
    return level


def profile(number_of, total, reach, skew):
    weights = [(1 << 20) // math.isqrt(rank ** skew) + 1 for rank in range(2, number_of + 1)]
    spare, given = total - reach - (number_of - 1), [1] * (number_of - 1)
    while spare > 0:
        free = [i for i in range(number_of - 1) if given[i] < reach]
        whole, remaining = sum([weights[i] for i in free]), spare
        for i in free:
            more = min(reach - given[i], max(1, remaining * weights[i] // whole), spare)
            given[i] = given[i] + more
            spare = spare - more
    return np.array([reach] + given)


def ragged_sizes(stream_key, number_of, total, bound, slope):
    if number_of == 2:
        one = jax.random.randint(stream_key, (), max(1, total - bound), min(bound, total - 1) + 1)
        return jnp.stack([one, total - one])
    tallies = jnp.asarray(profile(number_of, total, bound, slope), jnp.int32)
    couples = (number_of - 1) // 2
    giver, sink = tallies[1:1 + 2 * couples:2], tallies[2:2 + 2 * couples:2]
    margin = jnp.minimum(giver - 1, bound - sink)
    passed = jax.random.randint(jax.random.fold_in(stream_key, 1), (couples,), 0, 1 << 20) % (margin + 1)
    tallies = tallies.at[1:1 + 2 * couples:2].set(giver - passed).at[2:2 + 2 * couples:2].set(sink + passed)
    return tallies[jax.random.permutation(jax.random.fold_in(stream_key, 2), number_of)]


def shared_out(own_key, own, number, rows, count, top, most, skew):
    ranking = jax.random.permutation(own_key, count)
    heavy_load, usual = load_shares(count, rows * top, most, skew, True), load_shares(count, rows * top, most, skew, False)
    places = jnp.arange(count)

    def named(sizes, offset_by):
        used = int((sizes > 0).sum())
        fixed = max(1, used // 4)
        passed = fixed + (places - fixed + offset_by * (used - fixed)) % max(1, count - fixed)
        return jnp.zeros((count,), jnp.int32).at[ranking[jnp.where(places < fixed, places, passed)]].set(jnp.asarray(sizes, jnp.int32))

    sizes = jnp.where(number % 4 == 0, named(heavy_load, number // 4), named(usual, number - number // 4 - 1))
    mixed = jax.random.permutation(jax.random.fold_in(own, 3), count)
    giver, sink = mixed[0:count // 2 * 2:2], mixed[1:count // 2 * 2:2]
    margin = jnp.minimum(sizes[giver] - 1, most - sizes[sink]) // 2
    margin = jnp.where((giver == ranking[0]) | (sink == ranking[0]) | (sizes[sink] == 0), 0, jnp.maximum(margin, 0))
    passed = jax.random.randint(jax.random.fold_in(own, 4), (count // 2,), 0, 1 << 20) % (margin + 1)
    sizes = sizes.at[giver].add(-passed).at[sink].add(passed)
    items = jnp.searchsorted(jnp.cumsum(sizes), jnp.arange(rows * top), side="right").astype(jnp.int32)
    table = items.reshape(top, rows).T
    table = table[jax.random.permutation(jax.random.fold_in(own, 1), rows)]
    offset_by = jax.random.randint(jax.random.fold_in(own, 2), (rows, 1), 0, top)
    return jnp.take_along_axis(table, (jnp.arange(top)[None, :] + offset_by) % top, axis=1)


def load_shares(number_of, total, reach, slope, full):
    portions = [(1 << 20) // math.isqrt(standing ** slope) + 1 for standing in range(1, number_of + 1)]
    largest = reach if full else min(reach, max(-(-total // number_of), total * portions[0] // sum(portions)))
    least = 1 if total - largest >= number_of - 1 else 0
    counts, rest = [largest] + [least] * (number_of - 1), total - largest - least * (number_of - 1)
    while rest > 0:
        movable = [i for i in range(1, number_of) if counts[i] < largest] or [i for i in range(1, number_of) if counts[i] < reach]
        pool, remaining = sum([portions[i] for i in movable]), rest
        for i in movable:
            more = min(reach - counts[i], max(1, remaining * portions[i] // pool), rest)
            counts[i] = counts[i] + more
            rest = rest - more
    return np.array(counts)


def noise(own_key, dims, deviation, bound, cuts=(), kind=jnp.bfloat16):
    values = jax.random.normal(own_key, dims, jnp.float32) * deviation
    if len(cuts) > 0:
        values = levels(own_key, dims, cuts, -0.22, 0.18) * values
    return jnp.clip(values, min=-bound, max=bound).astype(kind)


def setup_inputs(seed: int = 0) -> dict:
    arg_keys = jax.random.split(jax.random.key(seed), 9)
    tokens = draw_tokens(jax.random.fold_in(arg_keys[8], 71), 0)
    w_proj = noise(arg_keys[1], (D, 4 * D), D ** -0.5, 0.25, ((1, 4),))
    w_out = noise(arg_keys[2], (D, D), D ** -0.5, 0.25)
    item_rows = draw_item_rows(jax.random.fold_in(arg_keys[8], 71), 0)
    lengths = jax.vmap(lambda own: ragged_sizes(own, HIST_DEV, TOK_DEV, MAXLEN, 2))(jax.random.split(arg_keys[4], DEVICES)).reshape((DEVICES, HIST_DEV)).astype(jnp.int32)
    target_owner_keys = jax.random.split(jax.random.fold_in(arg_keys[5], 1), TOKENS // TOK_DEV)
    target_owner_turns = jax.random.permutation(jax.random.fold_in(arg_keys[5], 3), TOKENS // TOK_DEV)
    target_owner = jax.vmap(lambda own, number: shared_out(jax.random.fold_in(arg_keys[5], 2), own, number, TOK_DEV, N_SHARD, 1, CAP, 1))(target_owner_keys, target_owner_turns).reshape((TOKENS, 1))
    target_row = with_ends(jax.random.randint(arg_keys[6], (TOKENS,), 0, ROWS_DEV), jax.random.fold_in(arg_keys[6], 1), 0, ROWS_DEV - 1).astype(jnp.int32)
    negative_rows = with_ends(jax.random.randint(arg_keys[7], (NEGS,), 0, ROWS_DEV), jax.random.fold_in(arg_keys[7], 1), 0, ROWS_DEV - 1).astype(jnp.int32)
    return dict(tokens=tokens, w_proj=w_proj, w_out=w_out, item_rows=item_rows, lengths=lengths, target_owner=target_owner, target_row=target_row, negative_rows=negative_rows)


epsilon = 1e-06
logit_divisor = 0.015625
loss_scale = 512.0

def reduce_last_dimension(operand, other_side):
    return lax.dot_general(operand, other_side, (((1,), (1,)), ((), ())), preferred_element_type=jnp.float32)

def contract_first(operand, other_side):
    return lax.dot_general(operand, other_side, (((0,), (0,)), ((), ())), preferred_element_type=jnp.float32)

def silu_slope(values):
    sigmoid = jax.nn.sigmoid(values)
    return sigmoid * (1.0 + values * (1.0 - sigmoid))

def history_mask(lengths_row, rows_count):
    history_ends = jnp.cumsum(lengths_row).astype(jnp.int32)
    positions = jnp.arange(rows_count, dtype=jnp.int32)
    history_ids = lax.optimization_barrier(jnp.sum((positions[:, None] >= history_ends[None, :-1]).astype(jnp.int32), axis=1))
    visible = (history_ids[:, None] == history_ids[None, :]) & (positions[None, :] <= positions[:, None])
    return jnp.where(visible, 1.0, 0.0).astype(jnp.float32)

def head_columns(activated, section, head_index):
    first_col = section * D + head_index * DH
    return activated[:, first_col:first_col + DH]

def head_scores(queries, key_rows):
    return reduce_last_dimension(queries, key_rows) * DH ** (-0.5)

def head_weights(scores, visible):
    return (jax.nn.silu(scores) * visible * (1.0 / MAXLEN)).astype(jnp.bfloat16)

def forward_layer(tokens, project, w_out, visible):
    wide_tokens = tokens.astype(jnp.float32)
    input_scale = lax.rsqrt(lax.optimization_barrier(jnp.mean(wide_tokens * wide_tokens, axis=1, keepdims=True)) + epsilon)
    normed = (wide_tokens * input_scale).astype(jnp.bfloat16)
    pre_act = project(normed)
    activated = lax.optimization_barrier(jax.nn.silu(pre_act).astype(jnp.bfloat16))
    heads_out = []
    for head_index in range(HEADS):
        queries = head_columns(activated, 2, head_index)
        key_rows = head_columns(activated, 3, head_index)
        value_rows = head_columns(activated, 1, head_index)
        weights = head_weights(head_scores(queries, key_rows), visible)
        heads_out.append(jnp.dot(weights, value_rows, preferred_element_type=jnp.float32))
    joined = lax.optimization_barrier(jnp.concatenate(heads_out, axis=1).astype(jnp.bfloat16))
    joined_wide = joined.astype(jnp.float32)
    middle_scale = lax.rsqrt(lax.optimization_barrier(jnp.mean(joined_wide * joined_wide, axis=1, keepdims=True)) + epsilon)
    gate_wide = activated[:, :D].astype(jnp.float32)
    gated = (joined_wide * middle_scale * gate_wide).astype(jnp.bfloat16)
    layer_out = wide_tokens + jnp.dot(gated, w_out, preferred_element_type=jnp.float32)
    return (layer_out, (wide_tokens, input_scale, pre_act, activated, joined, middle_scale, gated))

def loss_head(layer_out, clicked_product_vectors, sampled_decoys):
    out_scale = lax.rsqrt(lax.optimization_barrier(jnp.sum(layer_out * layer_out, axis=1, keepdims=True)) + epsilon)
    normalized_example_vectors = lax.optimization_barrier((layer_out * out_scale).astype(jnp.bfloat16))
    normalized_complete_embedding = normalized_example_vectors.astype(jnp.float32)
    correct_logit_entry = lax.optimization_barrier(jnp.sum(normalized_complete_embedding * clicked_product_vectors.astype(jnp.float32), axis=1)) / logit_divisor
    decoy_logit_entries = reduce_last_dimension(normalized_example_vectors, sampled_decoys) / logit_divisor
    target_exp = jnp.exp(correct_logit_entry)
    negative_exp = jnp.exp(decoy_logit_entries)
    totals = target_exp + lax.optimization_barrier(jnp.sum(negative_exp, axis=1))
    target_prob = target_exp / totals
    negative_probs = (loss_scale * negative_exp / totals[:, None]).astype(jnp.bfloat16)
    target_coef = (loss_scale * (target_prob - 1.0))[:, None]
    grad_unit = target_coef * clicked_product_vectors.astype(jnp.float32) + jnp.dot(negative_probs, sampled_decoys, preferred_element_type=jnp.float32)
    grad_out = out_scale * grad_unit - layer_out * out_scale ** 3 * lax.optimization_barrier(jnp.sum(layer_out * grad_unit, axis=1, keepdims=True))
    grad_target = target_coef * normalized_complete_embedding
    return (grad_out, grad_target, negative_probs, normalized_example_vectors)

def backward_layer(grad_out, saved_state, project_back, w_out, visible):
    wide_tokens, input_scale, pre_act, activated, joined, middle_scale, gated = saved_state
    grad_out_b = grad_out.astype(jnp.bfloat16)
    weight_part = contract_first(gated, grad_out_b)
    grad_gated = reduce_last_dimension(grad_out_b, w_out)
    joined_wide = joined.astype(jnp.float32)
    gate_wide = activated[:, :D].astype(jnp.float32)
    grad_gate = grad_gated * joined_wide * middle_scale
    grad_norm = grad_gated * gate_wide
    grad_joined = middle_scale * grad_norm - joined_wide * middle_scale ** 3 * lax.optimization_barrier(jnp.mean(joined_wide * grad_norm, axis=1, keepdims=True))
    grad_joined_b = grad_joined.astype(jnp.bfloat16)
    grad_values = []
    grad_queries = []
    grad_keys = []
    for head_index in range(HEADS):
        queries = head_columns(activated, 2, head_index)
        key_rows = head_columns(activated, 3, head_index)
        value_rows = head_columns(activated, 1, head_index)
        scores = head_scores(queries, key_rows)
        weights = head_weights(scores, visible)
        grad_head = grad_joined_b[:, head_index * DH:(head_index + 1) * DH]
        grad_weights = reduce_last_dimension(grad_head, value_rows)
        grad_values.append(contract_first(weights, grad_head))
        grad_scores = (grad_weights * visible * (1.0 / MAXLEN) * silu_slope(scores) * DH ** (-0.5)).astype(jnp.bfloat16)
        grad_queries.append(jnp.dot(grad_scores, key_rows, preferred_element_type=jnp.float32))
        grad_keys.append(contract_first(grad_scores, queries))
    grad_act = jnp.concatenate([grad_gate] + grad_values + grad_queries + grad_keys, axis=1)
    grad_pre = (grad_act * silu_slope(pre_act)).astype(jnp.bfloat16)
    grad_normed = project_back(grad_pre)
    grad_input = input_scale * grad_normed - wide_tokens * input_scale ** 3 * lax.optimization_barrier(jnp.mean(wide_tokens * grad_normed, axis=1, keepdims=True))
    return ((grad_out + grad_input).astype(jnp.bfloat16), weight_part)

def reference(tokens, w_proj, w_out, item_rows, lengths, target_owner, target_row, negative_rows):
    block_count = N_DP * N_SHARD
    block_rows = TOK_DEV
    rows_wide = item_rows.astype(jnp.float32)
    item_scale = lax.rsqrt(lax.optimization_barrier(jnp.sum(rows_wide * rows_wide, axis=1, keepdims=True)) + epsilon)
    unit_items = (rows_wide * item_scale).astype(jnp.bfloat16)
    negative_ids = (jnp.arange(NEGS, dtype=jnp.int32) // NEG_DEV * ROWS_DEV + negative_rows).astype(jnp.int32)
    sampled_decoys = jnp.take(unit_items, negative_ids, axis=0)
    target_ids = (target_owner[:, 0] * ROWS_DEV + target_row).astype(jnp.int32)

    def project(normed):
        return jnp.dot(normed, w_proj, preferred_element_type=jnp.float32)

    def project_back(grad_pre):
        return reduce_last_dimension(grad_pre, w_proj)

    def block_step(running, block_data):
        weight_sum, item_sum, negative_sum = running
        block_tokens, block_lengths, block_ids = block_data
        visible = history_mask(block_lengths, block_rows)
        layer_out, saved_state = forward_layer(block_tokens, project, w_out, visible)
        clicked_product_vectors = jnp.take(unit_items, block_ids, axis=0)
        grad_out, grad_target, negative_probs, normalized_example_vectors = loss_head(layer_out, clicked_product_vectors, sampled_decoys)
        grad_tokens, weight_part = backward_layer(grad_out, saved_state, project_back, w_out, visible)
        item_sum = item_sum.at[block_ids].add(grad_target)
        negative_sum = negative_sum + contract_first(negative_probs, normalized_example_vectors)
        return ((weight_sum + weight_part, item_sum, negative_sum), grad_tokens)
    initial = (jnp.zeros((D, D), jnp.float32), jnp.zeros((ITEMS, D), jnp.float32), jnp.zeros((NEGS, D), jnp.float32))
    block_data = (tokens.reshape(block_count, block_rows, D), lengths, target_ids.reshape(block_count, block_rows))
    finals, grad_tokens = lax.scan(block_step, initial, block_data)
    weight_sum, item_sum, negative_sum = finals
    grad_items = item_sum.at[negative_ids].add(negative_sum)
    item_grads = (item_scale * grad_items - rows_wide * item_scale ** 3 * lax.optimization_barrier(jnp.sum(rows_wide * grad_items, axis=1, keepdims=True))) / loss_scale
    return (grad_tokens.reshape(TOKENS, D), weight_sum / loss_scale, item_grads)
```

```python
import functools

import jax
import jax.numpy as jnp
from jax import lax
from jax.experimental import pallas as pl
from jax.experimental.pallas import tpu as pltpu
from jax.sharding import PartitionSpec as P

D = 512
HEADS = 4
DH = 128
MAXLEN = 192


epsilon = 1e-06
logit_divisor = 0.015625
loss_scale = 512.0


def reduce_last_dimension(operand, other_side):
    return lax.dot_general(
        operand, other_side, (((1,), (1,)), ((), ())), preferred_element_type=jnp.float32
    )


def contract_first(operand, other_side):
    return lax.dot_general(
        operand, other_side, (((0,), (0,)), ((), ())), preferred_element_type=jnp.float32
    )


def silu_slope(values):
    sigmoid = jax.nn.sigmoid(values)
    return sigmoid * (1.0 + values * (1.0 - sigmoid))


def history_mask(lengths_row, rows_count):
    history_ends = jnp.cumsum(lengths_row)
    positions = jnp.arange(rows_count, dtype=jnp.int32)
    history_ids = jnp.sum((positions[:, None] >= history_ends[None, :-1]).astype(jnp.int32), axis=1)
    visible = (history_ids[:, None] == history_ids[None, :]) & (
        positions[None, :] <= positions[:, None]
    )
    return jnp.where(visible, 1.0, 0.0).astype(jnp.float32)


def head_columns(activated, section, head_index):
    first_col = section * D + head_index * DH
    return activated[:, first_col : first_col + DH]


def head_scores(queries, key_rows):
    return reduce_last_dimension(queries, key_rows) * DH ** (-0.5)


def head_weights(scores, visible):
    return (jax.nn.silu(scores) * visible * (1.0 / MAXLEN)).astype(jnp.bfloat16)


def forward_layer(tokens, project, w_out, visible):
    wide_tokens = tokens.astype(jnp.float32)
    input_scale = lax.rsqrt(jnp.mean(wide_tokens * wide_tokens, axis=1, keepdims=True) + epsilon)
    normed = (wide_tokens * input_scale).astype(jnp.bfloat16)
    pre_act = project(normed)
    activated = lax.optimization_barrier(jax.nn.silu(pre_act).astype(jnp.bfloat16))
    heads_out = []
    for head_index in range(HEADS):
        queries = head_columns(activated, 2, head_index)
        key_rows = head_columns(activated, 3, head_index)
        value_rows = head_columns(activated, 1, head_index)
        weights = head_weights(head_scores(queries, key_rows), visible)
        heads_out.append(jnp.dot(weights, value_rows, preferred_element_type=jnp.float32))
    joined = lax.optimization_barrier(jnp.concatenate(heads_out, axis=1).astype(jnp.bfloat16))
    joined_wide = joined.astype(jnp.float32)
    middle_scale = lax.rsqrt(jnp.mean(joined_wide * joined_wide, axis=1, keepdims=True) + epsilon)
    gate_wide = activated[:, :D].astype(jnp.float32)
    gated = (joined_wide * middle_scale * gate_wide).astype(jnp.bfloat16)
    layer_out = wide_tokens + jnp.dot(gated, w_out, preferred_element_type=jnp.float32)
    return (layer_out, (wide_tokens, input_scale, pre_act, activated, joined, middle_scale, gated))


def loss_head(layer_out, clicked_product_vectors, sampled_decoys):
    out_scale = lax.rsqrt(jnp.sum(layer_out * layer_out, axis=1, keepdims=True) + epsilon)
    normalized_example_vectors = lax.optimization_barrier(
        (layer_out * out_scale).astype(jnp.bfloat16)
    )
    normalized_complete_embedding = normalized_example_vectors.astype(jnp.float32)
    correct_logit_entry = (
        jnp.sum(normalized_complete_embedding * clicked_product_vectors.astype(jnp.float32), axis=1)
        / logit_divisor
    )
    decoy_logit_entries = (
        reduce_last_dimension(normalized_example_vectors, sampled_decoys) / logit_divisor
    )
    target_exp = jnp.exp(correct_logit_entry)
    negative_exp = jnp.exp(decoy_logit_entries)
    totals = target_exp + jnp.sum(negative_exp, axis=1)
    target_prob = target_exp / totals
    negative_probs = (loss_scale * negative_exp / totals[:, None]).astype(jnp.bfloat16)
    target_coef = (loss_scale * (target_prob - 1.0))[:, None]
    grad_unit = target_coef * clicked_product_vectors.astype(jnp.float32) + jnp.dot(
        negative_probs, sampled_decoys, preferred_element_type=jnp.float32
    )
    grad_out = out_scale * grad_unit - layer_out * out_scale**3 * jnp.sum(
        layer_out * grad_unit, axis=1, keepdims=True
    )
    grad_target = target_coef * normalized_complete_embedding
    return (grad_out, grad_target, negative_probs, normalized_example_vectors)


def backward_layer(grad_out, saved_state, project_back, w_out, visible):
    wide_tokens, input_scale, pre_act, activated, joined, middle_scale, gated = saved_state
    grad_out_b = grad_out.astype(jnp.bfloat16)
    weight_part = contract_first(gated, grad_out_b)
    grad_gated = reduce_last_dimension(grad_out_b, w_out)
    joined_wide = joined.astype(jnp.float32)
    gate_wide = activated[:, :D].astype(jnp.float32)
    grad_gate = grad_gated * joined_wide * middle_scale
    grad_norm = grad_gated * gate_wide
    grad_joined = middle_scale * grad_norm - joined_wide * middle_scale**3 * jnp.mean(
        joined_wide * grad_norm, axis=1, keepdims=True
    )
    grad_joined_b = grad_joined.astype(jnp.bfloat16)
    grad_values = []
    grad_queries = []
    grad_keys = []
    for head_index in range(HEADS):
        queries = head_columns(activated, 2, head_index)
        key_rows = head_columns(activated, 3, head_index)
        value_rows = head_columns(activated, 1, head_index)
        scores = head_scores(queries, key_rows)
        weights = head_weights(scores, visible)
        grad_head = grad_joined_b[:, head_index * DH : (head_index + 1) * DH]
        grad_weights = reduce_last_dimension(grad_head, value_rows)
        grad_values.append(contract_first(weights, grad_head))
        grad_scores = (
            grad_weights * visible * (1.0 / MAXLEN) * silu_slope(scores) * DH ** (-0.5)
        ).astype(jnp.bfloat16)
        grad_queries.append(jnp.dot(grad_scores, key_rows, preferred_element_type=jnp.float32))
        grad_keys.append(contract_first(grad_scores, queries))
    grad_act = jnp.concatenate([grad_gate] + grad_values + grad_queries + grad_keys, axis=1)
    grad_pre = (grad_act * silu_slope(pre_act)).astype(jnp.bfloat16)
    grad_normed = project_back(grad_pre)
    grad_input = input_scale * grad_normed - wide_tokens * input_scale**3 * jnp.mean(
        wide_tokens * grad_normed, axis=1, keepdims=True
    )
    return ((grad_out + grad_input).astype(jnp.bfloat16), weight_part)


def finish_rows(grad_items, rows_wide):
    item_scale = lax.rsqrt(jnp.sum(rows_wide * rows_wide, axis=1, keepdims=True) + epsilon)
    return (
        item_scale * grad_items
        - rows_wide * item_scale**3 * jnp.sum(rows_wide * grad_items, axis=1, keepdims=True)
    ) / loss_scale


def plain_shards(tokens, w_proj, w_out, item_rows, lengths, target_owner, target_row, negative_rows):
    tok_rows = tokens.shape[0]
    model_width = tokens.shape[1]
    shard_count = lax.axis_size("shard")
    capacity = 2 * tok_rows // shard_count
    visible = history_mask(lengths[0], tok_rows)

    def project(normed):
        return jnp.dot(
            normed,
            lax.all_gather(w_proj, "shard", axis=1, tiled=True),
            preferred_element_type=jnp.float32,
        )

    def project_back(grad_pre):
        return reduce_last_dimension(grad_pre, lax.all_gather(w_proj, "shard", axis=1, tiled=True))

    rows_wide = item_rows.astype(jnp.float32)
    item_scale = lax.rsqrt(jnp.sum(rows_wide * rows_wide, axis=1, keepdims=True) + epsilon)
    unit_items = (rows_wide * item_scale).astype(jnp.bfloat16)
    owners = target_owner[:, 0]
    owner_hits = (owners[:, None] == jnp.arange(shard_count, dtype=jnp.int32)[None, :]).astype(
        jnp.int32
    )
    earlier = jnp.cumsum(owner_hits, axis=0) - owner_hits
    slot_index = jnp.sum(earlier * owner_hits, axis=1)
    position = owners * capacity + slot_index
    requests = jnp.zeros((shard_count * capacity,), jnp.int32).at[position].set(target_row)
    asked_rows = lax.all_to_all(
        requests.reshape(shard_count, capacity), "shard", split_axis=0, concat_axis=0, tiled=True
    )
    asked_flat = asked_rows.reshape(-1)
    served = jnp.take(unit_items, asked_flat, axis=0).reshape(shard_count, capacity, model_width)
    fetched = lax.all_to_all(served, "shard", split_axis=0, concat_axis=0, tiled=True)
    clicked_product_vectors = jnp.take(
        fetched.reshape(shard_count * capacity, model_width), position, axis=0
    )
    sampled_decoys = lax.all_gather(
        jnp.take(unit_items, negative_rows, axis=0), "shard", axis=0, tiled=True
    )
    layer_out, saved_state = forward_layer(tokens, project, w_out, visible)
    grad_out, grad_target, negative_probs, normalized_example_vectors = loss_head(
        layer_out, clicked_product_vectors, sampled_decoys
    )
    grad_tokens, weight_part = backward_layer(grad_out, saved_state, project_back, w_out, visible)
    outgoing = (
        jnp.zeros((shard_count * capacity, model_width), jnp.float32).at[position].set(grad_target)
    )
    returned = lax.all_to_all(
        outgoing.reshape(shard_count, capacity, model_width).astype(jnp.bfloat16),
        "shard",
        split_axis=0,
        concat_axis=0,
        tiled=True,
    ).astype(jnp.float32)
    grad_items = (
        jnp.zeros((item_rows.shape[0], model_width), jnp.float32)
        .at[asked_flat]
        .add(returned.reshape(-1, model_width))
    )
    own_negatives = lax.psum_scatter(
        contract_first(negative_probs, normalized_example_vectors).astype(jnp.bfloat16),
        "shard",
        scatter_dimension=0,
        tiled=True,
    ).astype(jnp.float32)
    grad_items = grad_items.at[negative_rows].add(own_negatives)
    share_rows = item_rows.shape[0] // lax.axis_size("dp")
    summed_share = lax.psum_scatter(
        grad_items.astype(jnp.bfloat16), "dp", scatter_dimension=0, tiled=True
    ).astype(jnp.float32)
    share_start = lax.axis_index("dp") * share_rows
    share_wide = lax.dynamic_slice_in_dim(rows_wide, share_start, share_rows, 0)
    item_grads = lax.all_gather(
        finish_rows(summed_share, share_wide).astype(jnp.bfloat16), "dp", axis=0, tiled=True
    ).astype(jnp.float32)
    weight_grads = lax.psum(weight_part, ("dp", "shard")) / loss_scale
    return (grad_tokens, weight_grads, item_grads)


MESH = pl.DeviceIdType.MESH


def start_copy(src, dst, sems, index, target):
    send_sem, recv_sem = sems
    copy = pltpu.make_async_remote_copy(
        src_ref=src,
        dst_ref=dst,
        send_sem=send_sem.at[index],
        recv_sem=recv_sem.at[index],
        device_id=target,
        device_id_type=MESH,
    )
    copy.start()
    return copy


def greet(peers):
    barrier = pltpu.get_barrier_semaphore()
    for peer in peers:
        pl.semaphore_signal(barrier, inc=1, device_id=peer, device_id_type=MESH)
    pl.semaphore_wait(barrier, len(peers))


def places(n_dp, n_shard):
    dp = lax.axis_index("dp")
    shard = lax.axis_index("shard")
    core = lax.rem(dp, 2)
    height = dp // 2
    sibling = (dp + 1 - 2 * core, shard)
    shard_peers = [(dp, lax.rem(shard + k, n_shard)) for k in range(1, n_shard)]
    shard_from = [lax.rem(shard + n_shard - k, n_shard) for k in range(1, n_shard)]
    n_z = n_dp // 2
    z_to = [lax.rem(height + k, n_z) for k in range(1, n_z)]
    z_peers = [(z * 2 + core, shard) for z in z_to]
    z_from = [lax.rem(height + n_z - k, n_z) for k in range(1, n_z)]
    return dp, shard, core, height, sibling, shard_peers, shard_from, z_to, z_peers, z_from


def token_slots(position, slots):
    tok_rows = position.shape[0]
    columns = lax.broadcasted_iota(jnp.int32, (tok_rows, slots), 1)
    return columns == position


def row_picks(asked_row, rows_count):
    rows = lax.broadcasted_iota(jnp.int32, (rows_count, asked_row.shape[1]), 0)
    return jnp.where(rows == asked_row, 1.0, 0.0).astype(jnp.bfloat16)


def fetch_kernel(
    n_dp,
    n_shard,
    capacity,
    w_ref,
    items_ref,
    owner_col_ref,
    owner_row_ref,
    target_col_ref,
    negative_col_ref,
    w_full,
    clicked,
    negatives,
    asked,
    position_ref,
    requests,
    served,
    fetched,
    unit,
    w_send,
    w_recv,
    pair_send,
    pair_recv,
    ask_send,
    ask_recv,
    neg_send,
    neg_recv,
    row_send,
    row_recv,
):
    dp, shard, core, height, sibling, peers, sources, z_to, z_peers, z_from = places(n_dp, n_shard)
    greet(peers + [sibling])
    rows_count = items_ref.shape[0]
    half = w_ref.shape[0] // 2
    mine = pl.ds(pl.multiple_of(core * half, half), half)
    copies = []
    w_copies = []
    for k, peer in enumerate(peers):
        w_copies.append(
            start_copy(w_ref.at[mine], w_full.at[shard, mine], (w_send, w_recv), k, peer)
        )
    owner_col = owner_col_ref[...]
    tok_rows = owner_col.shape[0]
    token_a = lax.broadcasted_iota(jnp.int32, (tok_rows, tok_rows), 0)
    token_b = lax.broadcasted_iota(jnp.int32, (tok_rows, tok_rows), 1)
    same = (owner_row_ref[...] == owner_col) & (token_b < token_a)
    slot = jnp.sum(jnp.where(same, 1.0, 0.0), axis=1, keepdims=True).astype(jnp.int32)
    position = owner_col * capacity + slot
    position_ref[...] = position
    slots = token_slots(position, n_shard * capacity)
    target = target_col_ref[...].astype(jnp.float32)
    request = jnp.sum(jnp.where(slots, target, 0.0), axis=0, keepdims=True).astype(jnp.int32)
    for j in range(n_shard):
        part = request[:, j * capacity : (j + 1) * capacity]
        requests[j] = jnp.broadcast_to(part, (8, capacity))
    ask_copies = []
    for k, peer in enumerate(peers):
        ask_copies.append(
            start_copy(requests.at[peer[1]], asked.at[shard], (ask_send, ask_recv), k, peer)
        )
    asked[shard] = requests[shard]
    rows_wide = items_ref[...].astype(jnp.float32)
    item_scale = lax.rsqrt(jnp.sum(rows_wide * rows_wide, axis=1, keepdims=True) + epsilon)
    unit[...] = (rows_wide * item_scale).astype(jnp.bfloat16)
    neg_col = negative_col_ref[...]
    neg_picks = token_slots(neg_col, rows_count)
    negatives[shard] = jnp.dot(
        jnp.where(neg_picks, 1.0, 0.0).astype(jnp.bfloat16),
        unit[...],
        preferred_element_type=jnp.float32,
    ).astype(jnp.bfloat16)
    neg_copies = []
    for k, peer in enumerate(peers):
        neg_copies.append(
            start_copy(negatives.at[shard], negatives.at[shard], (neg_send, neg_recv), k, peer)
        )
    row_copies = []
    for k, source in enumerate(sources):
        ask_copies[k].wait_recv()
        picks = row_picks(asked[source][0:1], rows_count)
        served[source] = contract_first(picks, unit[...]).astype(jnp.bfloat16)
        row_copies.append(
            start_copy(
                served.at[source], fetched.at[shard], (row_send, row_recv), k, (dp, source)
            )
        )
    picks = row_picks(requests[shard][0:1], rows_count)
    fetched[shard] = contract_first(picks, unit[...]).astype(jnp.bfloat16)
    w_full[shard] = w_ref[...]
    for k, source in enumerate(sources):
        w_copies[k].wait_recv()
        piece = w_full.at[source, mine]
        copies.append(start_copy(piece, piece, (pair_send, pair_recv), k, sibling))
    for copy in neg_copies + row_copies:
        copy.wait_recv()
    slots_one = jnp.where(slots, 1.0, 0.0).astype(jnp.bfloat16)
    total = jnp.zeros(clicked.shape, jnp.float32)
    for j in range(n_shard):
        total += jnp.dot(
            slots_one[:, j * capacity : (j + 1) * capacity],
            fetched[j],
            preferred_element_type=jnp.float32,
        )
    clicked[...] = total.astype(jnp.bfloat16)
    for copy in copies:
        copy.wait()
    for copy in w_copies + ask_copies + neg_copies + row_copies:
        copy.wait_send()


def return_kernel(
    n_dp,
    n_shard,
    capacity,
    grad_target_ref,
    neg_part_ref,
    w_part_ref,
    position_ref,
    asked_ref,
    negative_col_ref,
    items_ref,
    gathered,
    w_gathered,
    out_shard,
    in_shard,
    out_pair,
    in_pair,
    out_z,
    in_z,
    a_send,
    a_recv,
    b_send,
    b_recv,
    c_send,
    c_recv,
    d_send,
    d_recv,
    e_send,
    e_recv,
    f_send,
    f_recv,
    g_send,
    g_recv,
):
    dp, shard, core, height, sibling, peers, sources, z_to, z_peers, z_from = places(n_dp, n_shard)
    greet(peers + [sibling] + z_peers)
    rows_count, width = items_ref.shape
    n_z = n_dp // 2
    neg_rows = negative_col_ref.shape[0]
    w_rows = w_part_ref.shape[0] // n_shard
    share = rows_count // n_dp
    w_share = w_rows // n_dp
    slots = token_slots(position_ref[...], n_shard * capacity)
    slots_one = jnp.where(slots, 1.0, 0.0).astype(jnp.bfloat16)
    grad_target = grad_target_ref[...]
    for j in range(n_shard):
        out_shard[j, 0:capacity] = contract_first(
            slots_one[:, j * capacity : (j + 1) * capacity], grad_target
        ).astype(jnp.bfloat16)
        out_shard[j, capacity : capacity + neg_rows] = neg_part_ref[
            j * neg_rows : (j + 1) * neg_rows
        ].astype(jnp.bfloat16)
        out_shard[j, capacity + neg_rows :] = w_part_ref[
            j * w_rows : (j + 1) * w_rows
        ].astype(jnp.bfloat16)
    a_copies = []
    for k, peer in enumerate(peers):
        a_copies.append(
            start_copy(out_shard.at[peer[1]], in_shard.at[shard], (a_send, a_recv), k, peer)
        )
    in_shard[shard] = out_shard[shard]
    grad_items = jnp.zeros((rows_count, width), jnp.float32)
    neg_sum = jnp.zeros((neg_rows, width), jnp.float32)
    w_sum = jnp.zeros((w_rows, width), jnp.float32)
    for source, copy in zip([shard] + sources, [None] + a_copies):
        if copy is not None:
            copy.wait_recv()
        picks = row_picks(asked_ref[source][0:1], rows_count)
        grad_items += jnp.dot(
            picks, in_shard[source, 0:capacity], preferred_element_type=jnp.float32
        )
        neg_sum += in_shard[source, capacity : capacity + neg_rows].astype(jnp.float32)
        w_sum += in_shard[source, capacity + neg_rows :].astype(jnp.float32)
    neg_picks = token_slots(negative_col_ref[...], rows_count)
    neg_ones = jnp.where(neg_picks, 1.0, 0.0).astype(jnp.bfloat16)
    grad_items += contract_first(neg_ones, neg_sum.astype(jnp.bfloat16))
    for z in range(n_z):
        for c in range(2):
            d = z * 2 + c
            out_pair[c, z, 0:share] = grad_items[d * share : (d + 1) * share].astype(jnp.bfloat16)
            out_pair[c, z, share:] = w_sum[d * w_share : (d + 1) * w_share].astype(jnp.bfloat16)
    b_copy = start_copy(out_pair.at[1 - core], in_pair, (b_send, b_recv), 0, sibling)
    b_copy.wait_recv()
    out_z[...] = (
        out_pair[core].astype(jnp.float32) + in_pair[...].astype(jnp.float32)
    ).astype(jnp.bfloat16)
    c_copies = []
    for k, peer in enumerate(z_peers):
        c_copies.append(
            start_copy(out_z.at[z_to[k]], in_z.at[height], (c_send, c_recv), k, peer)
        )
    total = out_z[height].astype(jnp.float32)
    for k, z in enumerate(z_from):
        c_copies[k].wait_recv()
        total += in_z[z].astype(jnp.float32)
    own = pl.ds(pl.multiple_of(dp * share, share), share)
    finished = finish_rows(total[0:share], items_ref[own].astype(jnp.float32))
    gathered[core, height, 0:share] = finished.astype(jnp.bfloat16)
    gathered[core, height, share:] = (total[share:] / loss_scale).astype(jnp.bfloat16)
    d_copies = []
    mine = gathered.at[core, height]
    for k, peer in enumerate(z_peers):
        d_copies.append(start_copy(mine, mine, (d_send, d_recv), k, peer))
    e_copies = [start_copy(mine, mine, (e_send, e_recv), 0, sibling)]
    for k, z in enumerate(z_from):
        d_copies[k].wait_recv()
        piece = gathered.at[core, z]
        e_copies.append(start_copy(piece, piece, (e_send, e_recv), k + 1, sibling))
    for z in range(n_z):
        w_gathered[shard, core, z * w_share : (z + 1) * w_share] = gathered[core, z, share:]
    f_copies = []
    mine = w_gathered.at[shard, core]
    for k, peer in enumerate(peers):
        f_copies.append(start_copy(mine, mine, (f_send, f_recv), k, peer))
    g_copies = [start_copy(mine, mine, (g_send, g_recv), 0, sibling)]
    for k, source in enumerate(sources):
        f_copies[k].wait_recv()
        piece = w_gathered.at[source, core]
        g_copies.append(start_copy(piece, piece, (g_send, g_recv), k + 1, sibling))
    for copy in e_copies + g_copies:
        copy.wait()
    b_copy.wait_send()
    for copy in a_copies + c_copies + d_copies + f_copies:
        copy.wait_send()


def dma(count):
    return [pltpu.SemaphoreType.DMA((count,))] * 2


def vmem_specs(count):
    return [pl.BlockSpec(memory_space=pltpu.VMEM)] * count


def shards(tokens, w_proj, w_out, item_rows, lengths, target_owner, target_row, negative_rows):
    tok_rows, width = tokens.shape
    n_shard = lax.axis_size("shard")
    n_dp = lax.axis_size("dp")
    n_z = n_dp // 2
    capacity = 2 * tok_rows // n_shard
    rows_count = item_rows.shape[0]
    neg_rows = negative_rows.shape[0]
    w_cols = w_proj.shape[1]
    w_rows = width // n_shard
    share = rows_count // n_dp
    w_share = w_rows // n_dp
    b16 = jnp.bfloat16
    shape = jax.ShapeDtypeStruct
    negative_col = negative_rows.reshape(-1, 1)
    w_full, clicked, negatives, asked, position = pl.pallas_call(
        functools.partial(fetch_kernel, n_dp, n_shard, capacity),
        out_shape=[
            shape((n_shard, width, w_cols), b16),
            shape((tok_rows, width), b16),
            shape((n_shard, neg_rows, width), b16),
            shape((n_shard, 8, capacity), jnp.int32),
            shape((tok_rows, 1), jnp.int32),
        ],
        in_specs=vmem_specs(6),
        out_specs=vmem_specs(5),
        scratch_shapes=[
            pltpu.VMEM((n_shard, 8, capacity), jnp.int32),
            pltpu.VMEM((n_shard, capacity, width), b16),
            pltpu.VMEM((n_shard, capacity, width), b16),
            pltpu.VMEM((rows_count, width), b16),
        ]
        + dma(n_shard - 1) * 5,
        compiler_params=pltpu.CompilerParams(
            collective_id=0, has_side_effects=True, vmem_limit_bytes=48 * 2**20
        ),
        name="fetch",
    )(
        w_proj,
        item_rows,
        target_owner,
        target_owner.reshape(1, -1),
        target_row.reshape(-1, 1),
        negative_col,
    )
    visible = history_mask(lengths[0], tok_rows)

    def project(normed):
        return jnp.concatenate(
            [
                jnp.dot(normed, w_full[j], preferred_element_type=jnp.float32)
                for j in range(n_shard)
            ],
            axis=1,
        )

    def project_back(grad_pre):
        return sum(
            reduce_last_dimension(grad_pre[:, j * w_cols : (j + 1) * w_cols], w_full[j])
            for j in range(n_shard)
        )

    layer_out, saved_state = forward_layer(tokens, project, w_out, visible)
    grad_out, grad_target, negative_probs, normalized = loss_head(
        layer_out, clicked, negatives.reshape(-1, width)
    )
    grad_tokens, w_part = backward_layer(grad_out, saved_state, project_back, w_out, visible)
    neg_part = contract_first(negative_probs, normalized)
    gathered, w_gathered = pl.pallas_call(
        functools.partial(return_kernel, n_dp, n_shard, capacity),
        out_shape=[
            shape((2, n_z, share + w_share, width), b16),
            shape((n_shard, 2, n_z * w_share, width), b16),
        ],
        in_specs=vmem_specs(7),
        out_specs=vmem_specs(2),
        scratch_shapes=[
            pltpu.VMEM((n_shard, capacity + neg_rows + w_rows, width), b16),
            pltpu.VMEM((n_shard, capacity + neg_rows + w_rows, width), b16),
            pltpu.VMEM((2, n_z, share + w_share, width), b16),
            pltpu.VMEM((n_z, share + w_share, width), b16),
            pltpu.VMEM((n_z, share + w_share, width), b16),
            pltpu.VMEM((n_z, share + w_share, width), b16),
        ]
        + dma(n_shard - 1)
        + dma(1)
        + dma(n_z - 1) * 2
        + dma(n_z)
        + dma(n_shard - 1)
        + dma(n_shard),
        compiler_params=pltpu.CompilerParams(
            collective_id=1, has_side_effects=True, vmem_limit_bytes=48 * 2**20
        ),
        name="give_back",
    )(
        grad_target.astype(b16),
        neg_part.astype(b16),
        w_part.astype(b16),
        position,
        asked,
        negative_col,
        item_rows,
    )
    item_grads = (
        gathered[:, :, :share].transpose(1, 0, 2, 3).reshape(rows_count, width).astype(jnp.float32)
    )
    weight_grads = (
        w_gathered.reshape(n_shard, 2, n_z, w_share, width)
        .transpose(0, 2, 1, 3, 4)
        .reshape(width, width)
        .astype(jnp.float32)
    )
    return (grad_tokens, weight_grads, item_grads)


def fits_kernels(mesh):
    n_dp, n_shard = mesh.shape["dp"], mesh.shape["shard"]
    return n_dp % 2 == 0 and n_dp > 2 and n_shard > 1 and D % (16 * n_dp * n_shard) == 0


def solution(mesh):
    in_specs = (
        P(("dp", "shard"), None),
        P(None, "shard"),
        P(),
        P("shard", None),
        P(("dp", "shard"), None),
        P(("dp", "shard"), None),
        P(("dp", "shard")),
        P("shard"),
    )
    out_specs = (P(("dp", "shard"), None), P(), P("shard", None))
    return jax.shard_map(
        shards if fits_kernels(mesh) else plain_shards,
        mesh=mesh, in_specs=in_specs, out_specs=out_specs, check_vma=False)
```

```python
import functools

import jax
import jax.numpy as jnp
from jax import lax
from jax.experimental import pallas as pl
from jax.experimental.pallas import tpu as pltpu
from jax.sharding import PartitionSpec as P

D = 512
HEADS = 4
DH = 128
MAXLEN = 192


epsilon = 1e-06
logit_divisor = 0.015625
loss_scale = 512.0


def reduce_last_dimension(operand, other_side):
    return lax.dot_general(
        operand, other_side, (((1,), (1,)), ((), ())), preferred_element_type=jnp.float32
    )


def contract_first(operand, other_side):
    return lax.dot_general(
        operand, other_side, (((0,), (0,)), ((), ())), preferred_element_type=jnp.float32
    )


def silu_slope(values):
    sigmoid = jax.nn.sigmoid(values)
    return sigmoid * (1.0 + values * (1.0 - sigmoid))


def history_mask(lengths_row, rows_count):
    history_ends = jnp.cumsum(lengths_row)
    positions = jnp.arange(rows_count, dtype=jnp.int32)
    history_ids = jnp.sum((positions[:, None] >= history_ends[None, :-1]).astype(jnp.int32), axis=1)
    visible = (history_ids[:, None] == history_ids[None, :]) & (
        positions[None, :] <= positions[:, None]
    )
    return jnp.where(visible, 1.0, 0.0).astype(jnp.float32)


def head_columns(activated, section, head_index):
    first_col = section * D + head_index * DH
    return activated[:, first_col : first_col + DH]


def head_scores(queries, key_rows):
    return reduce_last_dimension(queries, key_rows) * DH ** (-0.5)


def head_weights(scores, visible):
    return (jax.nn.silu(scores) * visible * (1.0 / MAXLEN)).astype(jnp.bfloat16)


def forward_layer(tokens, project, w_out, visible):
    wide_tokens = tokens.astype(jnp.float32)
    input_scale = lax.rsqrt(jnp.mean(wide_tokens * wide_tokens, axis=1, keepdims=True) + epsilon)
    normed = (wide_tokens * input_scale).astype(jnp.bfloat16)
    pre_act = project(normed)
    activated = lax.optimization_barrier(jax.nn.silu(pre_act).astype(jnp.bfloat16))
    heads_out = []
    for head_index in range(HEADS):
        queries = head_columns(activated, 2, head_index)
        key_rows = head_columns(activated, 3, head_index)
        value_rows = head_columns(activated, 1, head_index)
        weights = head_weights(head_scores(queries, key_rows), visible)
        heads_out.append(jnp.dot(weights, value_rows, preferred_element_type=jnp.float32))
    joined = lax.optimization_barrier(jnp.concatenate(heads_out, axis=1).astype(jnp.bfloat16))
    joined_wide = joined.astype(jnp.float32)
    middle_scale = lax.rsqrt(jnp.mean(joined_wide * joined_wide, axis=1, keepdims=True) + epsilon)
    gate_wide = activated[:, :D].astype(jnp.float32)
    gated = (joined_wide * middle_scale * gate_wide).astype(jnp.bfloat16)
    layer_out = wide_tokens + jnp.dot(gated, w_out, preferred_element_type=jnp.float32)
    return (layer_out, (wide_tokens, input_scale, pre_act, activated, joined, middle_scale, gated))


def loss_head(layer_out, clicked_product_vectors, sampled_decoys):
    out_scale = lax.rsqrt(jnp.sum(layer_out * layer_out, axis=1, keepdims=True) + epsilon)
    normalized_example_vectors = lax.optimization_barrier(
        (layer_out * out_scale).astype(jnp.bfloat16)
    )
    normalized_complete_embedding = normalized_example_vectors.astype(jnp.float32)
    correct_logit_entry = (
        jnp.sum(normalized_complete_embedding * clicked_product_vectors.astype(jnp.float32), axis=1)
        / logit_divisor
    )
    decoy_logit_entries = (
        reduce_last_dimension(normalized_example_vectors, sampled_decoys) / logit_divisor
    )
    target_exp = jnp.exp(correct_logit_entry)
    negative_exp = jnp.exp(decoy_logit_entries)
    totals = target_exp + jnp.sum(negative_exp, axis=1)
    target_prob = target_exp / totals
    negative_probs = (loss_scale * negative_exp / totals[:, None]).astype(jnp.bfloat16)
    target_coef = (loss_scale * (target_prob - 1.0))[:, None]
    grad_unit = target_coef * clicked_product_vectors.astype(jnp.float32) + jnp.dot(
        negative_probs, sampled_decoys, preferred_element_type=jnp.float32
    )
    grad_out = out_scale * grad_unit - layer_out * out_scale**3 * jnp.sum(
        layer_out * grad_unit, axis=1, keepdims=True
    )
    grad_target = target_coef * normalized_complete_embedding
    return (grad_out, grad_target, negative_probs, normalized_example_vectors)


def backward_layer(grad_out, saved_state, project_back, w_out, visible):
    wide_tokens, input_scale, pre_act, activated, joined, middle_scale, gated = saved_state
    grad_out_b = grad_out.astype(jnp.bfloat16)
    weight_part = contract_first(gated, grad_out_b)
    grad_gated = reduce_last_dimension(grad_out_b, w_out)
    joined_wide = joined.astype(jnp.float32)
    gate_wide = activated[:, :D].astype(jnp.float32)
    grad_gate = grad_gated * joined_wide * middle_scale
    grad_norm = grad_gated * gate_wide
    grad_joined = middle_scale * grad_norm - joined_wide * middle_scale**3 * jnp.mean(
        joined_wide * grad_norm, axis=1, keepdims=True
    )
    grad_joined_b = grad_joined.astype(jnp.bfloat16)
    grad_values = []
    grad_queries = []
    grad_keys = []
    for head_index in range(HEADS):
        queries = head_columns(activated, 2, head_index)
        key_rows = head_columns(activated, 3, head_index)
        value_rows = head_columns(activated, 1, head_index)
        scores = head_scores(queries, key_rows)
        weights = head_weights(scores, visible)
        grad_head = grad_joined_b[:, head_index * DH : (head_index + 1) * DH]
        grad_weights = reduce_last_dimension(grad_head, value_rows)
        grad_values.append(contract_first(weights, grad_head))
        grad_scores = (
            grad_weights * visible * (1.0 / MAXLEN) * silu_slope(scores) * DH ** (-0.5)
        ).astype(jnp.bfloat16)
        grad_queries.append(jnp.dot(grad_scores, key_rows, preferred_element_type=jnp.float32))
        grad_keys.append(contract_first(grad_scores, queries))
    grad_act = jnp.concatenate([grad_gate] + grad_values + grad_queries + grad_keys, axis=1)
    grad_pre = (grad_act * silu_slope(pre_act)).astype(jnp.bfloat16)
    grad_normed = project_back(grad_pre)
    grad_input = input_scale * grad_normed - wide_tokens * input_scale**3 * jnp.mean(
        wide_tokens * grad_normed, axis=1, keepdims=True
    )
    return ((grad_out + grad_input).astype(jnp.bfloat16), weight_part)


def finish_rows(grad_items, rows_wide):
    item_scale = lax.rsqrt(jnp.sum(rows_wide * rows_wide, axis=1, keepdims=True) + epsilon)
    return (
        item_scale * grad_items
        - rows_wide * item_scale**3 * jnp.sum(rows_wide * grad_items, axis=1, keepdims=True)
    ) / loss_scale


def plain_shards(tokens, w_proj, w_out, item_rows, lengths, target_owner, target_row, negative_rows):
    tok_rows = tokens.shape[0]
    model_width = tokens.shape[1]
    shard_count = lax.axis_size("shard")
    capacity = 2 * tok_rows // shard_count
    visible = history_mask(lengths[0], tok_rows)

    def project(normed):
        return jnp.dot(
            normed,
            lax.all_gather(w_proj, "shard", axis=1, tiled=True),
            preferred_element_type=jnp.float32,
        )

    def project_back(grad_pre):
        return reduce_last_dimension(grad_pre, lax.all_gather(w_proj, "shard", axis=1, tiled=True))

    rows_wide = item_rows.astype(jnp.float32)
    item_scale = lax.rsqrt(jnp.sum(rows_wide * rows_wide, axis=1, keepdims=True) + epsilon)
    unit_items = (rows_wide * item_scale).astype(jnp.bfloat16)
    owners = target_owner[:, 0]
    owner_hits = (owners[:, None] == jnp.arange(shard_count, dtype=jnp.int32)[None, :]).astype(
        jnp.int32
    )
    earlier = jnp.cumsum(owner_hits, axis=0) - owner_hits
    slot_index = jnp.sum(earlier * owner_hits, axis=1)
    position = owners * capacity + slot_index
    requests = jnp.zeros((shard_count * capacity,), jnp.int32).at[position].set(target_row)
    asked_rows = lax.all_to_all(
        requests.reshape(shard_count, capacity), "shard", split_axis=0, concat_axis=0, tiled=True
    )
    asked_flat = asked_rows.reshape(-1)
    served = jnp.take(unit_items, asked_flat, axis=0).reshape(shard_count, capacity, model_width)
    fetched = lax.all_to_all(served, "shard", split_axis=0, concat_axis=0, tiled=True)
    clicked_product_vectors = jnp.take(
        fetched.reshape(shard_count * capacity, model_width), position, axis=0
    )
    sampled_decoys = lax.all_gather(
        jnp.take(unit_items, negative_rows, axis=0), "shard", axis=0, tiled=True
    )
    layer_out, saved_state = forward_layer(tokens, project, w_out, visible)
    grad_out, grad_target, negative_probs, normalized_example_vectors = loss_head(
        layer_out, clicked_product_vectors, sampled_decoys
    )
    grad_tokens, weight_part = backward_layer(grad_out, saved_state, project_back, w_out, visible)
    outgoing = (
        jnp.zeros((shard_count * capacity, model_width), jnp.float32).at[position].set(grad_target)
    )
    returned = lax.all_to_all(
        outgoing.reshape(shard_count, capacity, model_width).astype(jnp.bfloat16),
        "shard",
        split_axis=0,
        concat_axis=0,
        tiled=True,
    ).astype(jnp.float32)
    grad_items = (
        jnp.zeros((item_rows.shape[0], model_width), jnp.float32)
        .at[asked_flat]
        .add(returned.reshape(-1, model_width))
    )
    own_negatives = lax.psum_scatter(
        contract_first(negative_probs, normalized_example_vectors).astype(jnp.bfloat16),
        "shard",
        scatter_dimension=0,
        tiled=True,
    ).astype(jnp.float32)
    grad_items = grad_items.at[negative_rows].add(own_negatives)
    share_rows = item_rows.shape[0] // lax.axis_size("dp")
    summed_share = lax.psum_scatter(
        grad_items.astype(jnp.bfloat16), "dp", scatter_dimension=0, tiled=True
    ).astype(jnp.float32)
    share_start = lax.axis_index("dp") * share_rows
    share_wide = lax.dynamic_slice_in_dim(rows_wide, share_start, share_rows, 0)
    item_grads = lax.all_gather(
        finish_rows(summed_share, share_wide).astype(jnp.bfloat16), "dp", axis=0, tiled=True
    ).astype(jnp.float32)
    weight_grads = lax.psum(weight_part, ("dp", "shard")) / loss_scale
    return (grad_tokens, weight_grads, item_grads)


MESH = pl.DeviceIdType.MESH


def start_copy(src, dst, sems, index, target):
    send_sem, recv_sem = sems
    copy = pltpu.make_async_remote_copy(
        src_ref=src,
        dst_ref=dst,
        send_sem=send_sem.at[index],
        recv_sem=recv_sem.at[index],
        device_id=target,
        device_id_type=MESH,
    )
    copy.start()
    return copy


def places(n_dp, n_shard):
    dp = lax.axis_index("dp")
    shard = lax.axis_index("shard")
    core = lax.rem(dp, 2)
    height = dp // 2
    sibling = (dp + 1 - 2 * core, shard)
    shard_peers = [(dp, lax.rem(shard + k, n_shard)) for k in range(1, n_shard)]
    shard_from = [lax.rem(shard + n_shard - k, n_shard) for k in range(1, n_shard)]
    n_z = n_dp // 2
    z_to = [lax.rem(height + k, n_z) for k in range(1, n_z)]
    z_peers = [(z * 2 + core, shard) for z in z_to]
    z_from = [lax.rem(height + n_z - k, n_z) for k in range(1, n_z)]
    return dp, shard, core, height, sibling, shard_peers, shard_from, z_to, z_peers, z_from


def one_hot_columns(position, slots):
    columns = lax.broadcasted_iota(jnp.int32, (position.shape[0], slots), 1)
    return columns == position


def row_picks(asked_row, rows_count):
    rows = lax.broadcasted_iota(jnp.int32, (rows_count, asked_row.shape[1]), 0)
    return jnp.where(rows == asked_row, 1.0, 0.0).astype(jnp.bfloat16)


def as_column(row):
    count = row.shape[1]
    across = lax.broadcasted_iota(jnp.int32, (count, count), 0)
    along = lax.broadcasted_iota(jnp.int32, (count, count), 1)
    return jnp.sum(jnp.where(across == along, row, 0), axis=1, keepdims=True)


def as_row(column):
    count = column.shape[0]
    across = lax.broadcasted_iota(jnp.int32, (count, count), 0)
    along = lax.broadcasted_iota(jnp.int32, (count, count), 1)
    return jnp.sum(jnp.where(across == along, column, 0), axis=0, keepdims=True)


def ones_of(picks):
    return jnp.where(picks, 1.0, 0.0).astype(jnp.bfloat16)


def visible_pairs(lengths, rows_count):
    across = lax.broadcasted_iota(jnp.int32, (rows_count, rows_count), 0)
    along = lax.broadcasted_iota(jnp.int32, (rows_count, rows_count), 1)
    history_a = jnp.zeros((rows_count, rows_count), jnp.int32)
    history_b = jnp.zeros((rows_count, rows_count), jnp.int32)
    end = jnp.zeros((1, 1), jnp.int32)
    for j in range(lengths.shape[1] - 1):
        end = end + lengths[:, j : j + 1]
        history_a += jnp.where(across >= end, 1, 0)
        history_b += jnp.where(along >= end, 1, 0)
    return jnp.where((history_a == history_b) & (along <= across), 1.0 / MAXLEN, 0.0)


def layer_kernel(
    n_dp,
    n_shard,
    capacity,
    tokens_ref,
    w_ref,
    w_out_ref,
    items_ref,
    lengths_ref,
    owner_ref,
    target_ref,
    negative_ref,
    grad_tokens_ref,
    gathered,
    w_gathered,
    w_full,
    negatives,
    requests,
    asked,
    served,
    fetched,
    unit,
    pre,
    act,
    scores_ref,
    visible_ref,
    normed_ref,
    joined_ref,
    grad_joined_ref,
    grad_out_ref,
    grad_pre,
    out_rows,
    in_rows,
    pair_sums,
    pair_in,
    out_sums,
    in_sums,
    out_pair,
    in_pair,
    out_z,
    in_z,
    send_sem,
    recv_sem,
):
    dp, shard, core, height, sibling, peers, sources, z_to, z_peers, z_from = places(n_dp, n_shard)
    n_z = n_dp // 2
    others = sources
    near = range(n_shard - 1)
    barrier = pltpu.get_barrier_semaphore()
    greeted = peers + [sibling] + z_peers
    for peer in greeted:
        pl.semaphore_signal(barrier, inc=1, device_id=peer, device_id_type=MESH)
    used = [0]
    started = []

    def send(src, dst, target):
        copy = start_copy(src, dst, (send_sem, recv_sem), used[0], target)
        used[0] += 1
        started.append(copy)
        return copy

    rows_count, width = items_ref.shape
    tok_rows = tokens_ref.shape[0]
    neg_rows = negative_ref.shape[1]
    neg_half = neg_rows // 2
    half = w_ref.shape[0] // 2
    share = rows_count // n_dp
    w_rows = width // n_shard
    w_half = w_rows // 2
    w_share = w_half // n_z
    n_parts, part_cols = out_rows.shape[0], out_rows.shape[-1]

    owner_col = owner_ref[...]
    token_a = lax.broadcasted_iota(jnp.int32, (tok_rows, tok_rows), 0)
    token_b = lax.broadcasted_iota(jnp.int32, (tok_rows, tok_rows), 1)
    same = (as_row(owner_col) == owner_col) & (token_b < token_a)
    slot = jnp.sum(jnp.where(same, 1.0, 0.0), axis=1, keepdims=True).astype(jnp.int32)
    position = owner_col * capacity + slot
    slots = one_hot_columns(position, n_shard * capacity)
    target = as_column(target_ref[...])
    request = jnp.sum(jnp.where(slots, target, 0), axis=0, keepdims=True)
    for j in range(n_shard):
        part = request[:, j * capacity : (j + 1) * capacity]
        requests[j] = jnp.broadcast_to(part, (8, capacity))
    slots_one = ones_of(slots)

    pl.semaphore_wait(barrier, len(greeted))
    ask_copies = [send(requests.at[peer[1]], asked.at[shard], peer) for peer in peers]
    mine = pl.ds(pl.multiple_of(core * half, half), half)
    w_copies = [send(w_ref.at[mine], w_full.at[shard, mine], peer) for peer in peers]
    asked[shard] = requests[shard]

    rows_wide = items_ref[...].astype(jnp.float32)
    item_scale = lax.rsqrt(jnp.sum(rows_wide * rows_wide, axis=1, keepdims=True) + epsilon)
    unit[...] = (rows_wide * item_scale).astype(jnp.bfloat16)
    negative_col = as_column(negative_ref[...])
    own_negatives = jnp.dot(
        ones_of(one_hot_columns(negative_col, rows_count)),
        unit[...],
        preferred_element_type=jnp.float32,
    ).astype(jnp.bfloat16)
    negatives[shard, 0] = own_negatives[:neg_half]
    negatives[shard, 1] = own_negatives[neg_half:]
    neg_piece = negatives.at[shard, core]
    neg_copies = [send(neg_piece, neg_piece, peer) for peer in peers]
    w_full[shard] = w_ref[...]
    wide_tokens = tokens_ref[...].astype(jnp.float32)
    input_scale = lax.rsqrt(jnp.mean(wide_tokens * wide_tokens, axis=1, keepdims=True) + epsilon)
    normed_ref[...] = (wide_tokens * input_scale).astype(jnp.bfloat16)
    visible_ref[...] = visible_pairs(lengths_ref[...], tok_rows)

    def section(j):
        values = jnp.dot(normed_ref[...], w_full[j], preferred_element_type=jnp.float32)
        pre[j] = values
        act[j] = (values * lax.logistic(values)).astype(jnp.bfloat16)

    section(shard)
    for k, source in enumerate(others):
        ask_copies[k].wait_recv()
        picks = row_picks(asked[source][0:1], rows_count)
        served[source] = contract_first(picks, unit[...]).astype(jnp.bfloat16)
    picks = row_picks(requests[shard][0:1], rows_count)
    fetched[shard] = contract_first(picks, unit[...]).astype(jnp.bfloat16)
    w_pairs = []
    for k, source in enumerate(others):
        w_copies[k].wait_recv()
        piece = w_full.at[source, mine]
        w_pairs.append(send(piece, piece, sibling))
    row_copies = [
        send(served.at[source], fetched.at[shard], (dp, source)) for source in others
    ]
    neg_pairs = []
    for k, source in enumerate(others):
        neg_copies[k].wait_recv()
        piece = negatives.at[source, core]
        neg_pairs.append(send(piece, piece, sibling))
    for k, source in enumerate(others):
        w_pairs[k].wait_recv()
        section(source)

    def head_part(j, head):
        return act[j, :, head * DH : (head + 1) * DH]

    for head in range(HEADS):
        scores = head_scores(head_part(2, head), head_part(3, head))
        scores_ref[head] = scores
        weights = (scores * lax.logistic(scores) * visible_ref[...]).astype(jnp.bfloat16)
        joined_ref[:, head * DH : (head + 1) * DH] = jnp.dot(
            weights, head_part(1, head), preferred_element_type=jnp.float32
        ).astype(jnp.bfloat16)
    joined_wide = joined_ref[...].astype(jnp.float32)
    middle_scale = lax.rsqrt(jnp.mean(joined_wide * joined_wide, axis=1, keepdims=True) + epsilon)
    gate_wide = act[0].astype(jnp.float32)
    gated = (joined_wide * middle_scale * gate_wide).astype(jnp.bfloat16)
    layer_out = tokens_ref[...].astype(jnp.float32) + jnp.dot(
        gated, w_out_ref[...], preferred_element_type=jnp.float32
    )
    out_scale = lax.rsqrt(jnp.sum(layer_out * layer_out, axis=1, keepdims=True) + epsilon)
    unit_b = (layer_out * out_scale).astype(jnp.bfloat16)
    for copy in neg_pairs:
        copy.wait_recv()
    negative_exps = []
    for j in range(n_shard):
        for c in range(2):
            logits = reduce_last_dimension(unit_b, negatives[j, c]) / logit_divisor
            negative_exps.append(jnp.exp(logits))
    negative_exp = jnp.concatenate(negative_exps, axis=1)
    for copy in row_copies:
        copy.wait_recv()
    clicked = jnp.zeros((tok_rows, width), jnp.float32)
    for j in range(n_shard):
        clicked += jnp.dot(
            slots_one[:, j * capacity : (j + 1) * capacity],
            fetched[j],
            preferred_element_type=jnp.float32,
        )
    unit_wide = unit_b.astype(jnp.float32)
    target_logit = jnp.sum(unit_wide * clicked, axis=1, keepdims=True) / logit_divisor
    target_exp = jnp.exp(target_logit)
    totals = target_exp + jnp.sum(negative_exp, axis=1, keepdims=True)
    negative_probs = (loss_scale * negative_exp / totals).astype(jnp.bfloat16)
    target_coef = loss_scale * (target_exp / totals - 1.0)
    grad_target = (target_coef * unit_wide).astype(jnp.bfloat16)

    row_sends = []
    for h in range(n_parts):
        for j in range(n_shard):
            out_rows[h, j] = contract_first(
                slots_one[:, j * capacity : (j + 1) * capacity],
                grad_target[:, h * part_cols : (h + 1) * part_cols],
            ).astype(jnp.bfloat16)
        if h == 0:
            row_sends.append(
                [send(out_rows.at[h, peer[1]], in_rows.at[h, shard], peer) for peer in peers]
            )
    grad_unit = target_coef * clicked
    for j in range(n_shard):
        for c in range(2):
            first = (2 * j + c) * neg_half
            grad_unit += jnp.dot(
                negative_probs[:, first : first + neg_half],
                negatives[j, c],
                preferred_element_type=jnp.float32,
            )
    grad_out = out_scale * grad_unit - layer_out * out_scale**3 * jnp.sum(
        layer_out * grad_unit, axis=1, keepdims=True
    )
    grad_out_ref[...] = grad_out
    grad_out_b = grad_out.astype(jnp.bfloat16)
    neg_part = contract_first(negative_probs, unit_b).astype(jnp.bfloat16)
    w_part = contract_first(gated, grad_out_b).astype(jnp.bfloat16)
    for h in range(n_parts):
        cols = slice(h * part_cols, (h + 1) * part_cols)
        for j in range(n_shard):
            for c in range(2):
                first = (2 * j + c) * neg_half
                pair_sums[c, h, j, 0:neg_half] = neg_part[first : first + neg_half, cols]
                first = (2 * j + c) * w_half
                pair_sums[c, h, j, neg_half:] = w_part[first : first + w_half, cols]
    sum_pair = send(pair_sums.at[1 - core], pair_in, sibling)
    sum_pair.wait_recv()
    out_sums[...] = (
        pair_sums[core].astype(jnp.float32) + pair_in[...].astype(jnp.float32)
    ).astype(jnp.bfloat16)
    sum_sends = []
    for h in range(n_parts):
        if h > 0:
            row_sends.append(
                [send(out_rows.at[h, peer[1]], in_rows.at[h, shard], peer) for peer in peers]
            )
        sum_sends.append(
            [send(out_sums.at[h, peer[1]], in_sums.at[h, shard], peer) for peer in peers]
        )

    grad_gated = reduce_last_dimension(grad_out_b, w_out_ref[...])
    grad_pre[0] = (grad_gated * joined_wide * middle_scale * silu_slope(pre[0])).astype(
        jnp.bfloat16
    )
    grad_norm = grad_gated * gate_wide
    grad_joined_ref[...] = (
        middle_scale * grad_norm
        - joined_wide
        * middle_scale**3
        * jnp.mean(joined_wide * grad_norm, axis=1, keepdims=True)
    ).astype(jnp.bfloat16)

    def head_back(head):
        cols = slice(head * DH, (head + 1) * DH)
        scores = scores_ref[head]
        sigmoid = lax.logistic(scores)
        visible = visible_ref[...]
        weights = (scores * sigmoid * visible).astype(jnp.bfloat16)
        grad_head = grad_joined_ref[:, cols]
        grad_weights = reduce_last_dimension(grad_head, head_part(1, head))
        slope = sigmoid * (1.0 + scores * (1.0 - sigmoid))
        grad_scores = (grad_weights * visible * slope * DH ** (-0.5)).astype(jnp.bfloat16)
        grads = (
            contract_first(weights, grad_head),
            jnp.dot(grad_scores, head_part(3, head), preferred_element_type=jnp.float32),
            contract_first(grad_scores, head_part(2, head)),
        )
        for j, grad in enumerate(grads):
            grad_pre[j + 1, :, cols] = (grad * silu_slope(pre[j + 1, :, cols])).astype(
                jnp.bfloat16
            )

    def collect(h):
        grad_items = jnp.zeros((rows_count, part_cols), jnp.float32)
        sums = jnp.zeros((neg_half + w_half, part_cols), jnp.float32)
        for k, source in enumerate([shard] + others):
            if k > 0:
                row_sends[h][k - 1].wait_recv()
                sum_sends[h][k - 1].wait_recv()
            rows = out_rows[h, shard] if k == 0 else in_rows[h, source]
            part = out_sums[h, shard] if k == 0 else in_sums[h, source]
            picks = row_picks(asked[source][0:1], rows_count)
            grad_items += jnp.dot(picks, rows, preferred_element_type=jnp.float32)
            sums += part.astype(jnp.float32)
        rows = lax.broadcasted_iota(jnp.int32, (neg_half, rows_count), 1)
        own_rows = jnp.where(core == 0, negative_col[:neg_half], negative_col[neg_half:])
        grad_items += contract_first(
            ones_of(rows == own_rows), sums[0:neg_half].astype(jnp.bfloat16)
        )
        for z in range(n_z):
            for c in range(2):
                d = z * 2 + c
                out_pair[h, c, z] = grad_items[d * share : (d + 1) * share].astype(jnp.bfloat16)
            first = neg_half + z * w_share
            out_z[h, z, share:] = sums[first : first + w_share].astype(jnp.bfloat16)
        return send(out_pair.at[h, 1 - core], in_pair.at[h], sibling)

    def pass_on(h, pair):
        pair.wait_recv()
        for z in range(n_z):
            out_z[h, z, 0:share] = (
                out_pair[h, core, z].astype(jnp.float32) + in_pair[h, z].astype(jnp.float32)
            ).astype(jnp.bfloat16)
        return [
            send(out_z.at[h, z_to[k]], in_z.at[h, height], peer) for k, peer in enumerate(z_peers)
        ]

    head_back(0)
    pair = collect(0)
    head_back(1)
    z_sends = [pass_on(0, pair)]
    for h in range(1, n_parts):
        pair = collect(h)
        head_back(2)
        z_sends.append(pass_on(h, pair))
    for head in range(3 if n_parts > 1 else 2, HEADS):
        head_back(head)
    grad_normed = jnp.zeros((tok_rows, width), jnp.float32)
    for j in range(n_shard):
        grad_normed += reduce_last_dimension(grad_pre[j], w_full[j])
    wide_tokens = tokens_ref[...].astype(jnp.float32)
    grad_input = input_scale * grad_normed - wide_tokens * input_scale**3 * jnp.mean(
        wide_tokens * grad_normed, axis=1, keepdims=True
    )
    grad_tokens_ref[...] = (grad_out_ref[...] + grad_input).astype(jnp.bfloat16)

    totals_parts = []
    for h in range(n_parts):
        total = out_z[h, height].astype(jnp.float32)
        for k, z in enumerate(z_from):
            z_sends[h][k].wait_recv()
            total += in_z[h, z].astype(jnp.float32)
        totals_parts.append(total)
    total = jnp.concatenate(totals_parts, axis=1)
    w_gathered[shard, core, height] = (total[share:] / loss_scale).astype(jnp.bfloat16)
    w_mine = w_gathered.at[shard, core, height]
    w_z = [send(w_mine, w_mine, peer) for peer in z_peers]
    own = pl.ds(pl.multiple_of(dp * share, share), share)
    finished = finish_rows(total[0:share], items_ref[own].astype(jnp.float32))
    gathered[core, height] = finished.astype(jnp.bfloat16)
    items_mine = gathered.at[core, height]
    items_z = [send(items_mine, items_mine, peer) for peer in z_peers]
    last = [send(items_mine, items_mine, sibling)]
    for copy in w_z:
        copy.wait_recv()
    w_block = w_gathered.at[shard, core]
    w_around = [send(w_block, w_block, peer) for peer in peers]
    last.append(send(w_block, w_block, sibling))
    for k, source in enumerate(others):
        w_around[k].wait_recv()
        piece = w_gathered.at[source, core]
        last.append(send(piece, piece, sibling))
    for k, z in enumerate(z_from):
        items_z[k].wait_recv()
        piece = gathered.at[core, z]
        last.append(send(piece, piece, sibling))
    for copy in last:
        copy.wait_recv()
    for copy in started:
        copy.wait_send()


def vmem_specs(count):
    return [pl.BlockSpec(memory_space=pltpu.VMEM)] * count


def shards(tokens, w_proj, w_out, item_rows, lengths, target_owner, target_row, negative_rows):
    tok_rows, width = tokens.shape
    n_shard = lax.axis_size("shard")
    n_dp = lax.axis_size("dp")
    n_z = n_dp // 2
    capacity = 2 * tok_rows // n_shard
    rows_count = item_rows.shape[0]
    neg_half = negative_rows.shape[0] // 2
    share = rows_count // n_dp
    w_half = width // n_shard // 2
    w_share = w_half // n_z
    parts = 2
    cols = width // parts
    b16 = jnp.bfloat16
    f32 = jnp.float32
    shape = jax.ShapeDtypeStruct
    copies = 7 * (n_shard - 1) + 4 * parts * (n_shard + n_z) + 2 * (n_shard + n_z) + 8
    grad_tokens, gathered, w_gathered = pl.pallas_call(
        functools.partial(layer_kernel, n_dp, n_shard, capacity),
        out_shape=[
            shape((tok_rows, width), b16),
            shape((2, n_z, share, width), b16),
            shape((n_shard, 2, n_z, w_share, width), b16),
        ],
        in_specs=vmem_specs(8),
        out_specs=vmem_specs(3),
        scratch_shapes=[
            pltpu.VMEM((n_shard, width, width), b16),
            pltpu.VMEM((n_shard, 2, neg_half, width), b16),
            pltpu.VMEM((n_shard, 8, capacity), jnp.int32),
            pltpu.VMEM((n_shard, 8, capacity), jnp.int32),
            pltpu.VMEM((n_shard, capacity, width), b16),
            pltpu.VMEM((n_shard, capacity, width), b16),
            pltpu.VMEM((rows_count, width), b16),
            pltpu.VMEM((4, tok_rows, width), f32),
            pltpu.VMEM((4, tok_rows, width), b16),
            pltpu.VMEM((HEADS, tok_rows, tok_rows), f32),
            pltpu.VMEM((tok_rows, tok_rows), f32),
            pltpu.VMEM((tok_rows, width), b16),
            pltpu.VMEM((tok_rows, width), b16),
            pltpu.VMEM((tok_rows, width), b16),
            pltpu.VMEM((tok_rows, width), f32),
            pltpu.VMEM((4, tok_rows, width), b16),
            pltpu.VMEM((parts, n_shard, capacity, cols), b16),
            pltpu.VMEM((parts, n_shard, capacity, cols), b16),
            pltpu.VMEM((2, parts, n_shard, neg_half + w_half, cols), b16),
            pltpu.VMEM((parts, n_shard, neg_half + w_half, cols), b16),
            pltpu.VMEM((parts, n_shard, neg_half + w_half, cols), b16),
            pltpu.VMEM((parts, n_shard, neg_half + w_half, cols), b16),
            pltpu.VMEM((parts, 2, n_z, share, cols), b16),
            pltpu.VMEM((parts, n_z, share, cols), b16),
            pltpu.VMEM((parts, n_z, share + w_share, cols), b16),
            pltpu.VMEM((parts, n_z, share + w_share, cols), b16),
            pltpu.SemaphoreType.DMA((copies,)),
            pltpu.SemaphoreType.DMA((copies,)),
        ],
        compiler_params=pltpu.CompilerParams(
            collective_id=0, has_side_effects=True, vmem_limit_bytes=56 * 2**20
        ),
        name="layer",
    )(
        tokens,
        w_proj,
        w_out,
        item_rows,
        lengths,
        target_owner,
        target_row.reshape(1, -1),
        negative_rows.reshape(1, -1),
    )
    item_grads = gathered.transpose(1, 0, 2, 3).reshape(rows_count, width).astype(f32)
    return (grad_tokens, w_gathered.reshape(width, width).astype(f32), item_grads)


def fits_kernels(mesh):
    n_dp, n_shard = mesh.shape["dp"], mesh.shape["shard"]
    return n_dp % 2 == 0 and n_dp > 2 and n_shard == 4 and D % (16 * n_dp * n_shard) == 0


def solution(mesh):
    in_specs = (
        P(("dp", "shard"), None),
        P(None, "shard"),
        P(),
        P("shard", None),
        P(("dp", "shard"), None),
        P(("dp", "shard"), None),
        P(("dp", "shard")),
        P("shard"),
    )
    out_specs = (P(("dp", "shard"), None), P(), P("shard", None))
    return jax.shard_map(
        shards if fits_kernels(mesh) else plain_shards,
        mesh=mesh, in_specs=in_specs, out_specs=out_specs, check_vma=False)
```

```python
import functools

import jax
import jax.numpy as jnp
from jax import lax
from jax.experimental import pallas as pl
from jax.experimental.pallas import tpu as pltpu
from jax.sharding import PartitionSpec as P

D = 512
HEADS = 4
DH = 128
MAXLEN = 192


epsilon = 1e-06
logit_divisor = 0.015625
loss_scale = 512.0


def reduce_last_dimension(operand, other_side):
    return lax.dot_general(
        operand, other_side, (((1,), (1,)), ((), ())), preferred_element_type=jnp.float32
    )


def contract_first(operand, other_side):
    return lax.dot_general(
        operand, other_side, (((0,), (0,)), ((), ())), preferred_element_type=jnp.float32
    )


def silu_slope(values):
    sigmoid = jax.nn.sigmoid(values)
    return sigmoid * (1.0 + values * (1.0 - sigmoid))


def history_mask(lengths_row, rows_count):
    history_ends = jnp.cumsum(lengths_row)
    positions = jnp.arange(rows_count, dtype=jnp.int32)
    history_ids = jnp.sum((positions[:, None] >= history_ends[None, :-1]).astype(jnp.int32), axis=1)
    visible = (history_ids[:, None] == history_ids[None, :]) & (
        positions[None, :] <= positions[:, None]
    )
    return jnp.where(visible, 1.0, 0.0).astype(jnp.float32)


def head_columns(activated, section, head_index):
    first_col = section * D + head_index * DH
    return activated[:, first_col : first_col + DH]


def head_scores(queries, key_rows):
    return reduce_last_dimension(queries, key_rows) * DH ** (-0.5)


def head_weights(scores, visible):
    return (jax.nn.silu(scores) * visible * (1.0 / MAXLEN)).astype(jnp.bfloat16)


def forward_layer(tokens, project, w_out, visible):
    wide_tokens = tokens.astype(jnp.float32)
    input_scale = lax.rsqrt(jnp.mean(wide_tokens * wide_tokens, axis=1, keepdims=True) + epsilon)
    normed = (wide_tokens * input_scale).astype(jnp.bfloat16)
    pre_act = project(normed)
    activated = lax.optimization_barrier(jax.nn.silu(pre_act).astype(jnp.bfloat16))
    heads_out = []
    for head_index in range(HEADS):
        queries = head_columns(activated, 2, head_index)
        key_rows = head_columns(activated, 3, head_index)
        value_rows = head_columns(activated, 1, head_index)
        weights = head_weights(head_scores(queries, key_rows), visible)
        heads_out.append(jnp.dot(weights, value_rows, preferred_element_type=jnp.float32))
    joined = lax.optimization_barrier(jnp.concatenate(heads_out, axis=1).astype(jnp.bfloat16))
    joined_wide = joined.astype(jnp.float32)
    middle_scale = lax.rsqrt(jnp.mean(joined_wide * joined_wide, axis=1, keepdims=True) + epsilon)
    gate_wide = activated[:, :D].astype(jnp.float32)
    gated = (joined_wide * middle_scale * gate_wide).astype(jnp.bfloat16)
    layer_out = wide_tokens + jnp.dot(gated, w_out, preferred_element_type=jnp.float32)
    return (layer_out, (wide_tokens, input_scale, pre_act, activated, joined, middle_scale, gated))


def loss_head(layer_out, clicked_product_vectors, sampled_decoys):
    out_scale = lax.rsqrt(jnp.sum(layer_out * layer_out, axis=1, keepdims=True) + epsilon)
    normalized_example_vectors = lax.optimization_barrier(
        (layer_out * out_scale).astype(jnp.bfloat16)
    )
    normalized_complete_embedding = normalized_example_vectors.astype(jnp.float32)
    correct_logit_entry = (
        jnp.sum(normalized_complete_embedding * clicked_product_vectors.astype(jnp.float32), axis=1)
        / logit_divisor
    )
    decoy_logit_entries = (
        reduce_last_dimension(normalized_example_vectors, sampled_decoys) / logit_divisor
    )
    target_exp = jnp.exp(correct_logit_entry)
    negative_exp = jnp.exp(decoy_logit_entries)
    totals = target_exp + jnp.sum(negative_exp, axis=1)
    target_prob = target_exp / totals
    negative_probs = (loss_scale * negative_exp / totals[:, None]).astype(jnp.bfloat16)
    target_coef = (loss_scale * (target_prob - 1.0))[:, None]
    grad_unit = target_coef * clicked_product_vectors.astype(jnp.float32) + jnp.dot(
        negative_probs, sampled_decoys, preferred_element_type=jnp.float32
    )
    grad_out = out_scale * grad_unit - layer_out * out_scale**3 * jnp.sum(
        layer_out * grad_unit, axis=1, keepdims=True
    )
    grad_target = target_coef * normalized_complete_embedding
    return (grad_out, grad_target, negative_probs, normalized_example_vectors)


def backward_layer(grad_out, saved_state, project_back, w_out, visible):
    wide_tokens, input_scale, pre_act, activated, joined, middle_scale, gated = saved_state
    grad_out_b = grad_out.astype(jnp.bfloat16)
    weight_part = contract_first(gated, grad_out_b)
    grad_gated = reduce_last_dimension(grad_out_b, w_out)
    joined_wide = joined.astype(jnp.float32)
    gate_wide = activated[:, :D].astype(jnp.float32)
    grad_gate = grad_gated * joined_wide * middle_scale
    grad_norm = grad_gated * gate_wide
    grad_joined = middle_scale * grad_norm - joined_wide * middle_scale**3 * jnp.mean(
        joined_wide * grad_norm, axis=1, keepdims=True
    )
    grad_joined_b = grad_joined.astype(jnp.bfloat16)
    grad_values = []
    grad_queries = []
    grad_keys = []
    for head_index in range(HEADS):
        queries = head_columns(activated, 2, head_index)
        key_rows = head_columns(activated, 3, head_index)
        value_rows = head_columns(activated, 1, head_index)
        scores = head_scores(queries, key_rows)
        weights = head_weights(scores, visible)
        grad_head = grad_joined_b[:, head_index * DH : (head_index + 1) * DH]
        grad_weights = reduce_last_dimension(grad_head, value_rows)
        grad_values.append(contract_first(weights, grad_head))
        grad_scores = (
            grad_weights * visible * (1.0 / MAXLEN) * silu_slope(scores) * DH ** (-0.5)
        ).astype(jnp.bfloat16)
        grad_queries.append(jnp.dot(grad_scores, key_rows, preferred_element_type=jnp.float32))
        grad_keys.append(contract_first(grad_scores, queries))
    grad_act = jnp.concatenate([grad_gate] + grad_values + grad_queries + grad_keys, axis=1)
    grad_pre = (grad_act * silu_slope(pre_act)).astype(jnp.bfloat16)
    grad_normed = project_back(grad_pre)
    grad_input = input_scale * grad_normed - wide_tokens * input_scale**3 * jnp.mean(
        wide_tokens * grad_normed, axis=1, keepdims=True
    )
    return ((grad_out + grad_input).astype(jnp.bfloat16), weight_part)


def finish_rows(grad_items, rows_wide):
    item_scale = lax.rsqrt(jnp.sum(rows_wide * rows_wide, axis=1, keepdims=True) + epsilon)
    return (
        item_scale * grad_items
        - rows_wide * item_scale**3 * jnp.sum(rows_wide * grad_items, axis=1, keepdims=True)
    ) / loss_scale


def plain_shards(tokens, w_proj, w_out, item_rows, lengths, target_owner, target_row, negative_rows):
    tok_rows = tokens.shape[0]
    model_width = tokens.shape[1]
    shard_count = lax.axis_size("shard")
    capacity = 2 * tok_rows // shard_count
    visible = history_mask(lengths[0], tok_rows)

    def project(normed):
        return jnp.dot(
            normed,
            lax.all_gather(w_proj, "shard", axis=1, tiled=True),
            preferred_element_type=jnp.float32,
        )

    def project_back(grad_pre):
        return reduce_last_dimension(grad_pre, lax.all_gather(w_proj, "shard", axis=1, tiled=True))

    rows_wide = item_rows.astype(jnp.float32)
    item_scale = lax.rsqrt(jnp.sum(rows_wide * rows_wide, axis=1, keepdims=True) + epsilon)
    unit_items = (rows_wide * item_scale).astype(jnp.bfloat16)
    owners = target_owner[:, 0]
    owner_hits = (owners[:, None] == jnp.arange(shard_count, dtype=jnp.int32)[None, :]).astype(
        jnp.int32
    )
    earlier = jnp.cumsum(owner_hits, axis=0) - owner_hits
    slot_index = jnp.sum(earlier * owner_hits, axis=1)
    position = owners * capacity + slot_index
    requests = jnp.zeros((shard_count * capacity,), jnp.int32).at[position].set(target_row)
    asked_rows = lax.all_to_all(
        requests.reshape(shard_count, capacity), "shard", split_axis=0, concat_axis=0, tiled=True
    )
    asked_flat = asked_rows.reshape(-1)
    served = jnp.take(unit_items, asked_flat, axis=0).reshape(shard_count, capacity, model_width)
    fetched = lax.all_to_all(served, "shard", split_axis=0, concat_axis=0, tiled=True)
    clicked_product_vectors = jnp.take(
        fetched.reshape(shard_count * capacity, model_width), position, axis=0
    )
    sampled_decoys = lax.all_gather(
        jnp.take(unit_items, negative_rows, axis=0), "shard", axis=0, tiled=True
    )
    layer_out, saved_state = forward_layer(tokens, project, w_out, visible)
    grad_out, grad_target, negative_probs, normalized_example_vectors = loss_head(
        layer_out, clicked_product_vectors, sampled_decoys
    )
    grad_tokens, weight_part = backward_layer(grad_out, saved_state, project_back, w_out, visible)
    outgoing = (
        jnp.zeros((shard_count * capacity, model_width), jnp.float32).at[position].set(grad_target)
    )
    returned = lax.all_to_all(
        outgoing.reshape(shard_count, capacity, model_width).astype(jnp.bfloat16),
        "shard",
        split_axis=0,
        concat_axis=0,
        tiled=True,
    ).astype(jnp.float32)
    grad_items = (
        jnp.zeros((item_rows.shape[0], model_width), jnp.float32)
        .at[asked_flat]
        .add(returned.reshape(-1, model_width))
    )
    own_negatives = lax.psum_scatter(
        contract_first(negative_probs, normalized_example_vectors).astype(jnp.bfloat16),
        "shard",
        scatter_dimension=0,
        tiled=True,
    ).astype(jnp.float32)
    grad_items = grad_items.at[negative_rows].add(own_negatives)
    share_rows = item_rows.shape[0] // lax.axis_size("dp")
    summed_share = lax.psum_scatter(
        grad_items.astype(jnp.bfloat16), "dp", scatter_dimension=0, tiled=True
    ).astype(jnp.float32)
    share_start = lax.axis_index("dp") * share_rows
    share_wide = lax.dynamic_slice_in_dim(rows_wide, share_start, share_rows, 0)
    item_grads = lax.all_gather(
        finish_rows(summed_share, share_wide).astype(jnp.bfloat16), "dp", axis=0, tiled=True
    ).astype(jnp.float32)
    weight_grads = lax.psum(weight_part, ("dp", "shard")) / loss_scale
    return (grad_tokens, weight_grads, item_grads)


MESH = pl.DeviceIdType.MESH


def start_copy(src, dst, sems, index, target):
    send_sem, recv_sem = sems
    copy = pltpu.make_async_remote_copy(
        src_ref=src,
        dst_ref=dst,
        send_sem=send_sem.at[index],
        recv_sem=recv_sem.at[index],
        device_id=target,
        device_id_type=MESH,
    )
    copy.start()
    return copy


def places(n_dp, n_shard):
    dp = lax.axis_index("dp")
    shard = lax.axis_index("shard")
    core = lax.rem(dp, 2)
    height = dp // 2
    sibling = (dp + 1 - 2 * core, shard)
    shard_peers = [(dp, lax.rem(shard + k, n_shard)) for k in range(1, n_shard)]
    shard_from = [lax.rem(shard + n_shard - k, n_shard) for k in range(1, n_shard)]
    n_z = n_dp // 2
    z_to = [lax.rem(height + k, n_z) for k in range(1, n_z)]
    z_peers = [(z * 2 + core, shard) for z in z_to]
    z_from = [lax.rem(height + n_z - k, n_z) for k in range(1, n_z)]
    return dp, shard, core, height, sibling, shard_peers, shard_from, z_to, z_peers, z_from


def one_hot_columns(position, slots):
    columns = lax.broadcasted_iota(jnp.int32, (position.shape[0], slots), 1)
    return columns == position


def row_picks(asked_row, rows_count):
    rows = lax.broadcasted_iota(jnp.int32, (rows_count, asked_row.shape[1]), 0)
    return jnp.where(rows == asked_row, 1.0, 0.0).astype(jnp.bfloat16)


def as_column(row):
    count = row.shape[1]
    across = lax.broadcasted_iota(jnp.int32, (count, count), 0)
    along = lax.broadcasted_iota(jnp.int32, (count, count), 1)
    return jnp.sum(jnp.where(across == along, row, 0), axis=1, keepdims=True)


def as_row(column):
    count = column.shape[0]
    across = lax.broadcasted_iota(jnp.int32, (count, count), 0)
    along = lax.broadcasted_iota(jnp.int32, (count, count), 1)
    return jnp.sum(jnp.where(across == along, column, 0), axis=0, keepdims=True)


def ones_of(picks):
    return jnp.where(picks, 1.0, 0.0).astype(jnp.bfloat16)


def visible_pairs(lengths, rows_count):
    across = lax.broadcasted_iota(jnp.int32, (rows_count, rows_count), 0)
    along = lax.broadcasted_iota(jnp.int32, (rows_count, rows_count), 1)
    history_a = jnp.zeros((rows_count, rows_count), jnp.int32)
    history_b = jnp.zeros((rows_count, rows_count), jnp.int32)
    end = jnp.zeros((1, 1), jnp.int32)
    for j in range(lengths.shape[1] - 1):
        end = end + lengths[:, j : j + 1]
        history_a += jnp.where(across >= end, 1, 0)
        history_b += jnp.where(along >= end, 1, 0)
    return jnp.where((history_a == history_b) & (along <= across), 1.0 / MAXLEN, 0.0)


def layer_kernel(
    n_dp,
    n_shard,
    capacity,
    tokens_ref,
    w_ref,
    w_out_ref,
    items_ref,
    lengths_ref,
    owner_ref,
    target_ref,
    negative_ref,
    grad_tokens_ref,
    gathered,
    w_gathered,
    w_full,
    negatives,
    requests,
    asked,
    served,
    fetched,
    unit,
    pre,
    act,
    scores_ref,
    visible_ref,
    normed_ref,
    joined_ref,
    grad_joined_ref,
    grad_out_ref,
    grad_pre,
    out_rows,
    in_rows,
    pair_sums,
    pair_in,
    out_sums,
    in_sums,
    out_pair,
    in_pair,
    out_z,
    in_z,
    slots_back,
    picks_ref,
    w_pair,
    w_pair_in,
    w_out_z,
    w_in_z,
    w_out_shard,
    w_in_shard,
    send_sem,
    recv_sem,
):
    dp, shard, core, height, sibling, peers, sources, z_to, z_peers, z_from = places(n_dp, n_shard)
    n_z = n_dp // 2
    others = sources
    near = range(n_shard - 1)
    barrier = pltpu.get_barrier_semaphore()
    greeted = peers + [sibling] + z_peers
    for peer in greeted:
        pl.semaphore_signal(barrier, inc=1, device_id=peer, device_id_type=MESH)
    used = [0]
    started = []

    def send(src, dst, target):
        copy = start_copy(src, dst, (send_sem, recv_sem), used[0], target)
        used[0] += 1
        started.append(copy)
        return copy

    rows_count, width = items_ref.shape
    tok_rows = tokens_ref.shape[0]
    neg_rows = negative_ref.shape[1]
    neg_half = neg_rows // 2
    half = w_ref.shape[0] // 2
    share = rows_count // n_dp
    w_rows = width // n_shard
    w_share = w_rows // n_dp
    n_parts, part_cols = out_rows.shape[0], out_rows.shape[-1]

    owner_row = owner_ref[...]
    owner_col = as_column(owner_row)
    token_a = lax.broadcasted_iota(jnp.int32, (tok_rows, tok_rows), 0)
    token_b = lax.broadcasted_iota(jnp.int32, (tok_rows, tok_rows), 1)
    same = (owner_row == owner_col) & (token_b < token_a)
    slot = jnp.sum(jnp.where(same, 1.0, 0.0), axis=1, keepdims=True).astype(jnp.int32)
    position = owner_col * capacity + slot
    slots = one_hot_columns(position, n_shard * capacity)
    target = as_column(target_ref[...].reshape(1, -1))
    request = jnp.sum(jnp.where(slots, target, 0), axis=0, keepdims=True)
    for j in range(n_shard):
        part = request[:, j * capacity : (j + 1) * capacity]
        requests[j] = jnp.broadcast_to(part, (8, capacity))
    slots_one = ones_of(slots)
    slots_back[...] = row_picks(as_row(position), n_shard * capacity)

    pl.semaphore_wait(barrier, len(greeted))
    ask_copies = [send(requests.at[peer[1]], asked.at[shard], peer) for peer in peers]
    mine = pl.ds(pl.multiple_of(core * half, half), half)
    w_copies = [send(w_ref.at[mine], w_full.at[shard, mine], peer) for peer in peers]
    asked[shard] = requests[shard]

    rows_wide = items_ref[...].astype(jnp.float32)
    item_scale = lax.rsqrt(jnp.sum(rows_wide * rows_wide, axis=1, keepdims=True) + epsilon)
    unit[...] = (rows_wide * item_scale).astype(jnp.bfloat16)
    negative_row = negative_ref[...]
    negative_col = as_column(negative_row)
    own_negatives = jnp.dot(
        ones_of(one_hot_columns(negative_col, rows_count)),
        unit[...],
        preferred_element_type=jnp.float32,
    ).astype(jnp.bfloat16)
    negatives[shard, 0] = own_negatives[:neg_half]
    negatives[shard, 1] = own_negatives[neg_half:]
    neg_piece = negatives.at[shard, core]
    neg_copies = [send(neg_piece, neg_piece, peer) for peer in peers]
    w_full[shard] = w_ref[...]
    wide_tokens = tokens_ref[...].astype(jnp.float32)
    input_scale = lax.rsqrt(jnp.mean(wide_tokens * wide_tokens, axis=1, keepdims=True) + epsilon)
    normed_ref[...] = (wide_tokens * input_scale).astype(jnp.bfloat16)
    visible_ref[...] = visible_pairs(lengths_ref[...], tok_rows)

    def section(j):
        values = jnp.dot(normed_ref[...], w_full[j], preferred_element_type=jnp.float32)
        pre[j] = values
        act[j] = (values * lax.logistic(values)).astype(jnp.bfloat16)

    def rows_for(source):
        asked_row = asked[source][0:1]
        picks_ref[source] = row_picks(asked_row, rows_count)
        picks = ones_of(one_hot_columns(as_column(asked_row), rows_count))
        return jnp.dot(picks, unit[...], preferred_element_type=jnp.float32).astype(jnp.bfloat16)

    section(shard)
    for k, source in enumerate(others):
        ask_copies[k].wait_recv()
        served[source] = rows_for(source)
    fetched[shard] = rows_for(shard)
    w_pairs = []
    for k, source in enumerate(others):
        w_copies[k].wait_recv()
        piece = w_full.at[source, mine]
        w_pairs.append(send(piece, piece, sibling))
    row_copies = [
        send(served.at[source], fetched.at[shard], (dp, source)) for source in others
    ]
    neg_pairs = []
    for k, source in enumerate(others):
        neg_copies[k].wait_recv()
        piece = negatives.at[source, core]
        neg_pairs.append(send(piece, piece, sibling))
    for k, source in enumerate(others):
        w_pairs[k].wait_recv()
        section(source)

    def head_part(j, head):
        return act[j, :, head * DH : (head + 1) * DH]

    for head in range(HEADS):
        scores = head_scores(head_part(2, head), head_part(3, head))
        scores_ref[head] = scores
        weights = (scores * lax.logistic(scores) * visible_ref[...]).astype(jnp.bfloat16)
        joined_ref[:, head * DH : (head + 1) * DH] = jnp.dot(
            weights, head_part(1, head), preferred_element_type=jnp.float32
        ).astype(jnp.bfloat16)
    joined_wide = joined_ref[...].astype(jnp.float32)
    middle_scale = lax.rsqrt(jnp.mean(joined_wide * joined_wide, axis=1, keepdims=True) + epsilon)
    gate_wide = act[0].astype(jnp.float32)
    gated = (joined_wide * middle_scale * gate_wide).astype(jnp.bfloat16)
    layer_out = tokens_ref[...].astype(jnp.float32) + jnp.dot(
        gated, w_out_ref[...], preferred_element_type=jnp.float32
    )
    out_scale = lax.rsqrt(jnp.sum(layer_out * layer_out, axis=1, keepdims=True) + epsilon)
    unit_b = (layer_out * out_scale).astype(jnp.bfloat16)
    for copy in neg_pairs:
        copy.wait_recv()
    negative_exps = []
    for j in range(n_shard):
        for c in range(2):
            logits = reduce_last_dimension(unit_b, negatives[j, c]) / logit_divisor
            negative_exps.append(jnp.exp(logits))
    negative_exp = jnp.concatenate(negative_exps, axis=1)
    for copy in row_copies:
        copy.wait_recv()
    clicked = jnp.zeros((tok_rows, width), jnp.float32)
    for j in range(n_shard):
        clicked += jnp.dot(
            slots_one[:, j * capacity : (j + 1) * capacity],
            fetched[j],
            preferred_element_type=jnp.float32,
        )
    unit_wide = unit_b.astype(jnp.float32)
    target_logit = jnp.sum(unit_wide * clicked, axis=1, keepdims=True) / logit_divisor
    target_exp = jnp.exp(target_logit)
    totals = target_exp + jnp.sum(negative_exp, axis=1, keepdims=True)
    negative_probs = (loss_scale * negative_exp / totals).astype(jnp.bfloat16)
    target_coef = loss_scale * (target_exp / totals - 1.0)
    grad_target = (target_coef * unit_wide).astype(jnp.bfloat16)

    row_sends = []
    for h in range(n_parts):
        for j in range(n_shard):
            out_rows[h, j] = jnp.dot(
                slots_back[j * capacity : (j + 1) * capacity],
                grad_target[:, h * part_cols : (h + 1) * part_cols],
                preferred_element_type=jnp.float32,
            ).astype(jnp.bfloat16)
        if h == 0:
            row_sends.append(
                [send(out_rows.at[h, peer[1]], in_rows.at[h, shard], peer) for peer in peers]
            )
    grad_unit = target_coef * clicked
    for j in range(n_shard):
        for c in range(2):
            first = (2 * j + c) * neg_half
            grad_unit += jnp.dot(
                negative_probs[:, first : first + neg_half],
                negatives[j, c],
                preferred_element_type=jnp.float32,
            )
    grad_out = out_scale * grad_unit - layer_out * out_scale**3 * jnp.sum(
        layer_out * grad_unit, axis=1, keepdims=True
    )
    grad_out_ref[...] = grad_out
    grad_out_b = grad_out.astype(jnp.bfloat16)
    neg_part = contract_first(negative_probs, unit_b).astype(jnp.bfloat16)
    for h in range(n_parts):
        cols = slice(h * part_cols, (h + 1) * part_cols)
        for j in range(n_shard):
            for c in range(2):
                first = (2 * j + c) * neg_half
                pair_sums[c, h, j] = neg_part[first : first + neg_half, cols]
    sum_pair = send(pair_sums.at[1 - core], pair_in, sibling)
    w_part = contract_first(gated, grad_out_b).astype(jnp.bfloat16)
    for c in range(2):
        for j in range(n_shard):
            for z in range(n_z):
                first = ((c * n_shard + j) * n_z + z) * w_share
                w_pair[c, z, j] = w_part[first : first + w_share]
    w_pair_copy = send(w_pair.at[1 - core], w_pair_in, sibling)
    sum_pair.wait_recv()
    out_sums[...] = (
        pair_sums[core].astype(jnp.float32) + pair_in[...].astype(jnp.float32)
    ).astype(jnp.bfloat16)
    sum_sends = []
    for h in range(n_parts):
        if h > 0:
            row_sends.append(
                [send(out_rows.at[h, peer[1]], in_rows.at[h, shard], peer) for peer in peers]
            )
        sum_sends.append(
            [send(out_sums.at[h, peer[1]], in_sums.at[h, shard], peer) for peer in peers]
        )
    w_pair_copy.wait_recv()
    w_out_z[...] = (
        w_pair[core].astype(jnp.float32) + w_pair_in[...].astype(jnp.float32)
    ).astype(jnp.bfloat16)
    w_z_sends = [
        send(w_out_z.at[z_to[k]], w_in_z.at[height], peer) for k, peer in enumerate(z_peers)
    ]

    grad_gated = reduce_last_dimension(grad_out_b, w_out_ref[...])
    grad_pre[0] = (grad_gated * joined_wide * middle_scale * silu_slope(pre[0])).astype(
        jnp.bfloat16
    )
    grad_norm = grad_gated * gate_wide
    grad_joined_ref[...] = (
        middle_scale * grad_norm
        - joined_wide
        * middle_scale**3
        * jnp.mean(joined_wide * grad_norm, axis=1, keepdims=True)
    ).astype(jnp.bfloat16)

    def head_back(head):
        cols = slice(head * DH, (head + 1) * DH)
        scores = scores_ref[head]
        sigmoid = lax.logistic(scores)
        visible = visible_ref[...]
        weights = (scores * sigmoid * visible).astype(jnp.bfloat16)
        grad_head = grad_joined_ref[:, cols]
        grad_weights = reduce_last_dimension(grad_head, head_part(1, head))
        slope = sigmoid * (1.0 + scores * (1.0 - sigmoid))
        grad_scores = (grad_weights * visible * slope * DH ** (-0.5)).astype(jnp.bfloat16)
        grads = (
            contract_first(weights, grad_head),
            jnp.dot(grad_scores, head_part(3, head), preferred_element_type=jnp.float32),
            contract_first(grad_scores, head_part(2, head)),
        )
        for j, grad in enumerate(grads):
            grad_pre[j + 1, :, cols] = (grad * silu_slope(pre[j + 1, :, cols])).astype(
                jnp.bfloat16
            )

    def collect(h):
        grad_items = jnp.zeros((rows_count, part_cols), jnp.float32)
        sums = jnp.zeros((neg_half, part_cols), jnp.float32)
        for k, source in enumerate([shard] + others):
            if k > 0:
                row_sends[h][k - 1].wait_recv()
                sum_sends[h][k - 1].wait_recv()
            rows = out_rows[h, shard] if k == 0 else in_rows[h, source]
            part = out_sums[h, shard] if k == 0 else in_sums[h, source]
            grad_items += jnp.dot(picks_ref[source], rows, preferred_element_type=jnp.float32)
            sums += part.astype(jnp.float32)
        own_rows = jnp.where(core == 0, negative_row[:, :neg_half], negative_row[:, neg_half:])
        grad_items += jnp.dot(
            row_picks(own_rows, rows_count),
            sums.astype(jnp.bfloat16),
            preferred_element_type=jnp.float32,
        )
        for z in range(n_z):
            for c in range(2):
                d = z * 2 + c
                out_pair[h, c, z] = grad_items[d * share : (d + 1) * share].astype(jnp.bfloat16)
        return send(out_pair.at[h, 1 - core], in_pair.at[h], sibling)

    def pass_on(h, pair):
        pair.wait_recv()
        for z in range(n_z):
            out_z[h, z] = (
                out_pair[h, core, z].astype(jnp.float32) + in_pair[h, z].astype(jnp.float32)
            ).astype(jnp.bfloat16)
        return [
            send(out_z.at[h, z_to[k]], in_z.at[h, height], peer) for k, peer in enumerate(z_peers)
        ]

    head_back(0)
    pair = collect(0)
    head_back(1)
    z_sends = [pass_on(0, pair)]
    w_total = w_out_z[height].astype(jnp.float32)
    for k, z in enumerate(z_from):
        w_z_sends[k].wait_recv()
        w_total += w_in_z[z].astype(jnp.float32)
    w_out_shard[...] = w_total.astype(jnp.bfloat16)
    w_sends = [send(w_out_shard.at[peer[1]], w_in_shard.at[shard], peer) for peer in peers]
    pair = collect(1)
    head_back(2)
    z_sends.append(pass_on(1, pair))
    w_total = w_out_shard[shard].astype(jnp.float32)
    for k, source in enumerate(others):
        w_sends[k].wait_recv()
        w_total += w_in_shard[source].astype(jnp.float32)
    w_gathered[core, shard, height] = (w_total / loss_scale).astype(jnp.bfloat16)
    w_mine = w_gathered.at[core, shard, height]
    w_z = [send(w_mine, w_mine, peer) for peer in z_peers]
    for head in range(3, HEADS):
        head_back(head)
    for copy in w_z:
        copy.wait_recv()
    w_block = w_gathered.at[core, shard]
    w_around = [send(w_block, w_block, peer) for peer in peers]
    last = [send(w_block, w_block, sibling)]
    grad_normed = jnp.zeros((tok_rows, width), jnp.float32)
    for j in range(n_shard):
        grad_normed += reduce_last_dimension(grad_pre[j], w_full[j])
    wide_tokens = tokens_ref[...].astype(jnp.float32)
    grad_input = input_scale * grad_normed - wide_tokens * input_scale**3 * jnp.mean(
        wide_tokens * grad_normed, axis=1, keepdims=True
    )
    grad_tokens_ref[...] = (grad_out_ref[...] + grad_input).astype(jnp.bfloat16)

    totals_parts = []
    for h in range(n_parts):
        total = out_z[h, height].astype(jnp.float32)
        for k, z in enumerate(z_from):
            z_sends[h][k].wait_recv()
            total += in_z[h, z].astype(jnp.float32)
        totals_parts.append(total)
    total = jnp.concatenate(totals_parts, axis=1)
    own = pl.ds(pl.multiple_of(dp * share, share), share)
    finished = finish_rows(total, items_ref[own].astype(jnp.float32))
    gathered[height, core] = finished.astype(jnp.bfloat16)
    items_mine = gathered.at[height, core]
    items_z = [send(items_mine, items_mine, peer) for peer in z_peers]
    last.append(send(items_mine, items_mine, sibling))
    for k, source in enumerate(others):
        w_around[k].wait_recv()
        piece = w_gathered.at[core, source]
        last.append(send(piece, piece, sibling))
    for k, z in enumerate(z_from):
        items_z[k].wait_recv()
        piece = gathered.at[z, core]
        last.append(send(piece, piece, sibling))
    for copy in last:
        copy.wait_recv()
    for copy in started:
        copy.wait_send()


def vmem_specs(count):
    return [pl.BlockSpec(memory_space=pltpu.VMEM)] * count


def shards(tokens, w_proj, w_out, item_rows, lengths, target_owner, target_row, negative_rows):
    tok_rows, width = tokens.shape
    n_shard = lax.axis_size("shard")
    n_dp = lax.axis_size("dp")
    n_z = n_dp // 2
    capacity = 2 * tok_rows // n_shard
    rows_count = item_rows.shape[0]
    neg_half = negative_rows.shape[0] // 2
    share = rows_count // n_dp
    w_half = width // n_shard // 2
    w_share = w_half // n_z
    parts = 2
    cols = width // parts
    b16 = jnp.bfloat16
    f32 = jnp.float32
    shape = jax.ShapeDtypeStruct
    copies = 7 * (n_shard - 1) + 4 * parts * (n_shard + n_z) + 2 * (n_shard + n_z) + 8
    grad_tokens, gathered, w_gathered = pl.pallas_call(
        functools.partial(layer_kernel, n_dp, n_shard, capacity),
        out_shape=[
            shape((tok_rows, width), b16),
            shape((n_z, 2, share, width), b16),
            shape((2, n_shard, n_z, w_share, width), b16),
        ],
        in_specs=vmem_specs(8),
        out_specs=vmem_specs(3),
        scratch_shapes=[
            pltpu.VMEM((n_shard, width, width), b16),
            pltpu.VMEM((n_shard, 2, neg_half, width), b16),
            pltpu.VMEM((n_shard, 8, capacity), jnp.int32),
            pltpu.VMEM((n_shard, 8, capacity), jnp.int32),
            pltpu.VMEM((n_shard, capacity, width), b16),
            pltpu.VMEM((n_shard, capacity, width), b16),
            pltpu.VMEM((rows_count, width), b16),
            pltpu.VMEM((4, tok_rows, width), f32),
            pltpu.VMEM((4, tok_rows, width), b16),
            pltpu.VMEM((HEADS, tok_rows, tok_rows), f32),
            pltpu.VMEM((tok_rows, tok_rows), f32),
            pltpu.VMEM((tok_rows, width), b16),
            pltpu.VMEM((tok_rows, width), b16),
            pltpu.VMEM((tok_rows, width), b16),
            pltpu.VMEM((tok_rows, width), f32),
            pltpu.VMEM((4, tok_rows, width), b16),
            pltpu.VMEM((parts, n_shard, capacity, cols), b16),
            pltpu.VMEM((parts, n_shard, capacity, cols), b16),
            pltpu.VMEM((2, parts, n_shard, neg_half, cols), b16),
            pltpu.VMEM((parts, n_shard, neg_half, cols), b16),
            pltpu.VMEM((parts, n_shard, neg_half, cols), b16),
            pltpu.VMEM((parts, n_shard, neg_half, cols), b16),
            pltpu.VMEM((parts, 2, n_z, share, cols), b16),
            pltpu.VMEM((parts, n_z, share, cols), b16),
            pltpu.VMEM((parts, n_z, share, cols), b16),
            pltpu.VMEM((parts, n_z, share, cols), b16),
            pltpu.VMEM((n_shard * capacity, tok_rows), b16),
            pltpu.VMEM((n_shard, rows_count, capacity), b16),
            pltpu.VMEM((2, n_z, n_shard, w_share, width), b16),
            pltpu.VMEM((n_z, n_shard, w_share, width), b16),
            pltpu.VMEM((n_z, n_shard, w_share, width), b16),
            pltpu.VMEM((n_z, n_shard, w_share, width), b16),
            pltpu.VMEM((n_shard, w_share, width), b16),
            pltpu.VMEM((n_shard, w_share, width), b16),
            pltpu.SemaphoreType.DMA((copies,)),
            pltpu.SemaphoreType.DMA((copies,)),
        ],
        compiler_params=pltpu.CompilerParams(
            collective_id=0, has_side_effects=True, vmem_limit_bytes=56 * 2**20
        ),
        name="layer",
    )(
        tokens,
        w_proj,
        w_out,
        item_rows,
        lengths,
        target_owner.reshape(1, -1),
        target_row,
        negative_rows.reshape(1, -1),
    )
    item_grads = gathered.reshape(rows_count, width).astype(f32)
    return (grad_tokens, w_gathered.reshape(width, width).astype(f32), item_grads)


def fits_kernels(mesh):
    n_dp, n_shard = mesh.shape["dp"], mesh.shape["shard"]
    return n_dp % 2 == 0 and n_dp > 2 and n_shard == 4 and D % (16 * n_dp * n_shard) == 0


def solution(mesh):
    in_specs = (
        P(("dp", "shard"), None),
        P(None, "shard"),
        P(),
        P("shard", None),
        P(("dp", "shard"), None),
        P(("dp", "shard"), None),
        P(("dp", "shard")),
        P("shard"),
    )
    out_specs = (P(("dp", "shard"), None), P(), P("shard", None))
    return jax.shard_map(
        shards if fits_kernels(mesh) else plain_shards,
        mesh=mesh, in_specs=in_specs, out_specs=out_specs, check_vma=False)
```

```python
import functools

import jax
import jax.numpy as jnp
from jax import lax
from jax.experimental import pallas as pl
from jax.experimental.pallas import tpu as pltpu
from jax.sharding import PartitionSpec as P

D = 512
HEADS = 4
DH = 128
MAXLEN = 192


epsilon = 1e-06
logit_divisor = 0.015625
loss_scale = 512.0


def reduce_last_dimension(operand, other_side):
    return lax.dot_general(
        operand, other_side, (((1,), (1,)), ((), ())), preferred_element_type=jnp.float32
    )


def contract_first(operand, other_side):
    return lax.dot_general(
        operand, other_side, (((0,), (0,)), ((), ())), preferred_element_type=jnp.float32
    )


def silu_slope(values):
    sigmoid = jax.nn.sigmoid(values)
    return sigmoid * (1.0 + values * (1.0 - sigmoid))


def history_mask(lengths_row, rows_count):
    history_ends = jnp.cumsum(lengths_row)
    positions = jnp.arange(rows_count, dtype=jnp.int32)
    history_ids = jnp.sum((positions[:, None] >= history_ends[None, :-1]).astype(jnp.int32), axis=1)
    visible = (history_ids[:, None] == history_ids[None, :]) & (
        positions[None, :] <= positions[:, None]
    )
    return jnp.where(visible, 1.0, 0.0).astype(jnp.float32)


def head_columns(activated, section, head_index):
    first_col = section * D + head_index * DH
    return activated[:, first_col : first_col + DH]


def head_scores(queries, key_rows):
    return reduce_last_dimension(queries, key_rows) * DH ** (-0.5)


def head_weights(scores, visible):
    return (jax.nn.silu(scores) * visible * (1.0 / MAXLEN)).astype(jnp.bfloat16)


def forward_layer(tokens, project, w_out, visible):
    wide_tokens = tokens.astype(jnp.float32)
    input_scale = lax.rsqrt(jnp.mean(wide_tokens * wide_tokens, axis=1, keepdims=True) + epsilon)
    normed = (wide_tokens * input_scale).astype(jnp.bfloat16)
    pre_act = project(normed)
    activated = lax.optimization_barrier(jax.nn.silu(pre_act).astype(jnp.bfloat16))
    heads_out = []
    for head_index in range(HEADS):
        queries = head_columns(activated, 2, head_index)
        key_rows = head_columns(activated, 3, head_index)
        value_rows = head_columns(activated, 1, head_index)
        weights = head_weights(head_scores(queries, key_rows), visible)
        heads_out.append(jnp.dot(weights, value_rows, preferred_element_type=jnp.float32))
    joined = lax.optimization_barrier(jnp.concatenate(heads_out, axis=1).astype(jnp.bfloat16))
    joined_wide = joined.astype(jnp.float32)
    middle_scale = lax.rsqrt(jnp.mean(joined_wide * joined_wide, axis=1, keepdims=True) + epsilon)
    gate_wide = activated[:, :D].astype(jnp.float32)
    gated = (joined_wide * middle_scale * gate_wide).astype(jnp.bfloat16)
    layer_out = wide_tokens + jnp.dot(gated, w_out, preferred_element_type=jnp.float32)
    return (layer_out, (wide_tokens, input_scale, pre_act, activated, joined, middle_scale, gated))


def loss_head(layer_out, clicked_product_vectors, sampled_decoys):
    out_scale = lax.rsqrt(jnp.sum(layer_out * layer_out, axis=1, keepdims=True) + epsilon)
    normalized_example_vectors = lax.optimization_barrier(
        (layer_out * out_scale).astype(jnp.bfloat16)
    )
    normalized_complete_embedding = normalized_example_vectors.astype(jnp.float32)
    correct_logit_entry = (
        jnp.sum(normalized_complete_embedding * clicked_product_vectors.astype(jnp.float32), axis=1)
        / logit_divisor
    )
    decoy_logit_entries = (
        reduce_last_dimension(normalized_example_vectors, sampled_decoys) / logit_divisor
    )
    target_exp = jnp.exp(correct_logit_entry)
    negative_exp = jnp.exp(decoy_logit_entries)
    totals = target_exp + jnp.sum(negative_exp, axis=1)
    target_prob = target_exp / totals
    negative_probs = (loss_scale * negative_exp / totals[:, None]).astype(jnp.bfloat16)
    target_coef = (loss_scale * (target_prob - 1.0))[:, None]
    grad_unit = target_coef * clicked_product_vectors.astype(jnp.float32) + jnp.dot(
        negative_probs, sampled_decoys, preferred_element_type=jnp.float32
    )
    grad_out = out_scale * grad_unit - layer_out * out_scale**3 * jnp.sum(
        layer_out * grad_unit, axis=1, keepdims=True
    )
    grad_target = target_coef * normalized_complete_embedding
    return (grad_out, grad_target, negative_probs, normalized_example_vectors)


def backward_layer(grad_out, saved_state, project_back, w_out, visible):
    wide_tokens, input_scale, pre_act, activated, joined, middle_scale, gated = saved_state
    grad_out_b = grad_out.astype(jnp.bfloat16)
    weight_part = contract_first(gated, grad_out_b)
    grad_gated = reduce_last_dimension(grad_out_b, w_out)
    joined_wide = joined.astype(jnp.float32)
    gate_wide = activated[:, :D].astype(jnp.float32)
    grad_gate = grad_gated * joined_wide * middle_scale
    grad_norm = grad_gated * gate_wide
    grad_joined = middle_scale * grad_norm - joined_wide * middle_scale**3 * jnp.mean(
        joined_wide * grad_norm, axis=1, keepdims=True
    )
    grad_joined_b = grad_joined.astype(jnp.bfloat16)
    grad_values = []
    grad_queries = []
    grad_keys = []
    for head_index in range(HEADS):
        queries = head_columns(activated, 2, head_index)
        key_rows = head_columns(activated, 3, head_index)
        value_rows = head_columns(activated, 1, head_index)
        scores = head_scores(queries, key_rows)
        weights = head_weights(scores, visible)
        grad_head = grad_joined_b[:, head_index * DH : (head_index + 1) * DH]
        grad_weights = reduce_last_dimension(grad_head, value_rows)
        grad_values.append(contract_first(weights, grad_head))
        grad_scores = (
            grad_weights * visible * (1.0 / MAXLEN) * silu_slope(scores) * DH ** (-0.5)
        ).astype(jnp.bfloat16)
        grad_queries.append(jnp.dot(grad_scores, key_rows, preferred_element_type=jnp.float32))
        grad_keys.append(contract_first(grad_scores, queries))
    grad_act = jnp.concatenate([grad_gate] + grad_values + grad_queries + grad_keys, axis=1)
    grad_pre = (grad_act * silu_slope(pre_act)).astype(jnp.bfloat16)
    grad_normed = project_back(grad_pre)
    grad_input = input_scale * grad_normed - wide_tokens * input_scale**3 * jnp.mean(
        wide_tokens * grad_normed, axis=1, keepdims=True
    )
    return ((grad_out + grad_input).astype(jnp.bfloat16), weight_part)


def finish_rows(grad_items, rows_wide):
    item_scale = lax.rsqrt(jnp.sum(rows_wide * rows_wide, axis=1, keepdims=True) + epsilon)
    return (
        item_scale * grad_items
        - rows_wide * item_scale**3 * jnp.sum(rows_wide * grad_items, axis=1, keepdims=True)
    ) / loss_scale


def plain_shards(tokens, w_proj, w_out, item_rows, lengths, target_owner, target_row, negative_rows):
    tok_rows = tokens.shape[0]
    model_width = tokens.shape[1]
    shard_count = lax.axis_size("shard")
    capacity = 2 * tok_rows // shard_count
    visible = history_mask(lengths[0], tok_rows)

    def project(normed):
        return jnp.dot(
            normed,
            lax.all_gather(w_proj, "shard", axis=1, tiled=True),
            preferred_element_type=jnp.float32,
        )

    def project_back(grad_pre):
        return reduce_last_dimension(grad_pre, lax.all_gather(w_proj, "shard", axis=1, tiled=True))

    rows_wide = item_rows.astype(jnp.float32)
    item_scale = lax.rsqrt(jnp.sum(rows_wide * rows_wide, axis=1, keepdims=True) + epsilon)
    unit_items = (rows_wide * item_scale).astype(jnp.bfloat16)
    owners = target_owner[:, 0]
    owner_hits = (owners[:, None] == jnp.arange(shard_count, dtype=jnp.int32)[None, :]).astype(
        jnp.int32
    )
    earlier = jnp.cumsum(owner_hits, axis=0) - owner_hits
    slot_index = jnp.sum(earlier * owner_hits, axis=1)
    position = owners * capacity + slot_index
    requests = jnp.zeros((shard_count * capacity,), jnp.int32).at[position].set(target_row)
    asked_rows = lax.all_to_all(
        requests.reshape(shard_count, capacity), "shard", split_axis=0, concat_axis=0, tiled=True
    )
    asked_flat = asked_rows.reshape(-1)
    served = jnp.take(unit_items, asked_flat, axis=0).reshape(shard_count, capacity, model_width)
    fetched = lax.all_to_all(served, "shard", split_axis=0, concat_axis=0, tiled=True)
    clicked_product_vectors = jnp.take(
        fetched.reshape(shard_count * capacity, model_width), position, axis=0
    )
    sampled_decoys = lax.all_gather(
        jnp.take(unit_items, negative_rows, axis=0), "shard", axis=0, tiled=True
    )
    layer_out, saved_state = forward_layer(tokens, project, w_out, visible)
    grad_out, grad_target, negative_probs, normalized_example_vectors = loss_head(
        layer_out, clicked_product_vectors, sampled_decoys
    )
    grad_tokens, weight_part = backward_layer(grad_out, saved_state, project_back, w_out, visible)
    outgoing = (
        jnp.zeros((shard_count * capacity, model_width), jnp.float32).at[position].set(grad_target)
    )
    returned = lax.all_to_all(
        outgoing.reshape(shard_count, capacity, model_width).astype(jnp.bfloat16),
        "shard",
        split_axis=0,
        concat_axis=0,
        tiled=True,
    ).astype(jnp.float32)
    grad_items = (
        jnp.zeros((item_rows.shape[0], model_width), jnp.float32)
        .at[asked_flat]
        .add(returned.reshape(-1, model_width))
    )
    own_negatives = lax.psum_scatter(
        contract_first(negative_probs, normalized_example_vectors).astype(jnp.bfloat16),
        "shard",
        scatter_dimension=0,
        tiled=True,
    ).astype(jnp.float32)
    grad_items = grad_items.at[negative_rows].add(own_negatives)
    share_rows = item_rows.shape[0] // lax.axis_size("dp")
    summed_share = lax.psum_scatter(
        grad_items.astype(jnp.bfloat16), "dp", scatter_dimension=0, tiled=True
    ).astype(jnp.float32)
    share_start = lax.axis_index("dp") * share_rows
    share_wide = lax.dynamic_slice_in_dim(rows_wide, share_start, share_rows, 0)
    item_grads = lax.all_gather(
        finish_rows(summed_share, share_wide).astype(jnp.bfloat16), "dp", axis=0, tiled=True
    ).astype(jnp.float32)
    weight_grads = lax.psum(weight_part, ("dp", "shard")) / loss_scale
    return (grad_tokens, weight_grads, item_grads)


MESH = pl.DeviceIdType.MESH


def start_copy(src, dst, sems, index, target):
    send_sem, recv_sem = sems
    copy = pltpu.make_async_remote_copy(
        src_ref=src,
        dst_ref=dst,
        send_sem=send_sem.at[index],
        recv_sem=recv_sem.at[index],
        device_id=target,
        device_id_type=MESH,
    )
    copy.start()
    return copy


def places(n_dp, n_shard):
    dp = lax.axis_index("dp")
    shard = lax.axis_index("shard")
    core = lax.rem(dp, 2)
    height = dp // 2
    sibling = (dp + 1 - 2 * core, shard)
    shard_peers = [(dp, lax.rem(shard + k, n_shard)) for k in range(1, n_shard)]
    shard_from = [lax.rem(shard + n_shard - k, n_shard) for k in range(1, n_shard)]
    n_z = n_dp // 2
    z_to = [lax.rem(height + k, n_z) for k in range(1, n_z)]
    z_peers = [(z * 2 + core, shard) for z in z_to]
    z_from = [lax.rem(height + n_z - k, n_z) for k in range(1, n_z)]
    return dp, shard, core, height, sibling, shard_peers, shard_from, z_to, z_peers, z_from


def one_hot_columns(position, slots):
    columns = lax.broadcasted_iota(jnp.int32, (position.shape[0], slots), 1)
    return columns == position


def row_picks(asked_row, rows_count):
    rows = lax.broadcasted_iota(jnp.int32, (rows_count, asked_row.shape[1]), 0)
    return jnp.where(rows == asked_row, 1.0, 0.0).astype(jnp.bfloat16)


def as_column(row):
    count = row.shape[1]
    across = lax.broadcasted_iota(jnp.int32, (count, count), 0)
    along = lax.broadcasted_iota(jnp.int32, (count, count), 1)
    return jnp.sum(jnp.where(across == along, row, 0), axis=1, keepdims=True)


def as_row(column):
    count = column.shape[0]
    across = lax.broadcasted_iota(jnp.int32, (count, count), 0)
    along = lax.broadcasted_iota(jnp.int32, (count, count), 1)
    return jnp.sum(jnp.where(across == along, column, 0), axis=0, keepdims=True)


def ones_of(picks):
    return jnp.where(picks, 1.0, 0.0).astype(jnp.bfloat16)


def visible_pairs(lengths, rows_count):
    across = lax.broadcasted_iota(jnp.int32, (rows_count, rows_count), 0)
    along = lax.broadcasted_iota(jnp.int32, (rows_count, rows_count), 1)
    history_a = jnp.zeros((rows_count, rows_count), jnp.int32)
    history_b = jnp.zeros((rows_count, rows_count), jnp.int32)
    end = jnp.zeros((1, 1), jnp.int32)
    for j in range(lengths.shape[1] - 1):
        end = end + lengths[:, j : j + 1]
        history_a += jnp.where(across >= end, 1, 0)
        history_b += jnp.where(along >= end, 1, 0)
    return jnp.where((history_a == history_b) & (along <= across), 1.0 / MAXLEN, 0.0)


def layer_kernel(
    n_dp,
    n_shard,
    capacity,
    tokens_ref,
    w_ref,
    w_out_ref,
    items_ref,
    lengths_ref,
    owner_ref,
    target_ref,
    negative_ref,
    grad_tokens_ref,
    gathered,
    w_gathered,
    w_full,
    negatives,
    requests,
    asked,
    served,
    fetched,
    unit,
    pre,
    act,
    scores_ref,
    visible_ref,
    normed_ref,
    joined_ref,
    grad_joined_ref,
    grad_out_ref,
    grad_pre,
    out_rows,
    in_rows,
    pair_sums,
    pair_in,
    out_sums,
    in_sums,
    out_pair,
    in_pair,
    out_z,
    in_z,
    slots_back,
    picks_ref,
    w_pair,
    w_pair_in,
    w_out_z,
    w_in_z,
    w_out_shard,
    w_in_shard,
    send_sem,
    recv_sem,
):
    dp, shard, core, height, sibling, peers, sources, z_to, z_peers, z_from = places(n_dp, n_shard)
    n_z = n_dp // 2
    others = sources
    near = range(n_shard - 1)
    barrier = pltpu.get_barrier_semaphore()
    greeted = peers + [sibling] + z_peers
    for peer in greeted:
        pl.semaphore_signal(barrier, inc=1, device_id=peer, device_id_type=MESH)
    used = [0]
    started = []

    def send(src, dst, target):
        copy = start_copy(src, dst, (send_sem, recv_sem), used[0], target)
        used[0] += 1
        started.append(copy)
        return copy

    def left(copies):
        for copy in copies:
            copy.wait_send()
            started[:] = [other for other in started if other is not copy]

    rows_count, width = items_ref.shape
    tok_rows = tokens_ref.shape[0]
    neg_rows = negative_ref.shape[1]
    neg_half = neg_rows // 2
    half = w_ref.shape[0] // 2
    share = rows_count // n_dp
    w_rows = width // n_shard
    w_share = w_rows // n_dp
    n_parts, part_cols = out_rows.shape[0], out_rows.shape[-1]

    pl.semaphore_wait(barrier, len(greeted))
    edge = half // 4
    first_row = core * half
    odd = lax.rem(height, 2)
    partner = ((height + 1 - 2 * odd) * 2 + core, shard)
    rows_a = pl.ds(pl.multiple_of(first_row + odd * edge, edge), edge)
    rows_b = pl.ds(pl.multiple_of(first_row + (1 - odd) * edge, edge), edge)
    rows_c = pl.ds(pl.multiple_of(first_row + 2 * edge, edge), half - 2 * edge)
    a_copies = [send(w_ref.at[rows_a], w_full.at[shard, rows_a], peer) for peer in peers]
    owner_row = owner_ref[...]
    owner_col = as_column(owner_row)
    token_a = lax.broadcasted_iota(jnp.int32, (tok_rows, tok_rows), 0)
    token_b = lax.broadcasted_iota(jnp.int32, (tok_rows, tok_rows), 1)
    same = (owner_row == owner_col) & (token_b < token_a)
    slot = jnp.sum(jnp.where(same, 1.0, 0.0), axis=1, keepdims=True).astype(jnp.int32)
    position = owner_col * capacity + slot
    slots = one_hot_columns(position, n_shard * capacity)
    target = as_column(target_ref[...].reshape(1, -1))
    request = jnp.sum(jnp.where(slots, target, 0), axis=0, keepdims=True)
    for j in range(n_shard):
        part = request[:, j * capacity : (j + 1) * capacity]
        requests[j] = jnp.broadcast_to(part, (8, capacity))
    slots_one = ones_of(slots)
    slots_back[...] = row_picks(as_row(position), n_shard * capacity)

    ask_copies = [send(requests.at[peer[1]], asked.at[shard], peer) for peer in peers]
    left(a_copies)
    c_copies = [send(w_ref.at[rows_c], w_full.at[shard, rows_c], peer) for peer in peers]
    w_pairs = []
    b_copies = []
    for k, source in enumerate(others):
        a_copies[k].wait_recv()
        piece = w_full.at[source, rows_a]
        b_copies.append(send(piece, piece, partner))
        w_pairs.append(send(piece, piece, sibling))
    asked[shard] = requests[shard]

    rows_wide = items_ref[...].astype(jnp.float32)
    item_scale = lax.rsqrt(jnp.sum(rows_wide * rows_wide, axis=1, keepdims=True) + epsilon)
    unit[...] = (rows_wide * item_scale).astype(jnp.bfloat16)
    negative_row = negative_ref[...]
    negative_col = as_column(negative_row)
    own_negatives = jnp.dot(
        ones_of(one_hot_columns(negative_col, rows_count)),
        unit[...],
        preferred_element_type=jnp.float32,
    ).astype(jnp.bfloat16)
    negatives[shard, 0] = own_negatives[:neg_half]
    negatives[shard, 1] = own_negatives[neg_half:]
    neg_piece = negatives.at[shard, core]
    neg_copies = [send(neg_piece, neg_piece, peer) for peer in peers]
    w_full[shard] = w_ref[...]
    wide_tokens = tokens_ref[...].astype(jnp.float32)
    input_scale = lax.rsqrt(jnp.mean(wide_tokens * wide_tokens, axis=1, keepdims=True) + epsilon)
    normed_ref[...] = (wide_tokens * input_scale).astype(jnp.bfloat16)
    visible_ref[...] = visible_pairs(lengths_ref[...], tok_rows)

    def section(j):
        values = jnp.dot(normed_ref[...], w_full[j], preferred_element_type=jnp.float32)
        pre[j] = values
        act[j] = (values * lax.logistic(values)).astype(jnp.bfloat16)

    def rows_for(source):
        asked_row = asked[source][0:1]
        picks_ref[source] = row_picks(asked_row, rows_count)
        picks = ones_of(one_hot_columns(as_column(asked_row), rows_count))
        return jnp.dot(picks, unit[...], preferred_element_type=jnp.float32).astype(jnp.bfloat16)

    section(shard)
    for k, source in enumerate(others):
        ask_copies[k].wait_recv()
        served[source] = rows_for(source)
    fetched[shard] = rows_for(shard)
    left(c_copies)
    row_copies = [
        send(served.at[source], fetched.at[shard], (dp, source)) for source in others
    ]
    for rows, arriving in ((rows_c, c_copies), (rows_b, b_copies)):
        for k, source in enumerate(others):
            arriving[k].wait_recv()
            piece = w_full.at[source, rows]
            w_pairs.append(send(piece, piece, sibling))
    neg_pairs = []
    for k, source in enumerate(others):
        neg_copies[k].wait_recv()
        piece = negatives.at[source, core]
        neg_pairs.append(send(piece, piece, sibling))
    for k, source in enumerate(others):
        for copy in w_pairs[k :: n_shard - 1]:
            copy.wait_recv()
        section(source)

    def head_part(j, head):
        return act[j, :, head * DH : (head + 1) * DH]

    for head in range(HEADS):
        scores = head_scores(head_part(2, head), head_part(3, head))
        scores_ref[head] = scores
        weights = (scores * lax.logistic(scores) * visible_ref[...]).astype(jnp.bfloat16)
        joined_ref[:, head * DH : (head + 1) * DH] = jnp.dot(
            weights, head_part(1, head), preferred_element_type=jnp.float32
        ).astype(jnp.bfloat16)
    joined_wide = joined_ref[...].astype(jnp.float32)
    middle_scale = lax.rsqrt(jnp.mean(joined_wide * joined_wide, axis=1, keepdims=True) + epsilon)
    gate_wide = act[0].astype(jnp.float32)
    gated = (joined_wide * middle_scale * gate_wide).astype(jnp.bfloat16)
    layer_out = tokens_ref[...].astype(jnp.float32) + jnp.dot(
        gated, w_out_ref[...], preferred_element_type=jnp.float32
    )
    out_scale = lax.rsqrt(jnp.sum(layer_out * layer_out, axis=1, keepdims=True) + epsilon)
    unit_b = (layer_out * out_scale).astype(jnp.bfloat16)
    for copy in neg_pairs:
        copy.wait_recv()
    negative_exps = []
    for j in range(n_shard):
        for c in range(2):
            logits = reduce_last_dimension(unit_b, negatives[j, c]) / logit_divisor
            negative_exps.append(jnp.exp(logits))
    negative_exp = jnp.concatenate(negative_exps, axis=1)
    for copy in row_copies:
        copy.wait_recv()
    clicked = jnp.zeros((tok_rows, width), jnp.float32)
    for j in range(n_shard):
        clicked += jnp.dot(
            slots_one[:, j * capacity : (j + 1) * capacity],
            fetched[j],
            preferred_element_type=jnp.float32,
        )
    unit_wide = unit_b.astype(jnp.float32)
    target_logit = jnp.sum(unit_wide * clicked, axis=1, keepdims=True) / logit_divisor
    target_exp = jnp.exp(target_logit)
    totals = target_exp + jnp.sum(negative_exp, axis=1, keepdims=True)
    negative_probs = (loss_scale * negative_exp / totals).astype(jnp.bfloat16)
    target_coef = loss_scale * (target_exp / totals - 1.0)
    grad_target = (target_coef * unit_wide).astype(jnp.bfloat16)

    row_sends = []
    for h in range(n_parts):
        for j in range(n_shard):
            out_rows[h, j] = jnp.dot(
                slots_back[j * capacity : (j + 1) * capacity],
                grad_target[:, h * part_cols : (h + 1) * part_cols],
                preferred_element_type=jnp.float32,
            ).astype(jnp.bfloat16)
        if h == 0:
            row_sends.append(
                [send(out_rows.at[h, peer[1]], in_rows.at[h, shard], peer) for peer in peers]
            )
    grad_unit = target_coef * clicked
    for j in range(n_shard):
        for c in range(2):
            first = (2 * j + c) * neg_half
            grad_unit += jnp.dot(
                negative_probs[:, first : first + neg_half],
                negatives[j, c],
                preferred_element_type=jnp.float32,
            )
    grad_out = out_scale * grad_unit - layer_out * out_scale**3 * jnp.sum(
        layer_out * grad_unit, axis=1, keepdims=True
    )
    grad_out_ref[...] = grad_out
    grad_out_b = grad_out.astype(jnp.bfloat16)
    neg_part = contract_first(negative_probs, unit_b).astype(jnp.bfloat16)
    for h in range(n_parts):
        cols = slice(h * part_cols, (h + 1) * part_cols)
        for j in range(n_shard):
            for c in range(2):
                first = (2 * j + c) * neg_half
                pair_sums[c, h, j] = neg_part[first : first + neg_half, cols]
    sum_pair = send(pair_sums.at[1 - core], pair_in, sibling)
    w_part = contract_first(gated, grad_out_b).astype(jnp.bfloat16)
    for c in range(2):
        for j in range(n_shard):
            for z in range(n_z):
                first = ((c * n_shard + j) * n_z + z) * w_share
                w_pair[c, z, j] = w_part[first : first + w_share]
    w_pair_copy = send(w_pair.at[1 - core], w_pair_in, sibling)
    sum_pair.wait_recv()
    out_sums[...] = (
        pair_sums[core].astype(jnp.float32) + pair_in[...].astype(jnp.float32)
    ).astype(jnp.bfloat16)
    sum_sends = []
    for h in range(n_parts):
        if h > 0:
            row_sends.append(
                [send(out_rows.at[h, peer[1]], in_rows.at[h, shard], peer) for peer in peers]
            )
        sum_sends.append(
            [send(out_sums.at[h, peer[1]], in_sums.at[h, shard], peer) for peer in peers]
        )
    w_pair_copy.wait_recv()
    w_out_z[...] = (
        w_pair[core].astype(jnp.float32) + w_pair_in[...].astype(jnp.float32)
    ).astype(jnp.bfloat16)
    w_z_sends = [
        send(w_out_z.at[z_to[k]], w_in_z.at[height], peer) for k, peer in enumerate(z_peers)
    ]

    grad_gated = reduce_last_dimension(grad_out_b, w_out_ref[...])
    grad_pre[0] = (grad_gated * joined_wide * middle_scale * silu_slope(pre[0])).astype(
        jnp.bfloat16
    )
    grad_norm = grad_gated * gate_wide
    grad_joined_ref[...] = (
        middle_scale * grad_norm
        - joined_wide
        * middle_scale**3
        * jnp.mean(joined_wide * grad_norm, axis=1, keepdims=True)
    ).astype(jnp.bfloat16)

    def head_back(head):
        cols = slice(head * DH, (head + 1) * DH)
        scores = scores_ref[head]
        sigmoid = lax.logistic(scores)
        visible = visible_ref[...]
        weights = (scores * sigmoid * visible).astype(jnp.bfloat16)
        grad_head = grad_joined_ref[:, cols]
        grad_weights = reduce_last_dimension(grad_head, head_part(1, head))
        slope = sigmoid * (1.0 + scores * (1.0 - sigmoid))
        grad_scores = (grad_weights * visible * slope * DH ** (-0.5)).astype(jnp.bfloat16)
        grads = (
            contract_first(weights, grad_head),
            jnp.dot(grad_scores, head_part(3, head), preferred_element_type=jnp.float32),
            contract_first(grad_scores, head_part(2, head)),
        )
        for j, grad in enumerate(grads):
            grad_pre[j + 1, :, cols] = (grad * silu_slope(pre[j + 1, :, cols])).astype(
                jnp.bfloat16
            )

    def collect(h):
        grad_items = jnp.zeros((rows_count, part_cols), jnp.float32)
        sums = jnp.zeros((neg_half, part_cols), jnp.float32)
        for k, source in enumerate([shard] + others):
            if k > 0:
                row_sends[h][k - 1].wait_recv()
                sum_sends[h][k - 1].wait_recv()
            rows = out_rows[h, shard] if k == 0 else in_rows[h, source]
            part = out_sums[h, shard] if k == 0 else in_sums[h, source]
            grad_items += jnp.dot(picks_ref[source], rows, preferred_element_type=jnp.float32)
            sums += part.astype(jnp.float32)
        own_rows = jnp.where(core == 0, negative_row[:, :neg_half], negative_row[:, neg_half:])
        grad_items += jnp.dot(
            row_picks(own_rows, rows_count),
            sums.astype(jnp.bfloat16),
            preferred_element_type=jnp.float32,
        )
        for z in range(n_z):
            for c in range(2):
                d = z * 2 + c
                out_pair[h, c, z] = grad_items[d * share : (d + 1) * share].astype(jnp.bfloat16)
        return send(out_pair.at[h, 1 - core], in_pair.at[h], sibling)

    def pass_on(h, pair):
        pair.wait_recv()
        for z in range(n_z):
            out_z[h, z] = (
                out_pair[h, core, z].astype(jnp.float32) + in_pair[h, z].astype(jnp.float32)
            ).astype(jnp.bfloat16)
        return [
            send(out_z.at[h, z_to[k]], in_z.at[h, height], peer) for k, peer in enumerate(z_peers)
        ]

    head_back(0)
    pair = collect(0)
    z_sends = [pass_on(0, pair)]
    head_back(1)
    w_total = w_out_z[height].astype(jnp.float32)
    for k, z in enumerate(z_from):
        w_z_sends[k].wait_recv()
        w_total += w_in_z[z].astype(jnp.float32)
    w_out_shard[...] = w_total.astype(jnp.bfloat16)
    w_sends = [send(w_out_shard.at[peer[1]], w_in_shard.at[shard], peer) for peer in peers]
    pair = collect(1)
    head_back(2)
    z_sends.append(pass_on(1, pair))
    w_total = w_out_shard[shard].astype(jnp.float32)
    for k, source in enumerate(others):
        w_sends[k].wait_recv()
        w_total += w_in_shard[source].astype(jnp.float32)
    w_gathered[core, shard, height] = (w_total / loss_scale).astype(jnp.bfloat16)
    w_mine = w_gathered.at[core, shard, height]
    w_z = [send(w_mine, w_mine, peer) for peer in z_peers]
    for head in range(3, HEADS):
        head_back(head)
    for copy in w_z:
        copy.wait_recv()
    w_block = w_gathered.at[core, shard]
    w_around = [send(w_block, w_block, peer) for peer in peers]
    last = [send(w_block, w_block, sibling)]
    grad_normed = jnp.zeros((tok_rows, width), jnp.float32)
    for j in range(n_shard):
        grad_normed += reduce_last_dimension(grad_pre[j], w_full[j])
    wide_tokens = tokens_ref[...].astype(jnp.float32)
    grad_input = input_scale * grad_normed - wide_tokens * input_scale**3 * jnp.mean(
        wide_tokens * grad_normed, axis=1, keepdims=True
    )
    grad_tokens_ref[...] = (grad_out_ref[...] + grad_input).astype(jnp.bfloat16)

    totals_parts = []
    for h in range(n_parts):
        total = out_z[h, height].astype(jnp.float32)
        for k, z in enumerate(z_from):
            z_sends[h][k].wait_recv()
            total += in_z[h, z].astype(jnp.float32)
        totals_parts.append(total)
    total = jnp.concatenate(totals_parts, axis=1)
    own = pl.ds(pl.multiple_of(dp * share, share), share)
    finished = finish_rows(total, items_ref[own].astype(jnp.float32))
    gathered[height, core] = finished.astype(jnp.bfloat16)
    items_mine = gathered.at[height, core]
    items_z = [send(items_mine, items_mine, peer) for peer in z_peers]
    last.append(send(items_mine, items_mine, sibling))
    for k, source in enumerate(others):
        w_around[k].wait_recv()
        piece = w_gathered.at[core, source]
        last.append(send(piece, piece, sibling))
    for k, z in enumerate(z_from):
        items_z[k].wait_recv()
        piece = gathered.at[z, core]
        last.append(send(piece, piece, sibling))
    for copy in last:
        copy.wait_recv()
    for copy in started:
        copy.wait_send()


def vmem_specs(count):
    return [pl.BlockSpec(memory_space=pltpu.VMEM)] * count


def shards(tokens, w_proj, w_out, item_rows, lengths, target_owner, target_row, negative_rows):
    tok_rows, width = tokens.shape
    n_shard = lax.axis_size("shard")
    n_dp = lax.axis_size("dp")
    n_z = n_dp // 2
    capacity = 2 * tok_rows // n_shard
    rows_count = item_rows.shape[0]
    neg_half = negative_rows.shape[0] // 2
    share = rows_count // n_dp
    w_half = width // n_shard // 2
    w_share = w_half // n_z
    parts = 2
    cols = width // parts
    b16 = jnp.bfloat16
    f32 = jnp.float32
    shape = jax.ShapeDtypeStruct
    copies = 7 * (n_shard - 1) + 4 * parts * (n_shard + n_z) + 2 * (n_shard + n_z) + 8
    grad_tokens, gathered, w_gathered = pl.pallas_call(
        functools.partial(layer_kernel, n_dp, n_shard, capacity),
        out_shape=[
            shape((tok_rows, width), b16),
            shape((n_z, 2, share, width), b16),
            shape((2, n_shard, n_z, w_share, width), b16),
        ],
        in_specs=vmem_specs(8),
        out_specs=vmem_specs(3),
        scratch_shapes=[
            pltpu.VMEM((n_shard, width, width), b16),
            pltpu.VMEM((n_shard, 2, neg_half, width), b16),
            pltpu.VMEM((n_shard, 8, capacity), jnp.int32),
            pltpu.VMEM((n_shard, 8, capacity), jnp.int32),
            pltpu.VMEM((n_shard, capacity, width), b16),
            pltpu.VMEM((n_shard, capacity, width), b16),
            pltpu.VMEM((rows_count, width), b16),
            pltpu.VMEM((4, tok_rows, width), f32),
            pltpu.VMEM((4, tok_rows, width), b16),
            pltpu.VMEM((HEADS, tok_rows, tok_rows), f32),
            pltpu.VMEM((tok_rows, tok_rows), f32),
            pltpu.VMEM((tok_rows, width), b16),
            pltpu.VMEM((tok_rows, width), b16),
            pltpu.VMEM((tok_rows, width), b16),
            pltpu.VMEM((tok_rows, width), f32),
            pltpu.VMEM((4, tok_rows, width), b16),
            pltpu.VMEM((parts, n_shard, capacity, cols), b16),
            pltpu.VMEM((parts, n_shard, capacity, cols), b16),
            pltpu.VMEM((2, parts, n_shard, neg_half, cols), b16),
            pltpu.VMEM((parts, n_shard, neg_half, cols), b16),
            pltpu.VMEM((parts, n_shard, neg_half, cols), b16),
            pltpu.VMEM((parts, n_shard, neg_half, cols), b16),
            pltpu.VMEM((parts, 2, n_z, share, cols), b16),
            pltpu.VMEM((parts, n_z, share, cols), b16),
            pltpu.VMEM((parts, n_z, share, cols), b16),
            pltpu.VMEM((parts, n_z, share, cols), b16),
            pltpu.VMEM((n_shard * capacity, tok_rows), b16),
            pltpu.VMEM((n_shard, rows_count, capacity), b16),
            pltpu.VMEM((2, n_z, n_shard, w_share, width), b16),
            pltpu.VMEM((n_z, n_shard, w_share, width), b16),
            pltpu.VMEM((n_z, n_shard, w_share, width), b16),
            pltpu.VMEM((n_z, n_shard, w_share, width), b16),
            pltpu.VMEM((n_shard, w_share, width), b16),
            pltpu.VMEM((n_shard, w_share, width), b16),
            pltpu.SemaphoreType.DMA((copies,)),
            pltpu.SemaphoreType.DMA((copies,)),
        ],
        compiler_params=pltpu.CompilerParams(
            collective_id=0, has_side_effects=True, vmem_limit_bytes=56 * 2**20
        ),
        name="layer",
    )(
        tokens,
        w_proj,
        w_out,
        item_rows,
        lengths,
        target_owner.reshape(1, -1),
        target_row,
        negative_rows.reshape(1, -1),
    )
    item_grads = gathered.reshape(rows_count, width).astype(f32)
    return (grad_tokens, w_gathered.reshape(width, width).astype(f32), item_grads)


def fits_kernels(mesh):
    n_dp, n_shard = mesh.shape["dp"], mesh.shape["shard"]
    return n_dp % 2 == 0 and n_dp > 2 and n_shard == 4 and n_dp % 4 == 0 and D % (16 * n_dp * n_shard) == 0


def solution(mesh):
    in_specs = (
        P(("dp", "shard"), None),
        P(None, "shard"),
        P(),
        P("shard", None),
        P(("dp", "shard"), None),
        P(("dp", "shard"), None),
        P(("dp", "shard")),
        P("shard"),
    )
    out_specs = (P(("dp", "shard"), None), P(), P("shard", None))
    return jax.shard_map(
        shards if fits_kernels(mesh) else plain_shards,
        mesh=mesh, in_specs=in_specs, out_specs=out_specs, check_vma=False)
```

```python
import functools

import jax
import jax.numpy as jnp
from jax import lax
from jax.experimental import pallas as pl
from jax.experimental.pallas import tpu as pltpu
from jax.sharding import PartitionSpec as P

D = 512
HEADS = 4
DH = 128
MAXLEN = 192


epsilon = 1e-06
logit_divisor = 0.015625
loss_scale = 512.0


def reduce_last_dimension(operand, other_side):
    return lax.dot_general(
        operand, other_side, (((1,), (1,)), ((), ())), preferred_element_type=jnp.float32
    )


def contract_first(operand, other_side):
    return lax.dot_general(
        operand, other_side, (((0,), (0,)), ((), ())), preferred_element_type=jnp.float32
    )


def silu_slope(values):
    sigmoid = jax.nn.sigmoid(values)
    return sigmoid * (1.0 + values * (1.0 - sigmoid))


def history_mask(lengths_row, rows_count):
    history_ends = jnp.cumsum(lengths_row)
    positions = jnp.arange(rows_count, dtype=jnp.int32)
    history_ids = jnp.sum((positions[:, None] >= history_ends[None, :-1]).astype(jnp.int32), axis=1)
    visible = (history_ids[:, None] == history_ids[None, :]) & (
        positions[None, :] <= positions[:, None]
    )
    return jnp.where(visible, 1.0, 0.0).astype(jnp.float32)


def head_columns(activated, section, head_index):
    first_col = section * D + head_index * DH
    return activated[:, first_col : first_col + DH]


def head_scores(queries, key_rows):
    return reduce_last_dimension(queries, key_rows) * DH ** (-0.5)


def head_weights(scores, visible):
    return (jax.nn.silu(scores) * visible * (1.0 / MAXLEN)).astype(jnp.bfloat16)


def forward_layer(tokens, project, w_out, visible):
    wide_tokens = tokens.astype(jnp.float32)
    input_scale = lax.rsqrt(jnp.mean(wide_tokens * wide_tokens, axis=1, keepdims=True) + epsilon)
    normed = (wide_tokens * input_scale).astype(jnp.bfloat16)
    pre_act = project(normed)
    activated = lax.optimization_barrier(jax.nn.silu(pre_act).astype(jnp.bfloat16))
    heads_out = []
    for head_index in range(HEADS):
        queries = head_columns(activated, 2, head_index)
        key_rows = head_columns(activated, 3, head_index)
        value_rows = head_columns(activated, 1, head_index)
        weights = head_weights(head_scores(queries, key_rows), visible)
        heads_out.append(jnp.dot(weights, value_rows, preferred_element_type=jnp.float32))
    joined = lax.optimization_barrier(jnp.concatenate(heads_out, axis=1).astype(jnp.bfloat16))
    joined_wide = joined.astype(jnp.float32)
    middle_scale = lax.rsqrt(jnp.mean(joined_wide * joined_wide, axis=1, keepdims=True) + epsilon)
    gate_wide = activated[:, :D].astype(jnp.float32)
    gated = (joined_wide * middle_scale * gate_wide).astype(jnp.bfloat16)
    layer_out = wide_tokens + jnp.dot(gated, w_out, preferred_element_type=jnp.float32)
    return (layer_out, (wide_tokens, input_scale, pre_act, activated, joined, middle_scale, gated))


def loss_head(layer_out, clicked_product_vectors, sampled_decoys):
    out_scale = lax.rsqrt(jnp.sum(layer_out * layer_out, axis=1, keepdims=True) + epsilon)
    normalized_example_vectors = lax.optimization_barrier(
        (layer_out * out_scale).astype(jnp.bfloat16)
    )
    normalized_complete_embedding = normalized_example_vectors.astype(jnp.float32)
    correct_logit_entry = (
        jnp.sum(normalized_complete_embedding * clicked_product_vectors.astype(jnp.float32), axis=1)
        / logit_divisor
    )
    decoy_logit_entries = (
        reduce_last_dimension(normalized_example_vectors, sampled_decoys) / logit_divisor
    )
    target_exp = jnp.exp(correct_logit_entry)
    negative_exp = jnp.exp(decoy_logit_entries)
    totals = target_exp + jnp.sum(negative_exp, axis=1)
    target_prob = target_exp / totals
    negative_probs = (loss_scale * negative_exp / totals[:, None]).astype(jnp.bfloat16)
    target_coef = (loss_scale * (target_prob - 1.0))[:, None]
    grad_unit = target_coef * clicked_product_vectors.astype(jnp.float32) + jnp.dot(
        negative_probs, sampled_decoys, preferred_element_type=jnp.float32
    )
    grad_out = out_scale * grad_unit - layer_out * out_scale**3 * jnp.sum(
        layer_out * grad_unit, axis=1, keepdims=True
    )
    grad_target = target_coef * normalized_complete_embedding
    return (grad_out, grad_target, negative_probs, normalized_example_vectors)


def backward_layer(grad_out, saved_state, project_back, w_out, visible):
    wide_tokens, input_scale, pre_act, activated, joined, middle_scale, gated = saved_state
    grad_out_b = grad_out.astype(jnp.bfloat16)
    weight_part = contract_first(gated, grad_out_b)
    grad_gated = reduce_last_dimension(grad_out_b, w_out)
    joined_wide = joined.astype(jnp.float32)
    gate_wide = activated[:, :D].astype(jnp.float32)
    grad_gate = grad_gated * joined_wide * middle_scale
    grad_norm = grad_gated * gate_wide
    grad_joined = middle_scale * grad_norm - joined_wide * middle_scale**3 * jnp.mean(
        joined_wide * grad_norm, axis=1, keepdims=True
    )
    grad_joined_b = grad_joined.astype(jnp.bfloat16)
    grad_values = []
    grad_queries = []
    grad_keys = []
    for head_index in range(HEADS):
        queries = head_columns(activated, 2, head_index)
        key_rows = head_columns(activated, 3, head_index)
        value_rows = head_columns(activated, 1, head_index)
        scores = head_scores(queries, key_rows)
        weights = head_weights(scores, visible)
        grad_head = grad_joined_b[:, head_index * DH : (head_index + 1) * DH]
        grad_weights = reduce_last_dimension(grad_head, value_rows)
        grad_values.append(contract_first(weights, grad_head))
        grad_scores = (
            grad_weights * visible * (1.0 / MAXLEN) * silu_slope(scores) * DH ** (-0.5)
        ).astype(jnp.bfloat16)
        grad_queries.append(jnp.dot(grad_scores, key_rows, preferred_element_type=jnp.float32))
        grad_keys.append(contract_first(grad_scores, queries))
    grad_act = jnp.concatenate([grad_gate] + grad_values + grad_queries + grad_keys, axis=1)
    grad_pre = (grad_act * silu_slope(pre_act)).astype(jnp.bfloat16)
    grad_normed = project_back(grad_pre)
    grad_input = input_scale * grad_normed - wide_tokens * input_scale**3 * jnp.mean(
        wide_tokens * grad_normed, axis=1, keepdims=True
    )
    return ((grad_out + grad_input).astype(jnp.bfloat16), weight_part)


def finish_rows(grad_items, rows_wide):
    item_scale = lax.rsqrt(jnp.sum(rows_wide * rows_wide, axis=1, keepdims=True) + epsilon)
    return (
        item_scale * grad_items
        - rows_wide * item_scale**3 * jnp.sum(rows_wide * grad_items, axis=1, keepdims=True)
    ) / loss_scale


def plain_shards(tokens, w_proj, w_out, item_rows, lengths, target_owner, target_row, negative_rows):
    tok_rows = tokens.shape[0]
    model_width = tokens.shape[1]
    shard_count = lax.axis_size("shard")
    capacity = 2 * tok_rows // shard_count
    visible = history_mask(lengths[0], tok_rows)

    def project(normed):
        return jnp.dot(
            normed,
            lax.all_gather(w_proj, "shard", axis=1, tiled=True),
            preferred_element_type=jnp.float32,
        )

    def project_back(grad_pre):
        return reduce_last_dimension(grad_pre, lax.all_gather(w_proj, "shard", axis=1, tiled=True))

    rows_wide = item_rows.astype(jnp.float32)
    item_scale = lax.rsqrt(jnp.sum(rows_wide * rows_wide, axis=1, keepdims=True) + epsilon)
    unit_items = (rows_wide * item_scale).astype(jnp.bfloat16)
    owners = target_owner[:, 0]
    owner_hits = (owners[:, None] == jnp.arange(shard_count, dtype=jnp.int32)[None, :]).astype(
        jnp.int32
    )
    earlier = jnp.cumsum(owner_hits, axis=0) - owner_hits
    slot_index = jnp.sum(earlier * owner_hits, axis=1)
    position = owners * capacity + slot_index
    requests = jnp.zeros((shard_count * capacity,), jnp.int32).at[position].set(target_row)
    asked_rows = lax.all_to_all(
        requests.reshape(shard_count, capacity), "shard", split_axis=0, concat_axis=0, tiled=True
    )
    asked_flat = asked_rows.reshape(-1)
    served = jnp.take(unit_items, asked_flat, axis=0).reshape(shard_count, capacity, model_width)
    fetched = lax.all_to_all(served, "shard", split_axis=0, concat_axis=0, tiled=True)
    clicked_product_vectors = jnp.take(
        fetched.reshape(shard_count * capacity, model_width), position, axis=0
    )
    sampled_decoys = lax.all_gather(
        jnp.take(unit_items, negative_rows, axis=0), "shard", axis=0, tiled=True
    )
    layer_out, saved_state = forward_layer(tokens, project, w_out, visible)
    grad_out, grad_target, negative_probs, normalized_example_vectors = loss_head(
        layer_out, clicked_product_vectors, sampled_decoys
    )
    grad_tokens, weight_part = backward_layer(grad_out, saved_state, project_back, w_out, visible)
    outgoing = (
        jnp.zeros((shard_count * capacity, model_width), jnp.float32).at[position].set(grad_target)
    )
    returned = lax.all_to_all(
        outgoing.reshape(shard_count, capacity, model_width).astype(jnp.bfloat16),
        "shard",
        split_axis=0,
        concat_axis=0,
        tiled=True,
    ).astype(jnp.float32)
    grad_items = (
        jnp.zeros((item_rows.shape[0], model_width), jnp.float32)
        .at[asked_flat]
        .add(returned.reshape(-1, model_width))
    )
    own_negatives = lax.psum_scatter(
        contract_first(negative_probs, normalized_example_vectors).astype(jnp.bfloat16),
        "shard",
        scatter_dimension=0,
        tiled=True,
    ).astype(jnp.float32)
    grad_items = grad_items.at[negative_rows].add(own_negatives)
    share_rows = item_rows.shape[0] // lax.axis_size("dp")
    summed_share = lax.psum_scatter(
        grad_items.astype(jnp.bfloat16), "dp", scatter_dimension=0, tiled=True
    ).astype(jnp.float32)
    share_start = lax.axis_index("dp") * share_rows
    share_wide = lax.dynamic_slice_in_dim(rows_wide, share_start, share_rows, 0)
    item_grads = lax.all_gather(
        finish_rows(summed_share, share_wide).astype(jnp.bfloat16), "dp", axis=0, tiled=True
    ).astype(jnp.float32)
    weight_grads = lax.psum(weight_part, ("dp", "shard")) / loss_scale
    return (grad_tokens, weight_grads, item_grads)


MESH = pl.DeviceIdType.MESH


def start_copy(src, dst, sems, index, target):
    send_sem, recv_sem = sems
    copy = pltpu.make_async_remote_copy(
        src_ref=src,
        dst_ref=dst,
        send_sem=send_sem.at[index],
        recv_sem=recv_sem.at[index],
        device_id=target,
        device_id_type=MESH,
    )
    copy.start()
    return copy


def places(n_dp, n_shard):
    dp = lax.axis_index("dp")
    shard = lax.axis_index("shard")
    core = lax.rem(dp, 2)
    height = dp // 2
    sibling = (dp + 1 - 2 * core, shard)
    shard_peers = [(dp, lax.rem(shard + k, n_shard)) for k in range(1, n_shard)]
    shard_from = [lax.rem(shard + n_shard - k, n_shard) for k in range(1, n_shard)]
    n_z = n_dp // 2
    z_to = [lax.rem(height + k, n_z) for k in range(1, n_z)]
    z_peers = [(z * 2 + core, shard) for z in z_to]
    z_from = [lax.rem(height + n_z - k, n_z) for k in range(1, n_z)]
    return dp, shard, core, height, sibling, shard_peers, shard_from, z_to, z_peers, z_from


def one_hot_columns(position, slots):
    columns = lax.broadcasted_iota(jnp.int32, (position.shape[0], slots), 1)
    return columns == position


def row_picks(asked_row, rows_count):
    rows = lax.broadcasted_iota(jnp.int32, (rows_count, asked_row.shape[1]), 0)
    return jnp.where(rows == asked_row, 1.0, 0.0).astype(jnp.bfloat16)


def as_column(row):
    count = row.shape[1]
    across = lax.broadcasted_iota(jnp.int32, (count, count), 0)
    along = lax.broadcasted_iota(jnp.int32, (count, count), 1)
    return jnp.sum(jnp.where(across == along, row, 0), axis=1, keepdims=True)


def as_row(column):
    count = column.shape[0]
    across = lax.broadcasted_iota(jnp.int32, (count, count), 0)
    along = lax.broadcasted_iota(jnp.int32, (count, count), 1)
    return jnp.sum(jnp.where(across == along, column, 0), axis=0, keepdims=True)


def ones_of(picks):
    return jnp.where(picks, 1.0, 0.0).astype(jnp.bfloat16)


def visible_pairs(lengths, rows_count):
    across = lax.broadcasted_iota(jnp.int32, (rows_count, rows_count), 0)
    along = lax.broadcasted_iota(jnp.int32, (rows_count, rows_count), 1)
    history_a = jnp.zeros((rows_count, rows_count), jnp.int32)
    history_b = jnp.zeros((rows_count, rows_count), jnp.int32)
    end = jnp.zeros((1, 1), jnp.int32)
    for j in range(lengths.shape[1] - 1):
        end = end + lengths[:, j : j + 1]
        history_a += jnp.where(across >= end, 1, 0)
        history_b += jnp.where(along >= end, 1, 0)
    return jnp.where((history_a == history_b) & (along <= across), 1.0 / MAXLEN, 0.0)


def layer_kernel(
    n_dp,
    n_shard,
    capacity,
    tokens_ref,
    w_ref,
    w_out_ref,
    items_ref,
    lengths_ref,
    owner_ref,
    target_ref,
    negative_ref,
    grad_tokens_ref,
    item_grads_ref,
    weight_grads_ref,
    gathered,
    w_gathered,
    w_full,
    negatives,
    requests,
    asked,
    served,
    fetched,
    unit,
    pre,
    act,
    scores_ref,
    visible_ref,
    normed_ref,
    joined_ref,
    grad_joined_ref,
    grad_out_ref,
    grad_pre,
    out_rows,
    in_rows,
    pair_sums,
    pair_in,
    out_sums,
    in_sums,
    out_pair,
    in_pair,
    out_z,
    in_z,
    slots_back,
    picks_ref,
    w_pair,
    w_pair_in,
    w_out_z,
    w_in_z,
    w_out_shard,
    w_in_shard,
    send_sem,
    recv_sem,
):
    dp, shard, core, height, sibling, peers, sources, z_to, z_peers, z_from = places(n_dp, n_shard)
    n_z = n_dp // 2
    others = sources
    near = range(n_shard - 1)
    barrier = pltpu.get_barrier_semaphore()
    greeted = peers + [sibling] + z_peers
    for peer in greeted:
        pl.semaphore_signal(barrier, inc=1, device_id=peer, device_id_type=MESH)
    used = [0]
    started = []

    def send(src, dst, target):
        copy = start_copy(src, dst, (send_sem, recv_sem), used[0], target)
        used[0] += 1
        started.append(copy)
        return copy

    def left(copies):
        for copy in copies:
            copy.wait_send()
            started[:] = [other for other in started if other is not copy]

    rows_count, width = items_ref.shape
    tok_rows = tokens_ref.shape[0]
    neg_rows = negative_ref.shape[1]
    neg_half = neg_rows // 2
    half = w_ref.shape[0] // 2
    share = rows_count // n_dp
    w_rows = width // n_shard
    w_share = w_rows // n_dp
    n_parts, part_cols = out_rows.shape[0], out_rows.shape[-1]

    pl.semaphore_wait(barrier, len(greeted))
    edge = half // 4
    first_row = core * half
    odd = lax.rem(height, 2)
    partner = ((height + 1 - 2 * odd) * 2 + core, shard)
    rows_a = pl.ds(pl.multiple_of(first_row + odd * edge, edge), edge)
    rows_b = pl.ds(pl.multiple_of(first_row + (1 - odd) * edge, edge), edge)
    rows_c = pl.ds(pl.multiple_of(first_row + 2 * edge, edge), half - 2 * edge)
    a_copies = [send(w_ref.at[rows_a], w_full.at[shard, rows_a], peer) for peer in peers]
    owner_row = owner_ref[...]
    owner_col = as_column(owner_row)
    token_a = lax.broadcasted_iota(jnp.int32, (tok_rows, tok_rows), 0)
    token_b = lax.broadcasted_iota(jnp.int32, (tok_rows, tok_rows), 1)
    same = (owner_row == owner_col) & (token_b < token_a)
    slot = jnp.sum(jnp.where(same, 1.0, 0.0), axis=1, keepdims=True).astype(jnp.int32)
    position = owner_col * capacity + slot
    slots = one_hot_columns(position, n_shard * capacity)
    target = as_column(target_ref[...].reshape(1, -1))
    request = jnp.sum(jnp.where(slots, target, 0), axis=0, keepdims=True)
    for j in range(n_shard):
        part = request[:, j * capacity : (j + 1) * capacity]
        requests[j] = jnp.broadcast_to(part, (8, capacity))
    slots_one = ones_of(slots)
    slots_back[...] = row_picks(as_row(position), n_shard * capacity)

    ask_copies = [send(requests.at[peer[1]], asked.at[shard], peer) for peer in peers]
    left(a_copies)
    c_copies = [send(w_ref.at[rows_c], w_full.at[shard, rows_c], peer) for peer in peers]
    w_pairs = []
    b_copies = []
    for k, source in enumerate(others):
        a_copies[k].wait_recv()
        piece = w_full.at[source, rows_a]
        b_copies.append(send(piece, piece, partner))
        w_pairs.append(send(piece, piece, sibling))
    asked[shard] = requests[shard]

    rows_wide = items_ref[...].astype(jnp.float32)
    item_scale = lax.rsqrt(jnp.sum(rows_wide * rows_wide, axis=1, keepdims=True) + epsilon)
    unit[...] = (rows_wide * item_scale).astype(jnp.bfloat16)
    negative_row = negative_ref[...]
    negative_col = as_column(negative_row)
    own_negatives = jnp.dot(
        ones_of(one_hot_columns(negative_col, rows_count)),
        unit[...],
        preferred_element_type=jnp.float32,
    ).astype(jnp.bfloat16)
    negatives[shard, 0] = own_negatives[:neg_half]
    negatives[shard, 1] = own_negatives[neg_half:]
    neg_piece = negatives.at[shard, core]
    neg_copies = [send(neg_piece, neg_piece, peer) for peer in peers]
    w_full[shard] = w_ref[...]
    wide_tokens = tokens_ref[...].astype(jnp.float32)
    input_scale = lax.rsqrt(jnp.mean(wide_tokens * wide_tokens, axis=1, keepdims=True) + epsilon)
    normed_ref[...] = (wide_tokens * input_scale).astype(jnp.bfloat16)
    visible_ref[...] = visible_pairs(lengths_ref[...], tok_rows)

    def section(j):
        values = jnp.dot(normed_ref[...], w_full[j], preferred_element_type=jnp.float32)
        pre[j] = values
        act[j] = (values * lax.logistic(values)).astype(jnp.bfloat16)

    def rows_for(source):
        asked_row = asked[source][0:1]
        picks_ref[source] = row_picks(asked_row, rows_count)
        picks = ones_of(one_hot_columns(as_column(asked_row), rows_count))
        return jnp.dot(picks, unit[...], preferred_element_type=jnp.float32).astype(jnp.bfloat16)

    section(shard)
    for k, source in enumerate(others):
        ask_copies[k].wait_recv()
        served[source] = rows_for(source)
    fetched[shard] = rows_for(shard)
    left(c_copies)
    row_copies = [
        send(served.at[source], fetched.at[shard], (dp, source)) for source in others
    ]
    for rows, arriving in ((rows_c, c_copies), (rows_b, b_copies)):
        for k, source in enumerate(others):
            arriving[k].wait_recv()
            piece = w_full.at[source, rows]
            w_pairs.append(send(piece, piece, sibling))
    neg_pairs = []
    for k, source in enumerate(others):
        neg_copies[k].wait_recv()
        piece = negatives.at[source, core]
        neg_pairs.append(send(piece, piece, sibling))
    for k, source in enumerate(others):
        for copy in w_pairs[k :: n_shard - 1]:
            copy.wait_recv()
        section(source)

    def head_part(j, head):
        return act[j, :, head * DH : (head + 1) * DH]

    for head in range(HEADS):
        scores = head_scores(head_part(2, head), head_part(3, head))
        scores_ref[head] = scores
        weights = (scores * lax.logistic(scores) * visible_ref[...]).astype(jnp.bfloat16)
        joined_ref[:, head * DH : (head + 1) * DH] = jnp.dot(
            weights, head_part(1, head), preferred_element_type=jnp.float32
        ).astype(jnp.bfloat16)
    joined_wide = joined_ref[...].astype(jnp.float32)
    middle_scale = lax.rsqrt(jnp.mean(joined_wide * joined_wide, axis=1, keepdims=True) + epsilon)
    gate_wide = act[0].astype(jnp.float32)
    gated = (joined_wide * middle_scale * gate_wide).astype(jnp.bfloat16)
    layer_out = tokens_ref[...].astype(jnp.float32) + jnp.dot(
        gated, w_out_ref[...], preferred_element_type=jnp.float32
    )
    out_scale = lax.rsqrt(jnp.sum(layer_out * layer_out, axis=1, keepdims=True) + epsilon)
    unit_b = (layer_out * out_scale).astype(jnp.bfloat16)
    for copy in neg_pairs:
        copy.wait_recv()
    negative_exps = []
    for j in range(n_shard):
        for c in range(2):
            logits = reduce_last_dimension(unit_b, negatives[j, c]) / logit_divisor
            negative_exps.append(jnp.exp(logits))
    negative_exp = jnp.concatenate(negative_exps, axis=1)
    for copy in row_copies:
        copy.wait_recv()
    clicked = jnp.zeros((tok_rows, width), jnp.float32)
    for j in range(n_shard):
        clicked += jnp.dot(
            slots_one[:, j * capacity : (j + 1) * capacity],
            fetched[j],
            preferred_element_type=jnp.float32,
        )
    unit_wide = unit_b.astype(jnp.float32)
    target_logit = jnp.sum(unit_wide * clicked, axis=1, keepdims=True) / logit_divisor
    target_exp = jnp.exp(target_logit)
    totals = target_exp + jnp.sum(negative_exp, axis=1, keepdims=True)
    negative_probs = (loss_scale * negative_exp / totals).astype(jnp.bfloat16)
    target_coef = loss_scale * (target_exp / totals - 1.0)
    grad_target = (target_coef * unit_wide).astype(jnp.bfloat16)

    row_sends = []
    for h in range(n_parts):
        for j in range(n_shard):
            out_rows[h, j] = jnp.dot(
                slots_back[j * capacity : (j + 1) * capacity],
                grad_target[:, h * part_cols : (h + 1) * part_cols],
                preferred_element_type=jnp.float32,
            ).astype(jnp.bfloat16)
        if h == 0:
            row_sends.append(
                [send(out_rows.at[h, peer[1]], in_rows.at[h, shard], peer) for peer in peers]
            )
    grad_unit = target_coef * clicked
    for j in range(n_shard):
        for c in range(2):
            first = (2 * j + c) * neg_half
            grad_unit += jnp.dot(
                negative_probs[:, first : first + neg_half],
                negatives[j, c],
                preferred_element_type=jnp.float32,
            )
    grad_out = out_scale * grad_unit - layer_out * out_scale**3 * jnp.sum(
        layer_out * grad_unit, axis=1, keepdims=True
    )
    grad_out_ref[...] = grad_out
    grad_out_b = grad_out.astype(jnp.bfloat16)
    neg_part = contract_first(negative_probs, unit_b).astype(jnp.bfloat16)
    for h in range(n_parts):
        cols = slice(h * part_cols, (h + 1) * part_cols)
        for j in range(n_shard):
            for c in range(2):
                first = (2 * j + c) * neg_half
                pair_sums[c, h, j] = neg_part[first : first + neg_half, cols]
    sum_pair = send(pair_sums.at[1 - core], pair_in, sibling)
    w_part = contract_first(gated, grad_out_b).astype(jnp.bfloat16)
    for c in range(2):
        for j in range(n_shard):
            for z in range(n_z):
                first = ((c * n_shard + j) * n_z + z) * w_share
                w_pair[c, z, j] = w_part[first : first + w_share]
    w_pair_copy = send(w_pair.at[1 - core], w_pair_in, sibling)
    sum_pair.wait_recv()
    out_sums[...] = (
        pair_sums[core].astype(jnp.float32) + pair_in[...].astype(jnp.float32)
    ).astype(jnp.bfloat16)
    sum_sends = []
    for h in range(n_parts):
        if h > 0:
            row_sends.append(
                [send(out_rows.at[h, peer[1]], in_rows.at[h, shard], peer) for peer in peers]
            )
        sum_sends.append(
            [send(out_sums.at[h, peer[1]], in_sums.at[h, shard], peer) for peer in peers]
        )
    w_pair_copy.wait_recv()
    w_out_z[...] = (
        w_pair[core].astype(jnp.float32) + w_pair_in[...].astype(jnp.float32)
    ).astype(jnp.bfloat16)
    w_z_sends = [
        send(w_out_z.at[z_to[k]], w_in_z.at[height], peer) for k, peer in enumerate(z_peers)
    ]

    grad_gated = reduce_last_dimension(grad_out_b, w_out_ref[...])
    grad_pre[0] = (grad_gated * joined_wide * middle_scale * silu_slope(pre[0])).astype(
        jnp.bfloat16
    )
    grad_norm = grad_gated * gate_wide
    grad_joined_ref[...] = (
        middle_scale * grad_norm
        - joined_wide
        * middle_scale**3
        * jnp.mean(joined_wide * grad_norm, axis=1, keepdims=True)
    ).astype(jnp.bfloat16)

    def head_back(head):
        cols = slice(head * DH, (head + 1) * DH)
        scores = scores_ref[head]
        sigmoid = lax.logistic(scores)
        visible = visible_ref[...]
        weights = (scores * sigmoid * visible).astype(jnp.bfloat16)
        grad_head = grad_joined_ref[:, cols]
        grad_weights = reduce_last_dimension(grad_head, head_part(1, head))
        slope = sigmoid * (1.0 + scores * (1.0 - sigmoid))
        grad_scores = (grad_weights * visible * slope * DH ** (-0.5)).astype(jnp.bfloat16)
        grads = (
            contract_first(weights, grad_head),
            jnp.dot(grad_scores, head_part(3, head), preferred_element_type=jnp.float32),
            contract_first(grad_scores, head_part(2, head)),
        )
        for j, grad in enumerate(grads):
            grad_pre[j + 1, :, cols] = (grad * silu_slope(pre[j + 1, :, cols])).astype(
                jnp.bfloat16
            )

    def collect(h):
        grad_items = jnp.zeros((rows_count, part_cols), jnp.float32)
        sums = jnp.zeros((neg_half, part_cols), jnp.float32)
        for k, source in enumerate([shard] + others):
            if k > 0:
                row_sends[h][k - 1].wait_recv()
                sum_sends[h][k - 1].wait_recv()
            rows = out_rows[h, shard] if k == 0 else in_rows[h, source]
            part = out_sums[h, shard] if k == 0 else in_sums[h, source]
            grad_items += jnp.dot(picks_ref[source], rows, preferred_element_type=jnp.float32)
            sums += part.astype(jnp.float32)
        own_rows = jnp.where(core == 0, negative_row[:, :neg_half], negative_row[:, neg_half:])
        grad_items += jnp.dot(
            row_picks(own_rows, rows_count),
            sums.astype(jnp.bfloat16),
            preferred_element_type=jnp.float32,
        )
        for z in range(n_z):
            for c in range(2):
                d = z * 2 + c
                out_pair[h, c, z] = grad_items[d * share : (d + 1) * share].astype(jnp.bfloat16)
        return send(out_pair.at[h, 1 - core], in_pair.at[h], sibling)

    def pass_on(h, pair):
        pair.wait_recv()
        for z in range(n_z):
            out_z[h, z] = (
                out_pair[h, core, z].astype(jnp.float32) + in_pair[h, z].astype(jnp.float32)
            ).astype(jnp.bfloat16)
        return [
            send(out_z.at[h, z_to[k]], in_z.at[h, height], peer) for k, peer in enumerate(z_peers)
        ]

    def share_out(h):
        total = out_z[h, height].astype(jnp.float32)
        for k, z in enumerate(z_from):
            z_sends[h][k].wait_recv()
            total += in_z[h, z].astype(jnp.float32)
        gathered[h, height, core] = total.astype(jnp.bfloat16)
        piece = gathered.at[h, height, core]
        along = [send(piece, piece, peer) for peer in z_peers]
        return along, [send(piece, piece, sibling)]

    def finish(z, c):
        rows = pl.ds(pl.multiple_of((z * 2 + c) * share, share), share)
        total = jnp.concatenate([gathered[h, z, c] for h in range(n_parts)], axis=1)
        item_grads_ref[rows] = finish_rows(
            total.astype(jnp.float32), items_ref[rows].astype(jnp.float32)
        )

    head_back(0)
    pair = collect(0)
    z_sends = [pass_on(0, pair)]
    head_back(1)
    w_total = w_out_z[height].astype(jnp.float32)
    for k, z in enumerate(z_from):
        w_z_sends[k].wait_recv()
        w_total += w_in_z[z].astype(jnp.float32)
    w_out_shard[...] = w_total.astype(jnp.bfloat16)
    w_sends = [send(w_out_shard.at[peer[1]], w_in_shard.at[shard], peer) for peer in peers]
    pair = collect(1)
    head_back(2)
    z_sends.append(pass_on(1, pair))
    w_total = w_out_shard[shard].astype(jnp.float32)
    for k, source in enumerate(others):
        w_sends[k].wait_recv()
        w_total += w_in_shard[source].astype(jnp.float32)
    w_gathered[core, shard, height] = (w_total / loss_scale).astype(jnp.bfloat16)
    w_mine = w_gathered.at[core, shard, height]
    w_z = [send(w_mine, w_mine, peer) for peer in z_peers]
    for head in range(3, HEADS):
        head_back(head)
    shared = [share_out(0)]
    for copy in w_z:
        copy.wait_recv()
    w_block = w_gathered.at[core, shard]
    w_around = [send(w_block, w_block, peer) for peer in peers]
    last = [send(w_block, w_block, sibling)]
    grad_normed = jnp.zeros((tok_rows, width), jnp.float32)
    for j in range(n_shard):
        grad_normed += reduce_last_dimension(grad_pre[j], w_full[j])
    wide_tokens = tokens_ref[...].astype(jnp.float32)
    grad_input = input_scale * grad_normed - wide_tokens * input_scale**3 * jnp.mean(
        wide_tokens * grad_normed, axis=1, keepdims=True
    )
    grad_tokens_ref[...] = (grad_out_ref[...] + grad_input).astype(jnp.bfloat16)

    shared.append(share_out(1))
    for k, source in enumerate(others):
        w_around[k].wait_recv()
        piece = w_gathered.at[core, source]
        last.append(send(piece, piece, sibling))
    finish(height, core)
    for copy in last:
        copy.wait_recv()
    weight_grads_ref[...] = w_gathered[...].astype(jnp.float32)
    for h in range(n_parts):
        along, pairs = shared[h]
        for k, z in enumerate(z_from):
            along[k].wait_recv()
            piece = gathered.at[h, z, core]
            pairs.append(send(piece, piece, sibling))
    for z in z_from:
        finish(z, core)
    for k, z in enumerate([height] + z_from):
        for along, pairs in shared:
            pairs[k].wait_recv()
        finish(z, 1 - core)
    for copy in started:
        copy.wait_send()


def vmem_specs(count):
    return [pl.BlockSpec(memory_space=pltpu.VMEM)] * count


def shards(tokens, w_proj, w_out, item_rows, lengths, target_owner, target_row, negative_rows):
    tok_rows, width = tokens.shape
    n_shard = lax.axis_size("shard")
    n_dp = lax.axis_size("dp")
    n_z = n_dp // 2
    capacity = 2 * tok_rows // n_shard
    rows_count = item_rows.shape[0]
    neg_half = negative_rows.shape[0] // 2
    share = rows_count // n_dp
    w_half = width // n_shard // 2
    w_share = w_half // n_z
    parts = 2
    cols = width // parts
    b16 = jnp.bfloat16
    f32 = jnp.float32
    shape = jax.ShapeDtypeStruct
    copies = 7 * (n_shard - 1) + 4 * parts * (n_shard + n_z) + 2 * (n_shard + n_z) + 8
    grad_tokens, item_grads, weight_grads = pl.pallas_call(
        functools.partial(layer_kernel, n_dp, n_shard, capacity),
        out_shape=[
            shape((tok_rows, width), b16),
            shape((rows_count, width), f32),
            shape((2, n_shard, n_z, w_share, width), f32),
        ],
        in_specs=vmem_specs(8),
        out_specs=vmem_specs(3),
        scratch_shapes=[
            pltpu.VMEM((parts, n_z, 2, share, cols), b16),
            pltpu.VMEM((2, n_shard, n_z, w_share, width), b16),
            pltpu.VMEM((n_shard, width, width), b16),
            pltpu.VMEM((n_shard, 2, neg_half, width), b16),
            pltpu.VMEM((n_shard, 8, capacity), jnp.int32),
            pltpu.VMEM((n_shard, 8, capacity), jnp.int32),
            pltpu.VMEM((n_shard, capacity, width), b16),
            pltpu.VMEM((n_shard, capacity, width), b16),
            pltpu.VMEM((rows_count, width), b16),
            pltpu.VMEM((4, tok_rows, width), f32),
            pltpu.VMEM((4, tok_rows, width), b16),
            pltpu.VMEM((HEADS, tok_rows, tok_rows), f32),
            pltpu.VMEM((tok_rows, tok_rows), f32),
            pltpu.VMEM((tok_rows, width), b16),
            pltpu.VMEM((tok_rows, width), b16),
            pltpu.VMEM((tok_rows, width), b16),
            pltpu.VMEM((tok_rows, width), f32),
            pltpu.VMEM((4, tok_rows, width), b16),
            pltpu.VMEM((parts, n_shard, capacity, cols), b16),
            pltpu.VMEM((parts, n_shard, capacity, cols), b16),
            pltpu.VMEM((2, parts, n_shard, neg_half, cols), b16),
            pltpu.VMEM((parts, n_shard, neg_half, cols), b16),
            pltpu.VMEM((parts, n_shard, neg_half, cols), b16),
            pltpu.VMEM((parts, n_shard, neg_half, cols), b16),
            pltpu.VMEM((parts, 2, n_z, share, cols), b16),
            pltpu.VMEM((parts, n_z, share, cols), b16),
            pltpu.VMEM((parts, n_z, share, cols), b16),
            pltpu.VMEM((parts, n_z, share, cols), b16),
            pltpu.VMEM((n_shard * capacity, tok_rows), b16),
            pltpu.VMEM((n_shard, rows_count, capacity), b16),
            pltpu.VMEM((2, n_z, n_shard, w_share, width), b16),
            pltpu.VMEM((n_z, n_shard, w_share, width), b16),
            pltpu.VMEM((n_z, n_shard, w_share, width), b16),
            pltpu.VMEM((n_z, n_shard, w_share, width), b16),
            pltpu.VMEM((n_shard, w_share, width), b16),
            pltpu.VMEM((n_shard, w_share, width), b16),
            pltpu.SemaphoreType.DMA((copies,)),
            pltpu.SemaphoreType.DMA((copies,)),
        ],
        compiler_params=pltpu.CompilerParams(
            collective_id=0, has_side_effects=True, vmem_limit_bytes=56 * 2**20
        ),
        name="layer",
    )(
        tokens,
        w_proj,
        w_out,
        item_rows,
        lengths,
        target_owner.reshape(1, -1),
        target_row,
        negative_rows.reshape(1, -1),
    )
    return (grad_tokens, weight_grads.reshape(width, width), item_grads)


def fits_kernels(mesh):
    n_dp, n_shard = mesh.shape["dp"], mesh.shape["shard"]
    return n_dp % 2 == 0 and n_dp > 2 and n_shard == 4 and n_dp % 4 == 0 and D % (16 * n_dp * n_shard) == 0


def solution(mesh):
    in_specs = (
        P(("dp", "shard"), None),
        P(None, "shard"),
        P(),
        P("shard", None),
        P(("dp", "shard"), None),
        P(("dp", "shard"), None),
        P(("dp", "shard")),
        P("shard"),
    )
    out_specs = (P(("dp", "shard"), None), P(), P("shard", None))
    return jax.shard_map(
        shards if fits_kernels(mesh) else plain_shards,
        mesh=mesh, in_specs=in_specs, out_specs=out_specs, check_vma=False)
```

```python
import functools

import jax
import jax.numpy as jnp
from jax import lax
from jax.experimental import pallas as pl
from jax.experimental.pallas import tpu as pltpu
from jax.sharding import PartitionSpec as P

D = 512
HEADS = 4
DH = 128
MAXLEN = 192


epsilon = 1e-06
logit_divisor = 0.015625
loss_scale = 512.0


def reduce_last_dimension(operand, other_side):
    return lax.dot_general(
        operand, other_side, (((1,), (1,)), ((), ())), preferred_element_type=jnp.float32
    )


def contract_first(operand, other_side):
    return lax.dot_general(
        operand, other_side, (((0,), (0,)), ((), ())), preferred_element_type=jnp.float32
    )


def silu_slope(values):
    sigmoid = jax.nn.sigmoid(values)
    return sigmoid * (1.0 + values * (1.0 - sigmoid))


def history_mask(lengths_row, rows_count):
    history_ends = jnp.cumsum(lengths_row)
    positions = jnp.arange(rows_count, dtype=jnp.int32)
    history_ids = jnp.sum((positions[:, None] >= history_ends[None, :-1]).astype(jnp.int32), axis=1)
    visible = (history_ids[:, None] == history_ids[None, :]) & (
        positions[None, :] <= positions[:, None]
    )
    return jnp.where(visible, 1.0, 0.0).astype(jnp.float32)


def head_columns(activated, section, head_index):
    first_col = section * D + head_index * DH
    return activated[:, first_col : first_col + DH]


def head_scores(queries, key_rows):
    return reduce_last_dimension(queries, key_rows) * DH ** (-0.5)


def head_weights(scores, visible):
    return (jax.nn.silu(scores) * visible * (1.0 / MAXLEN)).astype(jnp.bfloat16)


def forward_layer(tokens, project, w_out, visible):
    wide_tokens = tokens.astype(jnp.float32)
    input_scale = lax.rsqrt(jnp.mean(wide_tokens * wide_tokens, axis=1, keepdims=True) + epsilon)
    normed = (wide_tokens * input_scale).astype(jnp.bfloat16)
    pre_act = project(normed)
    activated = lax.optimization_barrier(jax.nn.silu(pre_act).astype(jnp.bfloat16))
    heads_out = []
    for head_index in range(HEADS):
        queries = head_columns(activated, 2, head_index)
        key_rows = head_columns(activated, 3, head_index)
        value_rows = head_columns(activated, 1, head_index)
        weights = head_weights(head_scores(queries, key_rows), visible)
        heads_out.append(jnp.dot(weights, value_rows, preferred_element_type=jnp.float32))
    joined = lax.optimization_barrier(jnp.concatenate(heads_out, axis=1).astype(jnp.bfloat16))
    joined_wide = joined.astype(jnp.float32)
    middle_scale = lax.rsqrt(jnp.mean(joined_wide * joined_wide, axis=1, keepdims=True) + epsilon)
    gate_wide = activated[:, :D].astype(jnp.float32)
    gated = (joined_wide * middle_scale * gate_wide).astype(jnp.bfloat16)
    layer_out = wide_tokens + jnp.dot(gated, w_out, preferred_element_type=jnp.float32)
    return (layer_out, (wide_tokens, input_scale, pre_act, activated, joined, middle_scale, gated))


def loss_head(layer_out, clicked_product_vectors, sampled_decoys):
    out_scale = lax.rsqrt(jnp.sum(layer_out * layer_out, axis=1, keepdims=True) + epsilon)
    normalized_example_vectors = lax.optimization_barrier(
        (layer_out * out_scale).astype(jnp.bfloat16)
    )
    normalized_complete_embedding = normalized_example_vectors.astype(jnp.float32)
    correct_logit_entry = (
        jnp.sum(normalized_complete_embedding * clicked_product_vectors.astype(jnp.float32), axis=1)
        / logit_divisor
    )
    decoy_logit_entries = (
        reduce_last_dimension(normalized_example_vectors, sampled_decoys) / logit_divisor
    )
    target_exp = jnp.exp(correct_logit_entry)
    negative_exp = jnp.exp(decoy_logit_entries)
    totals = target_exp + jnp.sum(negative_exp, axis=1)
    target_prob = target_exp / totals
    negative_probs = (loss_scale * negative_exp / totals[:, None]).astype(jnp.bfloat16)
    target_coef = (loss_scale * (target_prob - 1.0))[:, None]
    grad_unit = target_coef * clicked_product_vectors.astype(jnp.float32) + jnp.dot(
        negative_probs, sampled_decoys, preferred_element_type=jnp.float32
    )
    grad_out = out_scale * grad_unit - layer_out * out_scale**3 * jnp.sum(
        layer_out * grad_unit, axis=1, keepdims=True
    )
    grad_target = target_coef * normalized_complete_embedding
    return (grad_out, grad_target, negative_probs, normalized_example_vectors)


def backward_layer(grad_out, saved_state, project_back, w_out, visible):
    wide_tokens, input_scale, pre_act, activated, joined, middle_scale, gated = saved_state
    grad_out_b = grad_out.astype(jnp.bfloat16)
    weight_part = contract_first(gated, grad_out_b)
    grad_gated = reduce_last_dimension(grad_out_b, w_out)
    joined_wide = joined.astype(jnp.float32)
    gate_wide = activated[:, :D].astype(jnp.float32)
    grad_gate = grad_gated * joined_wide * middle_scale
    grad_norm = grad_gated * gate_wide
    grad_joined = middle_scale * grad_norm - joined_wide * middle_scale**3 * jnp.mean(
        joined_wide * grad_norm, axis=1, keepdims=True
    )
    grad_joined_b = grad_joined.astype(jnp.bfloat16)
    grad_values = []
    grad_queries = []
    grad_keys = []
    for head_index in range(HEADS):
        queries = head_columns(activated, 2, head_index)
        key_rows = head_columns(activated, 3, head_index)
        value_rows = head_columns(activated, 1, head_index)
        scores = head_scores(queries, key_rows)
        weights = head_weights(scores, visible)
        grad_head = grad_joined_b[:, head_index * DH : (head_index + 1) * DH]
        grad_weights = reduce_last_dimension(grad_head, value_rows)
        grad_values.append(contract_first(weights, grad_head))
        grad_scores = (
            grad_weights * visible * (1.0 / MAXLEN) * silu_slope(scores) * DH ** (-0.5)
        ).astype(jnp.bfloat16)
        grad_queries.append(jnp.dot(grad_scores, key_rows, preferred_element_type=jnp.float32))
        grad_keys.append(contract_first(grad_scores, queries))
    grad_act = jnp.concatenate([grad_gate] + grad_values + grad_queries + grad_keys, axis=1)
    grad_pre = (grad_act * silu_slope(pre_act)).astype(jnp.bfloat16)
    grad_normed = project_back(grad_pre)
    grad_input = input_scale * grad_normed - wide_tokens * input_scale**3 * jnp.mean(
        wide_tokens * grad_normed, axis=1, keepdims=True
    )
    return ((grad_out + grad_input).astype(jnp.bfloat16), weight_part)


def finish_rows(grad_items, rows_wide):
    item_scale = lax.rsqrt(jnp.sum(rows_wide * rows_wide, axis=1, keepdims=True) + epsilon)
    return (
        item_scale * grad_items
        - rows_wide * item_scale**3 * jnp.sum(rows_wide * grad_items, axis=1, keepdims=True)
    ) / loss_scale


def plain_shards(tokens, w_proj, w_out, item_rows, lengths, target_owner, target_row, negative_rows):
    tok_rows = tokens.shape[0]
    model_width = tokens.shape[1]
    shard_count = lax.axis_size("shard")
    capacity = 2 * tok_rows // shard_count
    visible = history_mask(lengths[0], tok_rows)

    def project(normed):
        return jnp.dot(
            normed,
            lax.all_gather(w_proj, "shard", axis=1, tiled=True),
            preferred_element_type=jnp.float32,
        )

    def project_back(grad_pre):
        return reduce_last_dimension(grad_pre, lax.all_gather(w_proj, "shard", axis=1, tiled=True))

    rows_wide = item_rows.astype(jnp.float32)
    item_scale = lax.rsqrt(jnp.sum(rows_wide * rows_wide, axis=1, keepdims=True) + epsilon)
    unit_items = (rows_wide * item_scale).astype(jnp.bfloat16)
    owners = target_owner[:, 0]
    owner_hits = (owners[:, None] == jnp.arange(shard_count, dtype=jnp.int32)[None, :]).astype(
        jnp.int32
    )
    earlier = jnp.cumsum(owner_hits, axis=0) - owner_hits
    slot_index = jnp.sum(earlier * owner_hits, axis=1)
    position = owners * capacity + slot_index
    requests = jnp.zeros((shard_count * capacity,), jnp.int32).at[position].set(target_row)
    asked_rows = lax.all_to_all(
        requests.reshape(shard_count, capacity), "shard", split_axis=0, concat_axis=0, tiled=True
    )
    asked_flat = asked_rows.reshape(-1)
    served = jnp.take(unit_items, asked_flat, axis=0).reshape(shard_count, capacity, model_width)
    fetched = lax.all_to_all(served, "shard", split_axis=0, concat_axis=0, tiled=True)
    clicked_product_vectors = jnp.take(
        fetched.reshape(shard_count * capacity, model_width), position, axis=0
    )
    sampled_decoys = lax.all_gather(
        jnp.take(unit_items, negative_rows, axis=0), "shard", axis=0, tiled=True
    )
    layer_out, saved_state = forward_layer(tokens, project, w_out, visible)
    grad_out, grad_target, negative_probs, normalized_example_vectors = loss_head(
        layer_out, clicked_product_vectors, sampled_decoys
    )
    grad_tokens, weight_part = backward_layer(grad_out, saved_state, project_back, w_out, visible)
    outgoing = (
        jnp.zeros((shard_count * capacity, model_width), jnp.float32).at[position].set(grad_target)
    )
    returned = lax.all_to_all(
        outgoing.reshape(shard_count, capacity, model_width).astype(jnp.bfloat16),
        "shard",
        split_axis=0,
        concat_axis=0,
        tiled=True,
    ).astype(jnp.float32)
    grad_items = (
        jnp.zeros((item_rows.shape[0], model_width), jnp.float32)
        .at[asked_flat]
        .add(returned.reshape(-1, model_width))
    )
    own_negatives = lax.psum_scatter(
        contract_first(negative_probs, normalized_example_vectors).astype(jnp.bfloat16),
        "shard",
        scatter_dimension=0,
        tiled=True,
    ).astype(jnp.float32)
    grad_items = grad_items.at[negative_rows].add(own_negatives)
    share_rows = item_rows.shape[0] // lax.axis_size("dp")
    summed_share = lax.psum_scatter(
        grad_items.astype(jnp.bfloat16), "dp", scatter_dimension=0, tiled=True
    ).astype(jnp.float32)
    share_start = lax.axis_index("dp") * share_rows
    share_wide = lax.dynamic_slice_in_dim(rows_wide, share_start, share_rows, 0)
    item_grads = lax.all_gather(
        finish_rows(summed_share, share_wide).astype(jnp.bfloat16), "dp", axis=0, tiled=True
    ).astype(jnp.float32)
    weight_grads = lax.psum(weight_part, ("dp", "shard")) / loss_scale
    return (grad_tokens, weight_grads, item_grads)


MESH = pl.DeviceIdType.MESH


def start_copy(src, dst, sems, index, target):
    send_sem, recv_sem = sems
    copy = pltpu.make_async_remote_copy(
        src_ref=src,
        dst_ref=dst,
        send_sem=send_sem.at[index],
        recv_sem=recv_sem.at[index],
        device_id=target,
        device_id_type=MESH,
    )
    copy.start()
    return copy


def places(n_dp, n_shard):
    dp = lax.axis_index("dp")
    shard = lax.axis_index("shard")
    core = lax.rem(dp, 2)
    height = dp // 2
    sibling = (dp + 1 - 2 * core, shard)
    shard_peers = [(dp, lax.rem(shard + k, n_shard)) for k in range(1, n_shard)]
    shard_from = [lax.rem(shard + n_shard - k, n_shard) for k in range(1, n_shard)]
    n_z = n_dp // 2
    z_to = [lax.rem(height + k, n_z) for k in range(1, n_z)]
    z_peers = [(z * 2 + core, shard) for z in z_to]
    z_from = [lax.rem(height + n_z - k, n_z) for k in range(1, n_z)]
    return dp, shard, core, height, sibling, shard_peers, shard_from, z_to, z_peers, z_from


def one_hot_columns(position, slots):
    columns = lax.broadcasted_iota(jnp.int32, (position.shape[0], slots), 1)
    return columns == position


def row_picks(asked_row, rows_count):
    rows = lax.broadcasted_iota(jnp.int32, (rows_count, asked_row.shape[1]), 0)
    return jnp.where(rows == asked_row, 1.0, 0.0).astype(jnp.bfloat16)


def as_column(row):
    count = row.shape[1]
    across = lax.broadcasted_iota(jnp.int32, (count, count), 0)
    along = lax.broadcasted_iota(jnp.int32, (count, count), 1)
    return jnp.sum(jnp.where(across == along, row, 0), axis=1, keepdims=True)


def as_row(column):
    count = column.shape[0]
    across = lax.broadcasted_iota(jnp.int32, (count, count), 0)
    along = lax.broadcasted_iota(jnp.int32, (count, count), 1)
    return jnp.sum(jnp.where(across == along, column, 0), axis=0, keepdims=True)


def ones_of(picks):
    return jnp.where(picks, 1.0, 0.0).astype(jnp.bfloat16)


def visible_pairs(lengths, rows_count):
    across = lax.broadcasted_iota(jnp.int32, (rows_count, rows_count), 0)
    along = lax.broadcasted_iota(jnp.int32, (rows_count, rows_count), 1)
    history_a = jnp.zeros((rows_count, rows_count), jnp.int32)
    history_b = jnp.zeros((rows_count, rows_count), jnp.int32)
    end = jnp.zeros((1, 1), jnp.int32)
    for j in range(lengths.shape[1] - 1):
        end = end + lengths[:, j : j + 1]
        history_a += jnp.where(across >= end, 1, 0)
        history_b += jnp.where(along >= end, 1, 0)
    return jnp.where((history_a == history_b) & (along <= across), 1.0 / MAXLEN, 0.0)


def layer_kernel(
    n_dp,
    n_shard,
    capacity,
    tokens_ref,
    w_ref,
    w_out_ref,
    items_ref,
    lengths_ref,
    owner_ref,
    target_ref,
    negative_ref,
    grad_tokens_ref,
    item_grads_ref,
    w_gathered,
    gathered,
    w_full,
    negatives,
    requests,
    asked,
    served,
    fetched,
    unit,
    pre,
    act,
    scores_ref,
    visible_ref,
    normed_ref,
    joined_ref,
    grad_joined_ref,
    grad_out_ref,
    grad_pre,
    out_rows,
    in_rows,
    pair_sums,
    pair_in,
    out_sums,
    in_sums,
    out_pair,
    in_pair,
    out_z,
    in_z,
    slots_back,
    picks_ref,
    w_pair,
    w_pair_in,
    w_out_z,
    w_in_z,
    w_out_shard,
    w_in_shard,
    send_sem,
    recv_sem,
):
    dp, shard, core, height, sibling, peers, sources, z_to, z_peers, z_from = places(n_dp, n_shard)
    n_z = n_dp // 2
    others = sources
    near = range(n_shard - 1)
    barrier = pltpu.get_barrier_semaphore()
    greeted = peers + [sibling] + z_peers
    for peer in greeted:
        pl.semaphore_signal(barrier, inc=1, device_id=peer, device_id_type=MESH)
    used = [0]
    started = []

    def send(src, dst, target):
        copy = start_copy(src, dst, (send_sem, recv_sem), used[0], target)
        used[0] += 1
        started.append(copy)
        return copy

    def left(copies):
        for copy in copies:
            copy.wait_send()
            started[:] = [other for other in started if other is not copy]

    rows_count, width = items_ref.shape
    tok_rows = tokens_ref.shape[0]
    neg_rows = negative_ref.shape[1]
    neg_half = neg_rows // 2
    half = w_ref.shape[0] // 2
    share = rows_count // n_dp
    w_rows = width // n_shard
    w_share = w_rows // n_dp
    n_parts, part_cols = out_rows.shape[0], out_rows.shape[-1]

    pl.semaphore_wait(barrier, len(greeted))
    edge = half // 4
    first_row = core * half
    odd = lax.rem(height, 2)
    partner = ((height + 1 - 2 * odd) * 2 + core, shard)
    rows_a = pl.ds(pl.multiple_of(first_row + odd * edge, edge), edge)
    rows_b = pl.ds(pl.multiple_of(first_row + (1 - odd) * edge, edge), edge)
    rows_c = pl.ds(pl.multiple_of(first_row + 2 * edge, edge), half - 2 * edge)
    a_copies = [send(w_ref.at[rows_a], w_full.at[shard, rows_a], peer) for peer in peers]
    owner_row = owner_ref[...]
    owner_col = as_column(owner_row)
    token_a = lax.broadcasted_iota(jnp.int32, (tok_rows, tok_rows), 0)
    token_b = lax.broadcasted_iota(jnp.int32, (tok_rows, tok_rows), 1)
    same = (owner_row == owner_col) & (token_b < token_a)
    slot = jnp.sum(jnp.where(same, 1.0, 0.0), axis=1, keepdims=True).astype(jnp.int32)
    position = owner_col * capacity + slot
    slots = one_hot_columns(position, n_shard * capacity)
    target = as_column(target_ref[...].reshape(1, -1))
    request = jnp.sum(jnp.where(slots, target, 0), axis=0, keepdims=True)
    for j in range(n_shard):
        part = request[:, j * capacity : (j + 1) * capacity]
        requests[j] = jnp.broadcast_to(part, (8, capacity))
    slots_one = ones_of(slots)
    slots_back[...] = row_picks(as_row(position), n_shard * capacity)

    ask_copies = [send(requests.at[peer[1]], asked.at[shard], peer) for peer in peers]
    left(a_copies)
    c_copies = [send(w_ref.at[rows_c], w_full.at[shard, rows_c], peer) for peer in peers]
    w_pairs = []
    b_copies = []
    for k, source in enumerate(others):
        a_copies[k].wait_recv()
        piece = w_full.at[source, rows_a]
        b_copies.append(send(piece, piece, partner))
        w_pairs.append(send(piece, piece, sibling))
    asked[shard] = requests[shard]

    rows_wide = items_ref[...].astype(jnp.float32)
    item_scale = lax.rsqrt(jnp.sum(rows_wide * rows_wide, axis=1, keepdims=True) + epsilon)
    unit[...] = (rows_wide * item_scale).astype(jnp.bfloat16)
    negative_row = negative_ref[...]
    negative_col = as_column(negative_row)
    own_negatives = jnp.dot(
        ones_of(one_hot_columns(negative_col, rows_count)),
        unit[...],
        preferred_element_type=jnp.float32,
    ).astype(jnp.bfloat16)
    negatives[shard, 0] = own_negatives[:neg_half]
    negatives[shard, 1] = own_negatives[neg_half:]
    neg_piece = negatives.at[shard, core]
    neg_copies = [send(neg_piece, neg_piece, peer) for peer in peers]
    w_full[shard] = w_ref[...]
    wide_tokens = tokens_ref[...].astype(jnp.float32)
    input_scale = lax.rsqrt(jnp.mean(wide_tokens * wide_tokens, axis=1, keepdims=True) + epsilon)
    normed_ref[...] = (wide_tokens * input_scale).astype(jnp.bfloat16)
    visible_ref[...] = visible_pairs(lengths_ref[...], tok_rows)

    def section(j):
        values = jnp.dot(normed_ref[...], w_full[j], preferred_element_type=jnp.float32)
        pre[j] = values
        act[j] = (values * lax.logistic(values)).astype(jnp.bfloat16)

    def rows_for(source):
        asked_row = asked[source][0:1]
        picks_ref[source] = row_picks(asked_row, rows_count)
        picks = ones_of(one_hot_columns(as_column(asked_row), rows_count))
        return jnp.dot(picks, unit[...], preferred_element_type=jnp.float32).astype(jnp.bfloat16)

    section(shard)
    for k, source in enumerate(others):
        ask_copies[k].wait_recv()
        served[source] = rows_for(source)
    fetched[shard] = rows_for(shard)
    left(c_copies)
    row_copies = [
        send(served.at[source], fetched.at[shard], (dp, source)) for source in others
    ]
    for rows, arriving in ((rows_c, c_copies), (rows_b, b_copies)):
        for k, source in enumerate(others):
            arriving[k].wait_recv()
            piece = w_full.at[source, rows]
            w_pairs.append(send(piece, piece, sibling))
    neg_pairs = []
    for k, source in enumerate(others):
        neg_copies[k].wait_recv()
        piece = negatives.at[source, core]
        neg_pairs.append(send(piece, piece, sibling))
    for k, source in enumerate(others):
        for copy in w_pairs[k :: n_shard - 1]:
            copy.wait_recv()
        section(source)

    def head_part(j, head):
        return act[j, :, head * DH : (head + 1) * DH]

    for head in range(HEADS):
        scores = head_scores(head_part(2, head), head_part(3, head))
        scores_ref[head] = scores
        weights = (scores * lax.logistic(scores) * visible_ref[...]).astype(jnp.bfloat16)
        joined_ref[:, head * DH : (head + 1) * DH] = jnp.dot(
            weights, head_part(1, head), preferred_element_type=jnp.float32
        ).astype(jnp.bfloat16)
    joined_wide = joined_ref[...].astype(jnp.float32)
    middle_scale = lax.rsqrt(jnp.mean(joined_wide * joined_wide, axis=1, keepdims=True) + epsilon)
    gate_wide = act[0].astype(jnp.float32)
    gated = (joined_wide * middle_scale * gate_wide).astype(jnp.bfloat16)
    layer_out = tokens_ref[...].astype(jnp.float32) + jnp.dot(
        gated, w_out_ref[...], preferred_element_type=jnp.float32
    )
    out_scale = lax.rsqrt(jnp.sum(layer_out * layer_out, axis=1, keepdims=True) + epsilon)
    unit_b = (layer_out * out_scale).astype(jnp.bfloat16)
    for copy in neg_pairs:
        copy.wait_recv()
    negative_exps = []
    for j in range(n_shard):
        for c in range(2):
            logits = reduce_last_dimension(unit_b, negatives[j, c]) / logit_divisor
            negative_exps.append(jnp.exp(logits))
    negative_exp = jnp.concatenate(negative_exps, axis=1)
    for copy in row_copies:
        copy.wait_recv()
    clicked = jnp.zeros((tok_rows, width), jnp.float32)
    for j in range(n_shard):
        clicked += jnp.dot(
            slots_one[:, j * capacity : (j + 1) * capacity],
            fetched[j],
            preferred_element_type=jnp.float32,
        )
    unit_wide = unit_b.astype(jnp.float32)
    target_logit = jnp.sum(unit_wide * clicked, axis=1, keepdims=True) / logit_divisor
    target_exp = jnp.exp(target_logit)
    totals = target_exp + jnp.sum(negative_exp, axis=1, keepdims=True)
    negative_probs = (loss_scale * negative_exp / totals).astype(jnp.bfloat16)
    target_coef = loss_scale * (target_exp / totals - 1.0)
    grad_target = (target_coef * unit_wide).astype(jnp.bfloat16)

    row_sends = []
    for h in range(n_parts):
        for j in range(n_shard):
            out_rows[h, j] = jnp.dot(
                slots_back[j * capacity : (j + 1) * capacity],
                grad_target[:, h * part_cols : (h + 1) * part_cols],
                preferred_element_type=jnp.float32,
            ).astype(jnp.bfloat16)
        if h == 0:
            row_sends.append(
                [send(out_rows.at[h, peer[1]], in_rows.at[h, shard], peer) for peer in peers]
            )
    grad_unit = target_coef * clicked
    for j in range(n_shard):
        for c in range(2):
            first = (2 * j + c) * neg_half
            grad_unit += jnp.dot(
                negative_probs[:, first : first + neg_half],
                negatives[j, c],
                preferred_element_type=jnp.float32,
            )
    grad_out = out_scale * grad_unit - layer_out * out_scale**3 * jnp.sum(
        layer_out * grad_unit, axis=1, keepdims=True
    )
    grad_out_ref[...] = grad_out
    grad_out_b = grad_out.astype(jnp.bfloat16)
    neg_part = contract_first(negative_probs, unit_b).astype(jnp.bfloat16)
    for h in range(n_parts):
        cols = slice(h * part_cols, (h + 1) * part_cols)
        for j in range(n_shard):
            for c in range(2):
                first = (2 * j + c) * neg_half
                pair_sums[c, h, j] = neg_part[first : first + neg_half, cols]
    sum_pair = send(pair_sums.at[1 - core], pair_in, sibling)
    w_part = contract_first(gated, grad_out_b).astype(jnp.bfloat16)
    for c in range(2):
        for j in range(n_shard):
            for z in range(n_z):
                first = ((c * n_shard + j) * n_z + z) * w_share
                w_pair[c, z, j] = w_part[first : first + w_share]
    w_pair_copy = send(w_pair.at[1 - core], w_pair_in, sibling)
    sum_pair.wait_recv()
    out_sums[...] = (
        pair_sums[core].astype(jnp.float32) + pair_in[...].astype(jnp.float32)
    ).astype(jnp.bfloat16)
    sum_sends = []
    for h in range(n_parts):
        if h > 0:
            row_sends.append(
                [send(out_rows.at[h, peer[1]], in_rows.at[h, shard], peer) for peer in peers]
            )
        sum_sends.append(
            [send(out_sums.at[h, peer[1]], in_sums.at[h, shard], peer) for peer in peers]
        )
    w_pair_copy.wait_recv()
    w_out_z[...] = (
        w_pair[core].astype(jnp.float32) + w_pair_in[...].astype(jnp.float32)
    ).astype(jnp.bfloat16)
    w_z_sends = [
        send(w_out_z.at[z_to[k]], w_in_z.at[height], peer) for k, peer in enumerate(z_peers)
    ]

    grad_gated = reduce_last_dimension(grad_out_b, w_out_ref[...])
    grad_pre[0] = (grad_gated * joined_wide * middle_scale * silu_slope(pre[0])).astype(
        jnp.bfloat16
    )
    grad_norm = grad_gated * gate_wide
    grad_joined_ref[...] = (
        middle_scale * grad_norm
        - joined_wide
        * middle_scale**3
        * jnp.mean(joined_wide * grad_norm, axis=1, keepdims=True)
    ).astype(jnp.bfloat16)

    def head_back(head):
        cols = slice(head * DH, (head + 1) * DH)
        scores = scores_ref[head]
        sigmoid = lax.logistic(scores)
        visible = visible_ref[...]
        weights = (scores * sigmoid * visible).astype(jnp.bfloat16)
        grad_head = grad_joined_ref[:, cols]
        grad_weights = reduce_last_dimension(grad_head, head_part(1, head))
        slope = sigmoid * (1.0 + scores * (1.0 - sigmoid))
        grad_scores = (grad_weights * visible * slope * DH ** (-0.5)).astype(jnp.bfloat16)
        grads = (
            contract_first(weights, grad_head),
            jnp.dot(grad_scores, head_part(3, head), preferred_element_type=jnp.float32),
            contract_first(grad_scores, head_part(2, head)),
        )
        for j, grad in enumerate(grads):
            grad_pre[j + 1, :, cols] = (grad * silu_slope(pre[j + 1, :, cols])).astype(
                jnp.bfloat16
            )

    def collect(h):
        grad_items = jnp.zeros((rows_count, part_cols), jnp.float32)
        sums = jnp.zeros((neg_half, part_cols), jnp.float32)
        for k, source in enumerate([shard] + others):
            if k > 0:
                row_sends[h][k - 1].wait_recv()
                sum_sends[h][k - 1].wait_recv()
            rows = out_rows[h, shard] if k == 0 else in_rows[h, source]
            part = out_sums[h, shard] if k == 0 else in_sums[h, source]
            grad_items += jnp.dot(picks_ref[source], rows, preferred_element_type=jnp.float32)
            sums += part.astype(jnp.float32)
        own_rows = jnp.where(core == 0, negative_row[:, :neg_half], negative_row[:, neg_half:])
        grad_items += jnp.dot(
            row_picks(own_rows, rows_count),
            sums.astype(jnp.bfloat16),
            preferred_element_type=jnp.float32,
        )
        for z in range(n_z):
            for c in range(2):
                d = z * 2 + c
                out_pair[h, c, z] = grad_items[d * share : (d + 1) * share].astype(jnp.bfloat16)
        return send(out_pair.at[h, 1 - core], in_pair.at[h], sibling)

    def pass_on(h, pair):
        pair.wait_recv()
        for z in range(n_z):
            out_z[h, z] = (
                out_pair[h, core, z].astype(jnp.float32) + in_pair[h, z].astype(jnp.float32)
            ).astype(jnp.bfloat16)
        return [
            send(out_z.at[h, z_to[k]], in_z.at[h, height], peer) for k, peer in enumerate(z_peers)
        ]

    def share_out(h):
        total = out_z[h, height].astype(jnp.float32)
        for k, z in enumerate(z_from):
            z_sends[h][k].wait_recv()
            total += in_z[h, z].astype(jnp.float32)
        gathered[h, height, core] = total.astype(jnp.bfloat16)
        piece = gathered.at[h, height, core]
        along = [send(piece, piece, peer) for peer in z_peers]
        return along, [send(piece, piece, sibling)]

    def finish(z, c):
        rows = pl.ds(pl.multiple_of((z * 2 + c) * share, share), share)
        total = jnp.concatenate([gathered[h, z, c] for h in range(n_parts)], axis=1)
        item_grads_ref[rows] = finish_rows(
            total.astype(jnp.float32), items_ref[rows].astype(jnp.float32)
        )

    head_back(0)
    pair = collect(0)
    z_sends = [pass_on(0, pair)]
    head_back(1)
    w_total = w_out_z[height].astype(jnp.float32)
    for k, z in enumerate(z_from):
        w_z_sends[k].wait_recv()
        w_total += w_in_z[z].astype(jnp.float32)
    w_out_shard[...] = w_total.astype(jnp.bfloat16)
    w_sends = [send(w_out_shard.at[peer[1]], w_in_shard.at[shard], peer) for peer in peers]
    pair = collect(1)
    head_back(2)
    z_sends.append(pass_on(1, pair))
    w_total = w_out_shard[shard].astype(jnp.float32)
    for k, source in enumerate(others):
        w_sends[k].wait_recv()
        w_total += w_in_shard[source].astype(jnp.float32)
    w_gathered[core, shard, height] = (w_total / loss_scale).astype(jnp.bfloat16)
    w_mine = w_gathered.at[core, shard, height]
    w_z = [send(w_mine, w_mine, peer) for peer in z_peers]
    for head in range(3, HEADS):
        head_back(head)
    shared = [share_out(0)]
    for copy in w_z:
        copy.wait_recv()
    w_block = w_gathered.at[core, shard]
    w_around = [send(w_block, w_block, peer) for peer in peers]
    last = [send(w_block, w_block, sibling)]
    grad_normed = jnp.zeros((tok_rows, width), jnp.float32)
    for j in range(n_shard):
        grad_normed += reduce_last_dimension(grad_pre[j], w_full[j])
    wide_tokens = tokens_ref[...].astype(jnp.float32)
    grad_input = input_scale * grad_normed - wide_tokens * input_scale**3 * jnp.mean(
        wide_tokens * grad_normed, axis=1, keepdims=True
    )
    grad_tokens_ref[...] = (grad_out_ref[...] + grad_input).astype(jnp.bfloat16)

    shared.append(share_out(1))
    for k, source in enumerate(others):
        w_around[k].wait_recv()
        piece = w_gathered.at[core, source]
        last.append(send(piece, piece, sibling))
    finish(height, core)
    for copy in last:
        copy.wait_recv()
    for h in range(n_parts):
        along, pairs = shared[h]
        for k, z in enumerate(z_from):
            along[k].wait_recv()
            piece = gathered.at[h, z, core]
            pairs.append(send(piece, piece, sibling))
    for z in z_from:
        finish(z, core)
    for k, z in enumerate([height] + z_from):
        for along, pairs in shared:
            pairs[k].wait_recv()
        finish(z, 1 - core)
    for copy in started:
        copy.wait_send()


def vmem_specs(count):
    return [pl.BlockSpec(memory_space=pltpu.VMEM)] * count


def shards(tokens, w_proj, w_out, item_rows, lengths, target_owner, target_row, negative_rows):
    tok_rows, width = tokens.shape
    n_shard = lax.axis_size("shard")
    n_dp = lax.axis_size("dp")
    n_z = n_dp // 2
    capacity = 2 * tok_rows // n_shard
    rows_count = item_rows.shape[0]
    neg_half = negative_rows.shape[0] // 2
    share = rows_count // n_dp
    w_half = width // n_shard // 2
    w_share = w_half // n_z
    parts = 2
    cols = width // parts
    b16 = jnp.bfloat16
    f32 = jnp.float32
    shape = jax.ShapeDtypeStruct
    copies = 7 * (n_shard - 1) + 4 * parts * (n_shard + n_z) + 2 * (n_shard + n_z) + 8
    grad_tokens, item_grads, weight_grads = pl.pallas_call(
        functools.partial(layer_kernel, n_dp, n_shard, capacity),
        out_shape=[
            shape((tok_rows, width), b16),
            shape((rows_count, width), f32),
            shape((2, n_shard, n_z, w_share, width), b16),
        ],
        in_specs=vmem_specs(8),
        out_specs=vmem_specs(3),
        scratch_shapes=[
            pltpu.VMEM((parts, n_z, 2, share, cols), b16),
            pltpu.VMEM((n_shard, width, width), b16),
            pltpu.VMEM((n_shard, 2, neg_half, width), b16),
            pltpu.VMEM((n_shard, 8, capacity), jnp.int32),
            pltpu.VMEM((n_shard, 8, capacity), jnp.int32),
            pltpu.VMEM((n_shard, capacity, width), b16),
            pltpu.VMEM((n_shard, capacity, width), b16),
            pltpu.VMEM((rows_count, width), b16),
            pltpu.VMEM((4, tok_rows, width), f32),
            pltpu.VMEM((4, tok_rows, width), b16),
            pltpu.VMEM((HEADS, tok_rows, tok_rows), f32),
            pltpu.VMEM((tok_rows, tok_rows), f32),
            pltpu.VMEM((tok_rows, width), b16),
            pltpu.VMEM((tok_rows, width), b16),
            pltpu.VMEM((tok_rows, width), b16),
            pltpu.VMEM((tok_rows, width), f32),
            pltpu.VMEM((4, tok_rows, width), b16),
            pltpu.VMEM((parts, n_shard, capacity, cols), b16),
            pltpu.VMEM((parts, n_shard, capacity, cols), b16),
            pltpu.VMEM((2, parts, n_shard, neg_half, cols), b16),
            pltpu.VMEM((parts, n_shard, neg_half, cols), b16),
            pltpu.VMEM((parts, n_shard, neg_half, cols), b16),
            pltpu.VMEM((parts, n_shard, neg_half, cols), b16),
            pltpu.VMEM((parts, 2, n_z, share, cols), b16),
            pltpu.VMEM((parts, n_z, share, cols), b16),
            pltpu.VMEM((parts, n_z, share, cols), b16),
            pltpu.VMEM((parts, n_z, share, cols), b16),
            pltpu.VMEM((n_shard * capacity, tok_rows), b16),
            pltpu.VMEM((n_shard, rows_count, capacity), b16),
            pltpu.VMEM((2, n_z, n_shard, w_share, width), b16),
            pltpu.VMEM((n_z, n_shard, w_share, width), b16),
            pltpu.VMEM((n_z, n_shard, w_share, width), b16),
            pltpu.VMEM((n_z, n_shard, w_share, width), b16),
            pltpu.VMEM((n_shard, w_share, width), b16),
            pltpu.VMEM((n_shard, w_share, width), b16),
            pltpu.SemaphoreType.DMA((copies,)),
            pltpu.SemaphoreType.DMA((copies,)),
        ],
        compiler_params=pltpu.CompilerParams(
            collective_id=0, has_side_effects=True, vmem_limit_bytes=56 * 2**20
        ),
        name="layer",
    )(
        tokens,
        w_proj,
        w_out,
        item_rows,
        lengths,
        target_owner.reshape(1, -1),
        target_row,
        negative_rows.reshape(1, -1),
    )
    return (grad_tokens, weight_grads.reshape(width, width).astype(f32), item_grads)


def fits_kernels(mesh):
    n_dp, n_shard = mesh.shape["dp"], mesh.shape["shard"]
    return n_dp % 2 == 0 and n_dp > 2 and n_shard == 4 and n_dp % 4 == 0 and D % (16 * n_dp * n_shard) == 0


def solution(mesh):
    in_specs = (
        P(("dp", "shard"), None),
        P(None, "shard"),
        P(),
        P("shard", None),
        P(("dp", "shard"), None),
        P(("dp", "shard"), None),
        P(("dp", "shard")),
        P("shard"),
    )
    out_specs = (P(("dp", "shard"), None), P(), P("shard", None))
    return jax.shard_map(
        shards if fits_kernels(mesh) else plain_shards,
        mesh=mesh, in_specs=in_specs, out_specs=out_specs, check_vma=False)
```
